32 devices in a mesh: ctx: 8 (over y, x, core), head: 4 (over z).
Axes of the slice: x: 2, y: 2, z: 4, core: 2. Of those that a mesh axis runs over, the one named last changes fastest.
Arguments:
- inputs: bfloat16 [4096, 2048], P('ctx'), may hold values from -6 to 6
- query_key_weight: bfloat16 [2, 2048, 2048], P(None, None, 'head'), may hold values from -0.125 to 0.125
- value_gate_weight: bfloat16 [2, 2048, 4096], P(None, None, 'head'), may hold values from -0.125 to 0.125
- decay_beta_weight: bfloat16 [2, 2048, 32], P(None, None, 'head'), may hold values from -0.125 to 0.125
- beta_bias: float32 [32], P('head'), may hold values from -5 to -3
- decay_scale: float32 [32], P('head'), may hold values from 0.0001 to 0.1
- norm_gain: float32 [128], replicated, may hold values from 0.1 to 1.9
- out_weight: bfloat16 [4096, 2048], P('head'), may hold values from -0.09375 to 0.09375
- boundaries: int32 [4096], P('ctx'), may hold values 0 or 1
- grad_mixed: bfloat16 [4096, 2048], P('ctx'), may hold values from -6 to 6
Outputs:
- mixed: bfloat16 [4096, 2048], P('ctx', 'head')
- grad_inputs: bfloat16 [4096, 2048], P('ctx', 'head')
- grad_query_key: float32 [2, 2048, 2048], P(None, 'ctx', 'head')
- grad_value_gate: float32 [2, 2048, 4096], P(None, 'ctx', 'head')
- grad_decay_beta: float32 [2, 2048, 32], P(None, 'ctx', 'head')
- grad_out_weight: float32 [4096, 2048], P('head', 'ctx')
The draws below stay inside these ranges and needn't reach their ends.
All inputs are finite; a program needn't handle non-finite values. No bound on the sum of `boundaries` on one device may be relied on, other than what follows from the above.
Results may differ from the reference program's by a relative error of at most 0.02.
Values may be sent and summed in bfloat16 or wider, within the bound.
No kernel may reach another device: no remote copies, remote signals or barrier semaphores. Data moves between devices by JAX's collectives and lax.ppermute only.
A program may use at most 192 MiB of HBM per device.

```python
import math
import jax
import jax.numpy as jnp
from jax import lax

D = 2048
KH = 16
VH = 32
DK = 128
DV = 128
SPAN = 64
TOK_DEV = 512
TOKENS = 4096
N_CTX = 8
N_HEAD = 4


def touch_ends(result, key, least, largest):
    longest = result.shape.index(max(result.shape))
    spots = []
    for shift in (0, 1):
        where = [jax.random.randint(jax.random.fold_in(key, axis), (), 0, length) for axis, length in enumerate(result.shape)]
        where[longest] = (where[longest] + shift) % result.shape[longest]
        spots.append(tuple(where))
    return result.at[spots[0]].set(least).at[spots[1]].set(largest)


def steps_of(rng, dims, cuts, smallest, largest):
    gain, own = 1.0, jax.random.fold_in(rng, 6)
    for position, shards_of in cuts:
        steps = jnp.exp(jax.random.uniform(jax.random.fold_in(own, position), (shards_of,), jnp.float32, smallest / len(cuts), largest / len(cuts)))
        gain = gain * jnp.repeat(steps, dims[position] // shards_of).reshape([-1 if axis == position else 1 for axis in range(len(dims))])
    return gain


def scatter_about(rng, extent, scale, limit, pieces=(), held_as=jnp.bfloat16):
    values = jax.random.normal(rng, extent, jnp.float32) * scale
    if len(pieces) > 0:
        values = steps_of(rng, extent, pieces, -0.22, 0.18) * values
    return jnp.clip(values, min=-limit, max=limit).astype(held_as)


def setup_inputs(seed: int = 0) -> dict:
    key_of = jax.random.split(jax.random.key(seed), 11)
    return {
        "inputs": scatter_about(key_of[0], (TOKENS, D), 1.0, 6.0, ((0, 8),)),
        "query_key_weight": scatter_about(key_of[1], (2, D, KH * DK), D ** -0.5, 0.125, ((2, 4),)),
        "value_gate_weight": scatter_about(key_of[2], (2, D, VH * DV), D ** -0.5, 0.125, ((2, 4),)),
        "decay_beta_weight": scatter_about(key_of[3], (2, D, VH), D ** -0.5, 0.125, ((2, 4),)),
        "beta_bias": jnp.clip(-5.0 + 2.0 * jax.random.uniform(key_of[4], (VH,), jnp.float32) ** steps_of(key_of[4], (VH,), ((0, 4),), -0.2, 0.2), -5.0, -3.0),
        "decay_scale": jnp.clip(jnp.exp(math.log(0.1) - 6.9077553 * jax.random.uniform(key_of[5], (VH,), jnp.float32) ** steps_of(key_of[5], (VH,), ((0, 4),), -0.2, 0.2)), 0.0001, 0.1),
        "norm_gain": jnp.clip(1.0 + 0.18 * jax.random.normal(key_of[6], (DV,), jnp.float32), 0.1, 1.9),
        "out_weight": scatter_about(key_of[7], (VH * DV, D), (VH * DV) ** -0.5, 0.09375, ((0, 4),)),
        "boundaries": touch_ends((jax.random.randint(key_of[8], (TOKENS,), 0, TOKENS) < 4).astype(jnp.int32), jax.random.fold_in(key_of[8], 1), 0, 1),
        "grad_mixed": scatter_about(key_of[9], (TOKENS, D), 1.0, 6.0, ((0, 8),)),
    }


EPS = 1e-06
PRECISE_MODE = lax.Precision.HIGHEST

def head_inputs(proj_query_key, proj_value_gate, proj_decay_beta, beta_bias, decay_scale):
    tok_count = proj_query_key.shape[1]
    key_heads = proj_query_key.shape[2] // DK
    value_heads = proj_value_gate.shape[2] // DV
    repeat_count = value_heads // key_heads
    query_rows = proj_query_key[0].reshape(tok_count, key_heads, DK)
    key_rows = proj_query_key[1].reshape(tok_count, key_heads, DK)
    query_rows = query_rows * lax.rsqrt(lax.optimization_barrier(jnp.sum(query_rows * query_rows, axis=-1, keepdims=True)) + EPS)
    key_rows = key_rows * lax.rsqrt(lax.optimization_barrier(jnp.sum(key_rows * key_rows, axis=-1, keepdims=True)) + EPS)
    query_rows = jnp.repeat(query_rows, repeat_count, axis=1) * DK ** (-0.5)
    key_rows = jnp.repeat(key_rows, repeat_count, axis=1)
    value_rows = proj_value_gate[0].reshape(tok_count, value_heads, DV)
    gate_rows = proj_value_gate[1].reshape(tok_count, value_heads, DV)
    beta_rows = jax.nn.sigmoid(proj_decay_beta[1] + beta_bias)
    log_decay = -decay_scale * jax.nn.softplus(proj_decay_beta[0])
    return (query_rows, key_rows, value_rows, gate_rows, beta_rows, log_decay)

def to_spans(array_in, spans):
    head_count = array_in.shape[1]
    shaped = array_in.reshape(spans, SPAN, head_count, -1)
    return jnp.transpose(shaped, (2, 0, 1, 3))

def span_terms(query_rows, key_rows, value_rows, beta_rows, log_decay, resets):
    spans = beta_rows.shape[0] // SPAN
    query_blocks = to_spans(query_rows, spans)
    key_blocks = to_spans(key_rows, spans)
    value_blocks = to_spans(value_rows, spans)
    beta_blocks = to_spans(beta_rows[:, :, None], spans)[..., 0]
    cumulative = jnp.cumsum(to_spans(log_decay[:, :, None], spans)[..., 0], axis=-1)
    doc_index = jnp.cumsum(resets.reshape(spans, SPAN), axis=-1)[None]
    positions = jnp.arange(SPAN)
    lower_incl = positions[:, None] >= positions[None, :]
    lower_strict = (positions[:, None] > positions[None, :]).astype(jnp.float32)
    same_doc = (doc_index[..., :, None] == doc_index[..., None, :]) & lower_incl
    log_gap = jnp.minimum(cumulative[..., :, None] - cumulative[..., None, :], 0.0)
    pair_decay = jnp.where(same_doc, jnp.exp(log_gap), 0.0)
    start_keep = jnp.where(doc_index == 0, jnp.exp(cumulative), 0.0)
    end_keep = jnp.where(doc_index == doc_index[..., -1:], jnp.exp(jnp.minimum(cumulative[..., -1:] - cumulative, 0.0)), 0.0)
    total_keep = start_keep[..., -1]
    key_gram = jnp.einsum('hnck,hnjk->hncj', key_blocks, key_blocks, precision=PRECISE_MODE)
    system = jnp.eye(SPAN, dtype=jnp.float32) + beta_blocks[..., :, None] * pair_decay * lower_strict * key_gram
    right_side = jnp.concatenate([beta_blocks[..., None] * value_blocks, (beta_blocks * start_keep)[..., None] * key_blocks], axis=-1)
    solved = jax.scipy.linalg.solve_triangular(system, right_side, lower=True, unit_diagonal=True)
    pseudo_base = solved[..., :DV]
    key_weights = solved[..., DV:]
    end_keys = end_keep[..., None] * key_blocks
    scores = pair_decay * jnp.einsum('hnck,hnjk->hncj', query_blocks, key_blocks, precision=PRECISE_MODE)
    start_queries = start_keep[..., None] * query_blocks
    return (start_queries, scores, pseudo_base, key_weights, end_keys, total_keep)

def run_spans(terms, state_in):

    def advance(carried_state, block_terms):
        block_query_rows, block_score_matrix, block_starting_offset, block_weight_matrix, block_final_keys, block_retained_decay = block_terms
        surrogate_values = block_starting_offset - jnp.einsum('xuy,xyf->xuf', block_weight_matrix, carried_state, precision=PRECISE_MODE)
        produced_output = jnp.einsum('xuy,xyf->xuf', block_query_rows, carried_state, precision=PRECISE_MODE) + jnp.einsum('adx,axo->ado', block_score_matrix, surrogate_values, precision=PRECISE_MODE)
        updated_state = block_retained_decay[:, None, None] * carried_state + jnp.einsum('gzy,gzq->gyq', block_final_keys, surrogate_values, precision=PRECISE_MODE)
        return (updated_state, produced_output)
    moved = tuple([jnp.moveaxis(member, 1, 0) for member in terms])
    final, produced_output = lax.scan(advance, state_in, moved)
    spans, head_count = (produced_output.shape[0], produced_output.shape[1])
    produced_output = jnp.transpose(produced_output, (0, 2, 1, 3)).reshape(spans * SPAN, head_count, DV)
    return (produced_output, final)

def mixer(proj_query_key, proj_value_gate, proj_decay_beta, beta_bias, decay_scale, norm_gain, resets, state_in):
    query_rows, key_rows, value_rows, gate_rows, beta_rows, log_decay = head_inputs(proj_query_key, proj_value_gate, proj_decay_beta, beta_bias, decay_scale)
    terms = span_terms(query_rows, key_rows, value_rows, beta_rows, log_decay, resets)
    produced_output, final = run_spans(terms, state_in)
    scale_rows = lax.rsqrt(lax.optimization_barrier(jnp.mean(produced_output * produced_output, axis=-1, keepdims=True)) + EPS)
    normed = produced_output * scale_rows * norm_gain * jax.nn.silu(gate_rows)
    return (normed.reshape(normed.shape[0], -1), final)

def rounded(partial_sum):
    return lax.optimization_barrier(partial_sum.astype(jnp.bfloat16)).astype(jnp.float32)

def settle(partials, axis_index):
    return lax.optimization_barrier(jnp.sum(rounded(partials), axis=axis_index))

def reference(inputs, query_key_weight, value_gate_weight, decay_beta_weight, beta_bias, decay_scale, norm_gain, out_weight, boundaries, grad_mixed):
    key_width = KH // N_HEAD * DK
    value_width = VH // N_HEAD * DV
    group_heads = VH // N_HEAD
    inputs_wide = inputs.astype(jnp.float32)
    grad_wide = grad_mixed.astype(jnp.float32)
    inputs_shards = inputs_wide.reshape(N_CTX, TOK_DEV, D)
    grad_shards = grad_wide.reshape(N_CTX, TOK_DEV, D)
    mixed_sum = jnp.zeros((TOKENS, D), jnp.float32)
    input_sum = jnp.zeros((TOKENS, D), jnp.float32)
    query_key_parts, value_gate_parts, decay_beta_parts, out_parts = ([], [], [], [])
    for group in range(N_HEAD):
        query_key_cols = query_key_weight[:, :, group * key_width:(group + 1) * key_width].astype(jnp.float32)
        value_gate_cols = value_gate_weight[:, :, group * value_width:(group + 1) * value_width].astype(jnp.float32)
        decay_beta_cols = decay_beta_weight[:, :, group * group_heads:(group + 1) * group_heads].astype(jnp.float32)
        out_rows = out_weight[group * value_width:(group + 1) * value_width]
        group_bias = beta_bias[group * group_heads:(group + 1) * group_heads]
        group_decay = decay_scale[group * group_heads:(group + 1) * group_heads]
        proj_query_key = jnp.einsum('td,sdf->stf', inputs_wide, query_key_cols)
        proj_value_gate = jnp.einsum('td,sdf->stf', inputs_wide, value_gate_cols)
        proj_decay_beta = jnp.einsum('td,sdf->stf', inputs_wide, decay_beta_cols)
        zero_state = jnp.zeros((group_heads, DK, DV), jnp.float32)

        def local_mixer(part_query_key, part_value_gate, part_decay_beta):
            return mixer(part_query_key, part_value_gate, part_decay_beta, group_bias, group_decay, norm_gain, boundaries, zero_state)[0]
        normed, pullback = jax.vjp(local_mixer, proj_query_key, proj_value_gate, proj_decay_beta)
        hidden = normed.astype(jnp.bfloat16)
        mixed_sum = mixed_sum + rounded(jnp.dot(hidden.astype(jnp.float32), out_rows.astype(jnp.float32), preferred_element_type=jnp.float32))
        delta_hidden = jnp.dot(grad_mixed.astype(jnp.float32), out_rows.T.astype(jnp.float32), preferred_element_type=jnp.float32)
        delta_query_key, delta_value_gate, delta_decay_beta = pullback(delta_hidden)
        delta_query_key = delta_query_key.astype(jnp.bfloat16).astype(jnp.float32)
        delta_value_gate = delta_value_gate.astype(jnp.bfloat16).astype(jnp.float32)
        delta_decay_beta = delta_decay_beta.astype(jnp.bfloat16).astype(jnp.float32)
        grad_rows = jnp.einsum('stf,sdf->td', delta_query_key, query_key_cols)
        grad_rows = grad_rows + jnp.einsum('stf,sdf->td', delta_value_gate, value_gate_cols)
        grad_rows = grad_rows + jnp.einsum('stf,sdf->td', delta_decay_beta, decay_beta_cols)
        input_sum = input_sum + rounded(grad_rows)
        query_key_parts.append(settle(jnp.einsum('ntd,sntf->sndf', inputs_shards, delta_query_key.reshape(2, N_CTX, TOK_DEV, -1)), 1))
        value_gate_parts.append(settle(jnp.einsum('ntd,sntf->sndf', inputs_shards, delta_value_gate.reshape(2, N_CTX, TOK_DEV, -1)), 1))
        decay_beta_parts.append(settle(jnp.einsum('ntd,sntf->sndf', inputs_shards, delta_decay_beta.reshape(2, N_CTX, TOK_DEV, -1)), 1))
        out_parts.append(settle(jnp.einsum('ntf,ntd->nfd', hidden.astype(jnp.float32).reshape(N_CTX, TOK_DEV, -1), grad_shards), 0))
    return (mixed_sum.astype(jnp.bfloat16), input_sum.astype(jnp.bfloat16), jnp.concatenate(query_key_parts, axis=2), jnp.concatenate(value_gate_parts, axis=2), jnp.concatenate(decay_beta_parts, axis=2), jnp.concatenate(out_parts, axis=0))
```

```python
import functools

import jax
import jax.numpy as jnp
from jax import lax
from jax.experimental import pallas as pl
from jax.experimental.pallas import tpu as pltpu
from jax.sharding import PartitionSpec as P

DK = 128
DV = 128
CHUNK = 128
EPS = 1e-06
QUERY_SCALE = DK ** (-0.5)

F32 = jnp.float32
BF16 = jnp.bfloat16
NN = ((1,), (0,))
NT = ((1,), (1,))
TN = ((0,), (0,))


def dot(a, b, dims=NN):
    return lax.dot_general(
        a.astype(BF16), b.astype(BF16), (dims, ((), ())), preferred_element_type=F32
    )


def exact(a, b, dims=NN):
    return lax.dot_general(
        a, b, (dims, ((), ())), precision=lax.Precision.HIGHEST, preferred_element_type=F32
    )


def softplus(x):
    return jnp.maximum(x, 0.0) + jnp.log1p(jnp.exp(-jnp.abs(x)))


def sigmoid(x):
    return 1.0 / (1.0 + jnp.exp(-x))


def row_sum(x):
    return jnp.sum(x, axis=-1, keepdims=True)


def grid_of(size):
    row = lax.broadcasted_iota(jnp.int32, (size, size), 0)
    col = lax.broadcasted_iota(jnp.int32, (size, size), 1)
    return row, col


def decays(decay_beta_ref, bias_ref, scale_ref, resets_ref):
    row, col = grid_of(CHUNK)
    lower = (row >= col).astype(F32)
    decay_logit = decay_beta_ref[0]
    beta = sigmoid(decay_beta_ref[1] + bias_ref[...])
    log_decay = -scale_ref[...] * softplus(decay_logit)
    resets = jnp.broadcast_to(resets_ref[0].astype(F32), (8, CHUNK))
    doc_row = dot(resets, lower, NT)[0:1]
    doc_col = dot(lower, resets, NT)[:, 0:1]
    cum_col = exact(lower, log_decay)
    cum_row = exact(log_decay, lower, ((0,), (1,)))
    same = (doc_col == doc_row) & (row >= col)
    start = jnp.where(doc_col == 0.0, jnp.exp(cum_col), 0.0)
    last = CHUNK - 1
    end = jnp.where(
        doc_col == doc_col[last:],
        jnp.exp(jnp.minimum(cum_col[last:] - cum_col, 0.0)),
        0.0,
    )
    return beta, cum_col, cum_row, same, start, end, start[last:], resets


def pair_decay(cum_col, cum_row, same, h):
    gap = jnp.minimum(cum_col[:, h : h + 1] - cum_row[h : h + 1, :], 0.0)
    return jnp.where(same, jnp.exp(gap), 0.0)


def head(ref, index, h):
    return ref[index][:, h * DK : (h + 1) * DK]


def unit_rows(x):
    inverse = lax.rsqrt(row_sum(x * x) + EPS)
    return x * inverse, inverse


def forward_kernel(
    query_key_ref,
    value_ref,
    decay_beta_ref,
    bias_ref,
    scale_ref,
    resets_ref,
    solve_ref,
    start_ref,
    map_ref,
    local_ref,
    total_ref,
    state_ref,
):
    heads = state_ref.shape[0]
    key_heads = query_key_ref.shape[2] // DK
    repeat = heads // key_heads
    row, col = grid_of(CHUNK)

    @pl.when(pl.program_id(0) == 0)
    def _():
        first = jnp.concatenate([(row == col).astype(F32), jnp.zeros((DK, DV), F32)], axis=1)
        for h in range(heads):
            state_ref[h] = first

    beta, cum_col, cum_row, same, start, end, total, _ = decays(
        decay_beta_ref, bias_ref, scale_ref, resets_ref
    )
    strict = row > col
    differ = row ^ col
    keys, queries, systems, scores = [], [], [], []
    for g in range(key_heads):
        q = unit_rows(head(query_key_ref, 0, g))[0] * QUERY_SCALE
        k = unit_rows(head(query_key_ref, 1, g))[0]
        queries.append(q)
        keys.append(k)
        key_gram = dot(k, k, NT)
        query_gram = dot(q, k, NT)
        for h in range(g * repeat, (g + 1) * repeat):
            decay = pair_decay(cum_col, cum_row, same, h)
            scores.append((decay * query_gram).astype(BF16))
            systems.append(jnp.where(strict, beta[:, h : h + 1] * decay * key_gram, 0.0))
    identity = (row == col).astype(F32)
    inverse = [
        (identity - jnp.where(differ == 1, system, 0.0)).astype(BF16) for system in systems
    ]
    level = 1
    while (1 << level) < CHUNK:
        here = (differ >> level) == 1
        inner = [
            dot(jnp.where(here, system, 0.0), x).astype(BF16)
            for system, x in zip(systems, inverse)
        ]
        inverse = [x - dot(x, y).astype(BF16) for x, y in zip(inverse, inner)]
        level += 1
    weights = []
    for h in range(heads):
        k = keys[h // repeat]
        v = value_ref[0][:, h * DV : (h + 1) * DV]
        b = beta[:, h : h + 1]
        right = jnp.concatenate([(b * start[:, h : h + 1]) * k, b * v], axis=1)
        weights.append(dot(inverse[h], right))
        solve_ref[0, h] = inverse[h]
    values = []
    for h in range(heads):
        state = state_ref[h].astype(BF16)
        start_ref[0, h] = state
        solved = weights[h]
        base = jnp.concatenate([jnp.zeros((CHUNK, DK), F32), solved[:, DK:]], axis=1)
        values.append((base - dot(solved[:, :DK], state)).astype(BF16))
    for h in range(heads):
        k, q = keys[h // repeat], queries[h // repeat]
        state = state_ref[h]
        out = dot(start[:, h : h + 1] * q, state) + dot(scores[h], values[h])
        map_ref[:, h * DK : (h + 1) * DK] = out[:, :DK].astype(BF16)
        local_ref[:, h * DV : (h + 1) * DV] = out[:, DK:]
        state = total[:, h : h + 1] * state + dot(end[:, h : h + 1] * k, values[h], TN)
        state_ref[h] = state
        total_ref[h] = state.astype(BF16)


def output_kernel(
    local_ref,
    map_ref,
    gate_ref,
    delta_ref,
    state_ref,
    gain_ref,
    hidden_ref,
    delta_gate_ref,
    delta_out_ref,
    delta_state_ref,
    total_ref,
):
    heads = state_ref.shape[0]
    step = pl.program_id(0)
    gain = gain_ref[...]
    for h in range(heads):
        cols = slice(h * DV, (h + 1) * DV)
        reach = map_ref[:, cols]
        out = local_ref[:, cols] + dot(reach, state_ref[h])
        gate = gate_ref[0][:, cols]
        delta = delta_ref[:, cols]
        scale = lax.rsqrt(row_sum(out * out) * (1.0 / DV) + EPS)
        normed = out * scale
        share = sigmoid(gate)
        silu = gate * share
        scaled = normed * gain
        hidden_ref[:, cols] = (scaled * silu).astype(BF16)
        delta_gate_ref[:, cols] = (
            delta * scaled * (share * (1.0 + gate * (1.0 - share)))
        ).astype(BF16)
        delta_normed = delta * gain * silu
        delta_out = scale * (
            delta_normed - normed * (row_sum(normed * delta_normed) * (1.0 / DV))
        )
        delta_out = delta_out.astype(BF16)
        delta_out_ref[:, cols] = delta_out
        part = dot(reach, delta_out, TN)

        @pl.when(step == 0)
        def _():
            total_ref[h] = part

        @pl.when(step > 0)
        def _():
            total_ref[h] += part

        delta_state_ref[h] = total_ref[h].astype(BF16)


def backward_kernel(
    query_key_ref,
    value_ref,
    decay_beta_ref,
    bias_ref,
    scale_ref,
    resets_ref,
    solve_ref,
    start_ref,
    state_in_ref,
    delta_out_ref,
    delta_final_ref,
    delta_query_key_ref,
    delta_value_ref,
    delta_decay_beta_ref,
    carry_ref,
):
    heads = carry_ref.shape[0]
    key_heads = query_key_ref.shape[2] // DK
    repeat = heads // key_heads
    row, col = grid_of(CHUNK)

    @pl.when(pl.program_id(0) == 0)
    def _():
        carry_ref[...] = delta_final_ref[...].astype(F32)

    beta, cum_col, cum_row, same, start, end, total, resets = decays(
        decay_beta_ref, bias_ref, scale_ref, resets_ref
    )
    strict = row > col
    lane = lax.broadcasted_iota(jnp.int32, (CHUNK, heads), 1)
    lane_one = lax.broadcasted_iota(jnp.int32, (1, heads), 1)
    state_of, value_of, right_of = [], [], []
    qs, ks, q_inv, k_inv, grams = [], [], [], [], []
    for g in range(key_heads):
        q, qi = unit_rows(head(query_key_ref, 0, g))
        k, ki = unit_rows(head(query_key_ref, 1, g))
        q = q * QUERY_SCALE
        qs.append(q)
        ks.append(k)
        q_inv.append(qi)
        k_inv.append(ki)
        grams.append((dot(k, k, NT), dot(q, k, NT)))
    for h in range(heads):
        before = start_ref[0, h]
        state = dot(before[:, :DK], state_in_ref[h]) + before[:, DK:].astype(F32)
        state_of.append(state.astype(BF16))
    for h in range(heads):
        k = ks[h // repeat]
        v = value_ref[0][:, h * DV : (h + 1) * DV]
        seen = dot(k, state_of[h])
        right_of.append(beta[:, h : h + 1] * (v - start[:, h : h + 1] * seen))
    for h in range(heads):
        value_of.append(dot(solve_ref[0, h], right_of[h]).astype(BF16))
    decay_of, delta_value_of, delta_right_of = [], [], []
    for h in range(heads):
        decay = pair_decay(cum_col, cum_row, same, h)
        decay_of.append(decay)
        k = ks[h // repeat]
        delta_out = delta_out_ref[:, h * DV : (h + 1) * DV]
        carry = carry_ref[h].astype(BF16)
        delta_value_of.append(
            dot(decay * grams[h // repeat][1], delta_out, TN)
            + dot(end[:, h : h + 1] * k, carry)
        )
    for h in range(heads):
        delta_right_of.append(dot(solve_ref[0, h], delta_value_of[h], TN))
    sums = jnp.zeros((CHUNK, heads), F32)
    logits = jnp.zeros((CHUNK, heads), F32)
    tail = jnp.zeros((1, heads), F32)
    lower_rows = []
    for g in range(key_heads):
        q, k = qs[g], ks[g]
        key_gram, query_gram = grams[g]
        delta_q = jnp.zeros((CHUNK, DK), F32)
        delta_k = jnp.zeros((CHUNK, DK), F32)
        for h in range(g * repeat, (g + 1) * repeat):
            cols = slice(h * DV, (h + 1) * DV)
            b, s, e = beta[:, h : h + 1], start[:, h : h + 1], end[:, h : h + 1]
            delta_out = delta_out_ref[:, cols]
            delta_right = delta_right_of[h]
            delta_value_ref[:, cols] = (b * delta_right).astype(BF16)
            pseudo = value_of[h]
            both = jnp.concatenate([delta_out, delta_right.astype(BF16)], axis=0)
            carry = carry_ref[h]
            pairs = dot(both, pseudo, NT)
            states = dot(both, state_of[h], NT)
            decay = decay_of[h]
            pair_q = decay * pairs[:CHUNK]
            pair_k = jnp.where(strict, (-b) * decay * pairs[CHUNK:], 0.0)
            cross = pair_q * query_gram + pair_k * key_gram
            state_q = s * states[:CHUNK]
            state_k = (b * s) * states[CHUNK:]
            end_k = e * dot(pseudo, carry, NT)
            delta_q += dot(pair_q, k) + state_q
            delta_k += (
                dot(pair_k, k)
                + dot(
                    jnp.concatenate([pair_q, pair_k], axis=0),
                    jnp.concatenate([q, k], axis=0),
                    TN,
                )
                + end_k
                - state_k
            )
            ends = row_sum(end_k * k)
            column = row_sum(cross + state_q * q - state_k * k) - ends
            sums = jnp.where(lane == h, column, sums)
            lower_rows.append(jnp.sum(cross, axis=0, keepdims=True))
            held = total[:, h : h + 1] * jnp.sum(
                state_of[h].astype(F32) * carry, axis=(0, 1), keepdims=True
            )
            tail = jnp.where(lane_one == h, held + jnp.sum(ends, axis=0, keepdims=True), tail)
            logits = jnp.where(lane == h, row_sum(delta_right * pseudo.astype(F32)), logits)
            carry_ref[h] = total[:, h : h + 1] * carry + dot(
                jnp.concatenate([s * q, (-b * s) * k], axis=0), both, TN
            )
        delta_q = delta_q * QUERY_SCALE
        unit = q * (1.0 / QUERY_SCALE)
        delta_q = q_inv[g] * (delta_q - unit * row_sum(unit * delta_q))
        delta_k = k_inv[g] * (delta_k - k * row_sum(k * delta_k))
        delta_query_key_ref[0, :, g * DK : (g + 1) * DK] = delta_q.astype(BF16)
        delta_query_key_ref[1, :, g * DK : (g + 1) * DK] = delta_k.astype(BF16)
    upper = (row <= col).astype(F32)
    reset_col = dot((row == col).astype(F32), resets, NT)[:, 0:1]
    pad = -heads % 8
    if pad:
        lower_rows.append(jnp.zeros((pad, CHUNK), F32))
    below = jnp.concatenate(lower_rows, axis=0)
    delta_log = exact(upper, sums) - exact(upper, below, NT)[:, :heads] + tail
    delta_log = jnp.where(reset_col == 0.0, delta_log, 0.0)
    delta_decay_beta_ref[0] = (
        delta_log * (-scale_ref[...]) * sigmoid(decay_beta_ref[0])
    ).astype(BF16)
    delta_decay_beta_ref[1] = (logits * (1.0 - beta)).astype(BF16)


def chain_forward_kernel(totals_ref, states_ref):
    devices, heads = totals_ref.shape[0], totals_ref.shape[1]
    for h in range(heads):
        state = jnp.zeros(states_ref.shape[2:], F32)
        for i in range(devices):
            states_ref[i, h] = state.astype(BF16)
            if i < devices - 1:
                step = totals_ref[i, h]
                high = state.astype(BF16)
                low = state - high.astype(F32)
                state = (
                    dot(step[:, :DK], high) + dot(step[:, :DK], low) + step[:, DK:].astype(F32)
                )


def chain_backward_kernel(totals_ref, deltas_ref, states_ref):
    devices, heads = totals_ref.shape[0], totals_ref.shape[1]
    for h in range(heads):
        state = jnp.zeros(states_ref.shape[2:], F32)
        for i in reversed(range(devices)):
            states_ref[i, h] = state.astype(BF16)
            if i > 0:
                step = totals_ref[i, h]
                high = state.astype(BF16)
                low = state - high.astype(F32)
                state = (
                    dot(step[:, :DK], high, TN)
                    + dot(step[:, :DK], low, TN)
                    + deltas_ref[i, h].astype(F32)
                )


PARAMS = pltpu.CompilerParams(
    dimension_semantics=("arbitrary",), vmem_limit_bytes=56 * 1024 * 1024
)
INTERPRET = False


def whole(shape):
    return pl.BlockSpec(shape, lambda c: (0,) * len(shape))


def run_forward(query_key, value_gate, decay_beta, bias, scale, resets):
    tokens, heads = query_key.shape[1], decay_beta.shape[2]
    chunks = tokens // CHUNK
    key_width, value_width = query_key.shape[2], heads * DV
    return pl.pallas_call(
        forward_kernel,
        grid=(chunks,),
        in_specs=[
            pl.BlockSpec((2, CHUNK, key_width), lambda c: (0, c, 0)),
            pl.BlockSpec((1, CHUNK, value_width), lambda c: (0, c, 0)),
            pl.BlockSpec((2, CHUNK, heads), lambda c: (0, c, 0)),
            whole((1, heads)),
            whole((1, heads)),
            pl.BlockSpec((1, 1, CHUNK), lambda c: (c, 0, 0)),
        ],
        out_specs=[
            pl.BlockSpec((1, heads, CHUNK, CHUNK), lambda c: (c, 0, 0, 0)),
            pl.BlockSpec((1, heads, DK, DK + DV), lambda c: (c, 0, 0, 0)),
            pl.BlockSpec((CHUNK, value_width), lambda c: (c, 0)),
            pl.BlockSpec((CHUNK, value_width), lambda c: (c, 0)),
            whole((heads, DK, DK + DV)),
        ],
        out_shape=[
            jax.ShapeDtypeStruct((chunks, heads, CHUNK, CHUNK), BF16),
            jax.ShapeDtypeStruct((chunks, heads, DK, DK + DV), BF16),
            jax.ShapeDtypeStruct((tokens, value_width), BF16),
            jax.ShapeDtypeStruct((tokens, value_width), F32),
            jax.ShapeDtypeStruct((heads, DK, DK + DV), BF16),
        ],
        scratch_shapes=[pltpu.VMEM((heads, DK, DK + DV), F32)],
        compiler_params=PARAMS,
        interpret=INTERPRET,
        name="forward_blocks",
    )(query_key, value_gate, decay_beta, bias, scale, resets)


def run_output(local, reach, value_gate, delta_hidden, state_in, gain):
    tokens, value_width = local.shape
    heads = value_width // DV
    chunks = tokens // CHUNK
    block = pl.BlockSpec((CHUNK, value_width), lambda c: (c, 0))
    return pl.pallas_call(
        output_kernel,
        grid=(chunks,),
        in_specs=[
            block,
            block,
            pl.BlockSpec((1, CHUNK, value_width), lambda c: (1, c, 0)),
            block,
            whole((heads, DK, DV)),
            whole((1, DV)),
        ],
        out_specs=[block, block, block, whole((heads, DK, DV))],
        out_shape=[
            jax.ShapeDtypeStruct((tokens, value_width), BF16),
            jax.ShapeDtypeStruct((tokens, value_width), BF16),
            jax.ShapeDtypeStruct((tokens, value_width), BF16),
            jax.ShapeDtypeStruct((heads, DK, DV), BF16),
        ],
        scratch_shapes=[pltpu.VMEM((heads, DK, DV), F32)],
        compiler_params=PARAMS,
        interpret=INTERPRET,
        name="gated_norm",
    )(local, reach, value_gate, delta_hidden, state_in, gain)


def run_backward(
    query_key, value_gate, decay_beta, bias, scale, resets, solve, starts, state_in, delta_out, final
):
    tokens, heads = query_key.shape[1], decay_beta.shape[2]
    chunks = tokens // CHUNK
    key_width, value_width = query_key.shape[2], heads * DV
    last = chunks - 1
    return pl.pallas_call(
        backward_kernel,
        grid=(chunks,),
        in_specs=[
            pl.BlockSpec((2, CHUNK, key_width), lambda c: (0, last - c, 0)),
            pl.BlockSpec((1, CHUNK, value_width), lambda c: (0, last - c, 0)),
            pl.BlockSpec((2, CHUNK, heads), lambda c: (0, last - c, 0)),
            whole((1, heads)),
            whole((1, heads)),
            pl.BlockSpec((1, 1, CHUNK), lambda c: (last - c, 0, 0)),
            pl.BlockSpec((1, heads, CHUNK, CHUNK), lambda c: (last - c, 0, 0, 0)),
            pl.BlockSpec((1, heads, DK, DK + DV), lambda c: (last - c, 0, 0, 0)),
            whole((heads, DK, DV)),
            pl.BlockSpec((CHUNK, value_width), lambda c: (last - c, 0)),
            whole((heads, DK, DV)),
        ],
        out_specs=[
            pl.BlockSpec((2, CHUNK, key_width), lambda c: (0, last - c, 0)),
            pl.BlockSpec((CHUNK, value_width), lambda c: (last - c, 0)),
            pl.BlockSpec((2, CHUNK, heads), lambda c: (0, last - c, 0)),
        ],
        out_shape=[
            jax.ShapeDtypeStruct(query_key.shape, BF16),
            jax.ShapeDtypeStruct((tokens, value_width), BF16),
            jax.ShapeDtypeStruct(decay_beta.shape, BF16),
        ],
        scratch_shapes=[pltpu.VMEM((heads, DK, DV), F32)],
        compiler_params=PARAMS,
        interpret=INTERPRET,
        name="backward_blocks",
    )(query_key, value_gate, decay_beta, bias, scale, resets, solve, starts, state_in, delta_out, final)


def spread(array, devices):
    heads, depth, width = array.shape
    if heads >= devices:
        return array.reshape(devices, heads // devices, depth, width)
    cuts = devices // heads
    parts = array.reshape(heads, depth, cuts, width // cuts)
    return jnp.transpose(parts, (0, 2, 1, 3)).reshape(devices, 1, depth, width // cuts)


def gather_parts(parts, heads):
    devices, each, depth, width = parts.shape
    if heads >= devices:
        return parts.reshape(heads, depth, width)
    cuts = devices // heads
    parts = parts.reshape(heads, cuts, depth, width)
    return jnp.transpose(parts, (0, 2, 1, 3)).reshape(heads, depth, cuts * width)


def swap(parts):
    return lax.all_to_all(parts, "ctx", split_axis=0, concat_axis=0, tiled=True)


def chain_forward(totals):
    devices, heads = lax.axis_size("ctx"), totals.shape[0]
    if heads >= devices:
        parts = spread(totals, devices)
    else:
        maps = jnp.repeat(totals[:, :, :DK], devices // heads, axis=0)[:, None]
        parts = jnp.concatenate([maps, spread(totals[:, :, DK:], devices)], axis=-1)
    held = swap(parts)
    states = pl.pallas_call(
        chain_forward_kernel,
        out_shape=jax.ShapeDtypeStruct((*held.shape[:3], held.shape[3] - DK), BF16),
        interpret=INTERPRET,
        name="chain_forward",
    )(held)
    return gather_parts(swap(states), heads), held


def chain_backward(held, deltas):
    devices, heads = lax.axis_size("ctx"), deltas.shape[0]
    parts = swap(spread(deltas, devices))
    states = pl.pallas_call(
        chain_backward_kernel,
        out_shape=jax.ShapeDtypeStruct(parts.shape, BF16),
        interpret=INTERPRET,
        name="chain_backward",
    )(held, parts)
    return gather_parts(swap(states), heads)


def product(spec, a, b):
    return jnp.einsum(spec, a, b, preferred_element_type=F32)


def scatter(partial, axis, dimension):
    return lax.psum_scatter(partial.astype(BF16), axis, scatter_dimension=dimension, tiled=True)


def body(
    inputs,
    query_key_weight,
    value_gate_weight,
    decay_beta_weight,
    beta_bias,
    decay_scale,
    norm_gain,
    out_weight,
    boundaries,
    grad_mixed,
):
    tokens, heads = inputs.shape[0], beta_bias.shape[0]
    query_key = product("td,sdf->stf", inputs, query_key_weight)
    value_gate = product("td,sdf->stf", inputs, value_gate_weight)
    decay_beta = product("td,sdf->stf", inputs, decay_beta_weight)
    bias, scale = beta_bias.reshape(1, heads), decay_scale.reshape(1, heads)
    resets = boundaries.reshape(tokens // CHUNK, 1, CHUNK)
    solve, starts, reach, local, totals = run_forward(
        query_key, value_gate, decay_beta, bias, scale, resets
    )
    state_in, held = chain_forward(totals)
    delta_hidden = product("td,fd->tf", grad_mixed, out_weight)
    hidden, delta_gate, delta_out, delta_state = run_output(
        local, reach, value_gate, delta_hidden, state_in, norm_gain.reshape(1, DV)
    )
    mixed = scatter(product("tf,fd->td", hidden, out_weight), "head", 1)
    grad_out_weight = scatter(product("tf,td->fd", hidden, grad_mixed), "ctx", 1)
    grad_gate = scatter(product("td,tf->df", inputs, delta_gate), "ctx", 0)
    delta_final = chain_backward(held, delta_state)
    delta_query_key, delta_value, delta_decay_beta = run_backward(
        query_key,
        value_gate,
        decay_beta,
        bias,
        scale,
        resets,
        solve,
        starts,
        state_in,
        delta_out,
        delta_final,
    )
    grad_value = scatter(product("td,tf->df", inputs, delta_value), "ctx", 0)
    grad_query_key = scatter(product("td,stf->sdf", inputs, delta_query_key), "ctx", 1)
    grad_decay_beta = scatter(product("td,stf->sdf", inputs, delta_decay_beta), "ctx", 1)
    grad_rows = (
        product("tf,df->td", delta_gate, value_gate_weight[1])
        + product("stf,sdf->td", delta_query_key, query_key_weight)
        + product("tf,df->td", delta_value, value_gate_weight[0])
        + product("stf,sdf->td", delta_decay_beta, decay_beta_weight)
    )
    grad_inputs = scatter(grad_rows, "head", 1)
    return (
        mixed,
        grad_inputs,
        grad_query_key.astype(F32),
        jnp.stack([grad_value, grad_gate]).astype(F32),
        grad_decay_beta.astype(F32),
        grad_out_weight.astype(F32),
    )


def solution(mesh):
    in_specs = (
        P("ctx", None),
        P(None, None, "head"),
        P(None, None, "head"),
        P(None, None, "head"),
        P("head"),
        P("head"),
        P(),
        P("head", None),
        P("ctx"),
        P("ctx", None),
    )
    out_specs = (
        P("ctx", "head"),
        P("ctx", "head"),
        P(None, "ctx", "head"),
        P(None, "ctx", "head"),
        P(None, "ctx", "head"),
        P("head", "ctx"),
    )
    return jax.shard_map(body, mesh=mesh, in_specs=in_specs, out_specs=out_specs, check_vma=False)
```

```python
import functools

import jax
import jax.numpy as jnp
from jax import lax
from jax.experimental import pallas as pl
from jax.experimental.pallas import tpu as pltpu
from jax.sharding import PartitionSpec as P

DK = 128
DV = 128
CHUNK = 128
EPS = 1e-06
QUERY_SCALE = DK ** (-0.5)
LANES = 128

F32 = jnp.float32
BF16 = jnp.bfloat16
NN = ((1,), (0,))
NT = ((1,), (1,))
TN = ((0,), (0,))


def dot(a, b, dims=NN):
    return lax.dot_general(
        a.astype(BF16), b.astype(BF16), (dims, ((), ())), preferred_element_type=F32
    )


def exact(a, b, dims=NN):
    return lax.dot_general(
        a, b, (dims, ((), ())), precision=lax.Precision.HIGHEST, preferred_element_type=F32
    )


def softplus(x):
    return jnp.maximum(x, 0.0) + jnp.log1p(jnp.exp(-jnp.abs(x)))


def sigmoid(x):
    return 1.0 / (1.0 + jnp.exp(-x))


def row_sum(x):
    return jnp.sum(x, axis=-1, keepdims=True)


def grid_of(size):
    row = lax.broadcasted_iota(jnp.int32, (size, size), 0)
    col = lax.broadcasted_iota(jnp.int32, (size, size), 1)
    return row, col


def decays(decay_beta_ref, bias_ref, scale_ref, resets_ref):
    row, col = grid_of(CHUNK)
    lower = (row >= col).astype(F32)
    decay_logit = decay_beta_ref[0]
    beta = sigmoid(decay_beta_ref[1] + bias_ref[...])
    log_decay = -scale_ref[...] * softplus(decay_logit)
    resets = jnp.broadcast_to(resets_ref[0].astype(F32), (8, CHUNK))
    doc_row = dot(resets, lower, NT)[0:1]
    doc_col = dot(lower, resets, NT)[:, 0:1]
    cum_col = exact(lower, log_decay)
    cum_row = exact(log_decay, lower, ((0,), (1,)))
    same = (doc_col == doc_row) & (row >= col)
    start = jnp.where(doc_col == 0.0, jnp.exp(cum_col), 0.0)
    last = CHUNK - 1
    end = jnp.where(
        doc_col == doc_col[last:],
        jnp.exp(jnp.minimum(cum_col[last:] - cum_col, 0.0)),
        0.0,
    )
    return beta, cum_col, cum_row, same, start, end, start[last:], resets


def pair_decay(cum_col, cum_row, same, h):
    gap = jnp.minimum(cum_col[:, h : h + 1] - cum_row[h : h + 1, :], 0.0)
    return jnp.where(same, jnp.exp(gap), 0.0)


def head(ref, index, h):
    return ref[index][:, h * DK : (h + 1) * DK]


def unit_rows(x):
    inverse = lax.rsqrt(row_sum(x * x) + EPS)
    return x * inverse, inverse


def forward_kernel(
    query_key_ref,
    value_ref,
    decay_beta_ref,
    bias_ref,
    scale_ref,
    resets_ref,
    solve_ref,
    start_ref,
    map_ref,
    local_ref,
    total_ref,
    state_ref,
):
    heads = state_ref.shape[0]
    key_heads = query_key_ref.shape[2] // DK
    repeat = heads // key_heads
    row, col = grid_of(CHUNK)

    @pl.when(pl.program_id(0) == 0)
    def _():
        first = jnp.concatenate([(row == col).astype(F32), jnp.zeros((DK, DV), F32)], axis=1)
        for h in range(heads):
            state_ref[h] = first

    beta, cum_col, cum_row, same, start, end, total, _ = decays(
        decay_beta_ref, bias_ref, scale_ref, resets_ref
    )
    strict = row > col
    differ = row ^ col
    keys, queries, systems, scores = [], [], [], []
    for g in range(key_heads):
        q = unit_rows(head(query_key_ref, 0, g))[0] * QUERY_SCALE
        k = unit_rows(head(query_key_ref, 1, g))[0]
        queries.append(q)
        keys.append(k)
        key_gram = dot(k, k, NT)
        query_gram = dot(q, k, NT)
        for h in range(g * repeat, (g + 1) * repeat):
            decay = pair_decay(cum_col, cum_row, same, h)
            scores.append((decay * query_gram).astype(BF16))
            systems.append(jnp.where(strict, beta[:, h : h + 1] * decay * key_gram, 0.0))
    identity = (row == col).astype(F32)
    inverse = [
        (identity - jnp.where(differ == 1, system, 0.0)).astype(BF16) for system in systems
    ]
    level = 1
    while (1 << level) < CHUNK:
        here = (differ >> level) == 1
        inner = [
            dot(jnp.where(here, system, 0.0), x).astype(BF16)
            for system, x in zip(systems, inverse)
        ]
        inverse = [x - dot(x, y).astype(BF16) for x, y in zip(inverse, inner)]
        level += 1
    weights = []
    for h in range(heads):
        k = keys[h // repeat]
        v = value_ref[:, h * DV : (h + 1) * DV]
        b = beta[:, h : h + 1]
        right = jnp.concatenate([(b * start[:, h : h + 1]) * k, b * v], axis=1)
        weights.append(dot(inverse[h], right))
        solve_ref[0, h] = inverse[h]
    values = []
    for h in range(heads):
        state = state_ref[h].astype(BF16)
        start_ref[0, h] = state
        solved = weights[h]
        base = jnp.concatenate([jnp.zeros((CHUNK, DK), F32), solved[:, DK:]], axis=1)
        values.append((base - dot(solved[:, :DK], state)).astype(BF16))
    for h in range(heads):
        k, q = keys[h // repeat], queries[h // repeat]
        state = state_ref[h]
        out = dot(start[:, h : h + 1] * q, state) + dot(scores[h], values[h])
        map_ref[:, h * DK : (h + 1) * DK] = out[:, :DK].astype(BF16)
        local_ref[:, h * DV : (h + 1) * DV] = out[:, DK:]
        state = total[:, h : h + 1] * state + dot(end[:, h : h + 1] * k, values[h], TN)
        state_ref[h] = state
        total_ref[h] = state.astype(BF16)


def output_kernel(
    local_ref,
    map_ref,
    gate_ref,
    delta_ref,
    state_ref,
    gain_ref,
    hidden_ref,
    delta_gate_ref,
    delta_out_ref,
    delta_state_ref,
    total_ref,
):
    heads = state_ref.shape[0]
    gain = gain_ref[...]

    @pl.when(pl.program_id(0) == 0)
    def _():
        total_ref[...] = jnp.zeros_like(total_ref)

    for h in range(heads):
        cols = slice(h * DV, (h + 1) * DV)
        reach = map_ref[:, cols]
        out = local_ref[:, cols] + dot(reach, state_ref[h])
        gate = gate_ref[:, cols]
        delta = delta_ref[:, cols]
        scale = lax.rsqrt(row_sum(out * out) * (1.0 / DV) + EPS)
        normed = out * scale
        share = sigmoid(gate)
        silu = gate * share
        scaled = normed * gain
        hidden_ref[:, cols] = (scaled * silu).astype(BF16)
        delta_gate_ref[:, cols] = (
            delta * scaled * (share * (1.0 + gate * (1.0 - share)))
        ).astype(BF16)
        delta_normed = delta * gain * silu
        delta_out = scale * (
            delta_normed - normed * (row_sum(normed * delta_normed) * (1.0 / DV))
        )
        delta_out = delta_out.astype(BF16)
        delta_out_ref[:, cols] = delta_out
        part = total_ref[h] + dot(reach, delta_out, TN)
        total_ref[h] = part
        delta_state_ref[h] = part.astype(BF16)


def backward_kernel(
    query_key_ref,
    value_ref,
    decay_beta_ref,
    bias_ref,
    scale_ref,
    resets_ref,
    solve_ref,
    start_ref,
    state_in_ref,
    delta_out_ref,
    delta_final_ref,
    delta_query_key_ref,
    delta_value_ref,
    carry_ref,
):
    heads = carry_ref.shape[0]
    key_heads = query_key_ref.shape[2] // DK
    repeat = heads // key_heads
    row, col = grid_of(CHUNK)

    @pl.when(pl.program_id(0) == 0)
    def _():
        carry_ref[...] = delta_final_ref[...].astype(F32)

    beta, cum_col, cum_row, same, start, end, total, resets = decays(
        decay_beta_ref, bias_ref, scale_ref, resets_ref
    )
    strict = row > col
    lane = lax.broadcasted_iota(jnp.int32, (CHUNK, heads), 1)
    lane_one = lax.broadcasted_iota(jnp.int32, (1, heads), 1)
    state_of, value_of, right_of = [], [], []
    qs, ks, q_inv, k_inv, grams = [], [], [], [], []
    for g in range(key_heads):
        q, qi = unit_rows(head(query_key_ref, 0, g))
        k, ki = unit_rows(head(query_key_ref, 1, g))
        q = q * QUERY_SCALE
        qs.append(q)
        ks.append(k)
        q_inv.append(qi)
        k_inv.append(ki)
        grams.append((dot(k, k, NT), dot(q, k, NT)))
    for h in range(heads):
        before = start_ref[0, h]
        state = dot(before[:, :DK], state_in_ref[h]) + before[:, DK:].astype(F32)
        state_of.append(state.astype(BF16))
    for h in range(heads):
        k = ks[h // repeat]
        v = value_ref[:, h * DV : (h + 1) * DV]
        seen = dot(k, state_of[h])
        right_of.append(beta[:, h : h + 1] * (v - start[:, h : h + 1] * seen))
    for h in range(heads):
        value_of.append(dot(solve_ref[0, h], right_of[h]).astype(BF16))
    decay_of, delta_value_of, delta_right_of = [], [], []
    for h in range(heads):
        decay = pair_decay(cum_col, cum_row, same, h)
        decay_of.append(decay)
        k = ks[h // repeat]
        delta_out = delta_out_ref[:, h * DV : (h + 1) * DV]
        carry = carry_ref[h].astype(BF16)
        delta_value_of.append(
            dot(decay * grams[h // repeat][1], delta_out, TN)
            + dot(end[:, h : h + 1] * k, carry)
        )
    for h in range(heads):
        delta_right_of.append(dot(solve_ref[0, h], delta_value_of[h], TN))
    sums = jnp.zeros((CHUNK, heads), F32)
    logits = jnp.zeros((CHUNK, heads), F32)
    tail = jnp.zeros((1, heads), F32)
    lower_rows = []
    for g in range(key_heads):
        q, k = qs[g], ks[g]
        key_gram, query_gram = grams[g]
        delta_q = jnp.zeros((CHUNK, DK), F32)
        delta_k = jnp.zeros((CHUNK, DK), F32)
        for h in range(g * repeat, (g + 1) * repeat):
            cols = slice(h * DV, (h + 1) * DV)
            b, s, e = beta[:, h : h + 1], start[:, h : h + 1], end[:, h : h + 1]
            delta_out = delta_out_ref[:, cols]
            delta_right = delta_right_of[h]
            delta_value_ref[:, cols] = (b * delta_right).astype(BF16)
            pseudo = value_of[h]
            both = jnp.concatenate([delta_out, delta_right.astype(BF16)], axis=0)
            carry = carry_ref[h]
            pairs = dot(both, pseudo, NT)
            states = dot(both, state_of[h], NT)
            decay = decay_of[h]
            pair_q = decay * pairs[:CHUNK]
            pair_k = jnp.where(strict, (-b) * decay * pairs[CHUNK:], 0.0)
            cross = pair_q * query_gram + pair_k * key_gram
            state_q = s * states[:CHUNK]
            state_k = (b * s) * states[CHUNK:]
            end_k = e * dot(pseudo, carry, NT)
            delta_q += dot(pair_q, k) + state_q
            delta_k += (
                dot(pair_k, k)
                + dot(
                    jnp.concatenate([pair_q, pair_k], axis=0),
                    jnp.concatenate([q, k], axis=0),
                    TN,
                )
                + end_k
                - state_k
            )
            ends = row_sum(end_k * k)
            column = row_sum(cross + state_q * q - state_k * k) - ends
            sums = jnp.where(lane == h, column, sums)
            lower_rows.append(jnp.sum(cross, axis=0, keepdims=True))
            held = total[:, h : h + 1] * jnp.sum(
                state_of[h].astype(F32) * carry, axis=(0, 1), keepdims=True
            )
            tail = jnp.where(lane_one == h, held + jnp.sum(ends, axis=0, keepdims=True), tail)
            logits = jnp.where(lane == h, row_sum(delta_right * pseudo.astype(F32)), logits)
            carry_ref[h] = total[:, h : h + 1] * carry + dot(
                jnp.concatenate([s * q, (-b * s) * k], axis=0), both, TN
            )
        delta_q = delta_q * QUERY_SCALE
        unit = q * (1.0 / QUERY_SCALE)
        delta_q = q_inv[g] * (delta_q - unit * row_sum(unit * delta_q))
        delta_k = k_inv[g] * (delta_k - k * row_sum(k * delta_k))
        delta_query_key_ref[:, g * DK : (g + 1) * DK] = delta_q.astype(BF16)
        delta_query_key_ref[:, (key_heads + g) * DK : (key_heads + g + 1) * DK] = (
            delta_k.astype(BF16)
        )
    upper = (row <= col).astype(F32)
    reset_col = dot((row == col).astype(F32), resets, NT)[:, 0:1]
    pad = -heads % 8
    if pad:
        lower_rows.append(jnp.zeros((pad, CHUNK), F32))
    below = jnp.concatenate(lower_rows, axis=0)
    delta_log = exact(upper, sums) - exact(upper, below, NT)[:, :heads] + tail
    delta_log = jnp.where(reset_col == 0.0, delta_log, 0.0)
    delta_decay = delta_log * (-scale_ref[...]) * sigmoid(decay_beta_ref[0])
    delta_beta = logits * (1.0 - beta)
    rest = jnp.zeros((CHUNK, LANES - 2 * heads), F32)
    delta_query_key_ref[:, 2 * key_heads * DK :] = jnp.concatenate(
        [delta_decay, delta_beta, rest], axis=1
    ).astype(BF16)


def chain_forward_kernel(totals_ref, states_ref):
    devices, heads = totals_ref.shape[0], totals_ref.shape[1]
    for h in range(heads):
        state = jnp.zeros(states_ref.shape[2:], F32)
        for i in range(devices):
            states_ref[i, h] = state.astype(BF16)
            if i < devices - 1:
                step = totals_ref[i, h]
                high = state.astype(BF16)
                low = state - high.astype(F32)
                state = (
                    dot(step[:, :DK], high) + dot(step[:, :DK], low) + step[:, DK:].astype(F32)
                )


def chain_backward_kernel(totals_ref, deltas_ref, states_ref):
    devices, heads = totals_ref.shape[0], totals_ref.shape[1]
    for h in range(heads):
        state = jnp.zeros(states_ref.shape[2:], F32)
        for i in reversed(range(devices)):
            states_ref[i, h] = state.astype(BF16)
            if i > 0:
                step = totals_ref[i, h]
                high = state.astype(BF16)
                low = state - high.astype(F32)
                state = (
                    dot(step[:, :DK], high, TN)
                    + dot(step[:, :DK], low, TN)
                    + deltas_ref[i, h].astype(F32)
                )


PARAMS = pltpu.CompilerParams(
    dimension_semantics=("arbitrary",), vmem_limit_bytes=56 * 1024 * 1024
)
INTERPRET = False


def whole(shape):
    return pl.BlockSpec(shape, lambda c: (0,) * len(shape))


def run_forward(query_key, value, decay_beta, bias, scale, resets):
    tokens, heads = query_key.shape[1], decay_beta.shape[2]
    chunks = tokens // CHUNK
    key_width, value_width = query_key.shape[2], heads * DV
    return pl.pallas_call(
        forward_kernel,
        grid=(chunks,),
        in_specs=[
            pl.BlockSpec((2, CHUNK, key_width), lambda c: (0, c, 0)),
            pl.BlockSpec((CHUNK, value_width), lambda c: (c, 0)),
            pl.BlockSpec((2, CHUNK, heads), lambda c: (0, c, 0)),
            whole((1, heads)),
            whole((1, heads)),
            pl.BlockSpec((1, 1, CHUNK), lambda c: (c, 0, 0)),
        ],
        out_specs=[
            pl.BlockSpec((1, heads, CHUNK, CHUNK), lambda c: (c, 0, 0, 0)),
            pl.BlockSpec((1, heads, DK, DK + DV), lambda c: (c, 0, 0, 0)),
            pl.BlockSpec((CHUNK, value_width), lambda c: (c, 0)),
            pl.BlockSpec((CHUNK, value_width), lambda c: (c, 0)),
            whole((heads, DK, DK + DV)),
        ],
        out_shape=[
            jax.ShapeDtypeStruct((chunks, heads, CHUNK, CHUNK), BF16),
            jax.ShapeDtypeStruct((chunks, heads, DK, DK + DV), BF16),
            jax.ShapeDtypeStruct((tokens, value_width), BF16),
            jax.ShapeDtypeStruct((tokens, value_width), F32),
            jax.ShapeDtypeStruct((heads, DK, DK + DV), BF16),
        ],
        scratch_shapes=[pltpu.VMEM((heads, DK, DK + DV), F32)],
        compiler_params=PARAMS,
        interpret=INTERPRET,
        name="forward_blocks",
    )(query_key, value, decay_beta, bias, scale, resets)


def run_output(local, reach, gate, delta_hidden, state_in, gain):
    tokens, value_width = local.shape
    heads = value_width // DV
    chunks = tokens // CHUNK
    block = pl.BlockSpec((CHUNK, value_width), lambda c: (c, 0))
    return pl.pallas_call(
        output_kernel,
        grid=(chunks,),
        in_specs=[
            block,
            block,
            block,
            block,
            whole((heads, DK, DV)),
            whole((1, DV)),
        ],
        out_specs=[block, block, block, whole((heads, DK, DV))],
        out_shape=[
            jax.ShapeDtypeStruct((tokens, value_width), BF16),
            jax.ShapeDtypeStruct((tokens, value_width), BF16),
            jax.ShapeDtypeStruct((tokens, value_width), BF16),
            jax.ShapeDtypeStruct((heads, DK, DV), BF16),
        ],
        scratch_shapes=[pltpu.VMEM((heads, DK, DV), F32)],
        compiler_params=PARAMS,
        interpret=INTERPRET,
        name="gated_norm",
    )(local, reach, gate, delta_hidden, state_in, gain)


def run_backward(
    query_key, value, decay_beta, bias, scale, resets, solve, starts, state_in, delta_out, final
):
    tokens, heads = query_key.shape[1], decay_beta.shape[2]
    chunks = tokens // CHUNK
    key_width, value_width = query_key.shape[2], heads * DV
    last = chunks - 1
    return pl.pallas_call(
        backward_kernel,
        grid=(chunks,),
        in_specs=[
            pl.BlockSpec((2, CHUNK, key_width), lambda c: (0, last - c, 0)),
            pl.BlockSpec((CHUNK, value_width), lambda c: (last - c, 0)),
            pl.BlockSpec((2, CHUNK, heads), lambda c: (0, last - c, 0)),
            whole((1, heads)),
            whole((1, heads)),
            pl.BlockSpec((1, 1, CHUNK), lambda c: (last - c, 0, 0)),
            pl.BlockSpec((1, heads, CHUNK, CHUNK), lambda c: (last - c, 0, 0, 0)),
            pl.BlockSpec((1, heads, DK, DK + DV), lambda c: (last - c, 0, 0, 0)),
            whole((heads, DK, DV)),
            pl.BlockSpec((CHUNK, value_width), lambda c: (last - c, 0)),
            whole((heads, DK, DV)),
        ],
        out_specs=[
            pl.BlockSpec((CHUNK, 2 * key_width + LANES), lambda c: (last - c, 0)),
            pl.BlockSpec((CHUNK, value_width), lambda c: (last - c, 0)),
        ],
        out_shape=[
            jax.ShapeDtypeStruct((tokens, 2 * key_width + LANES), BF16),
            jax.ShapeDtypeStruct((tokens, value_width), BF16),
        ],
        scratch_shapes=[pltpu.VMEM((heads, DK, DV), F32)],
        compiler_params=PARAMS,
        interpret=INTERPRET,
        name="backward_blocks",
    )(query_key, value, decay_beta, bias, scale, resets, solve, starts, state_in, delta_out, final)


def spread(array, devices):
    heads, depth, width = array.shape
    if heads >= devices:
        return array.reshape(devices, heads // devices, depth, width)
    cuts = devices // heads
    parts = array.reshape(heads, depth, cuts, width // cuts)
    return jnp.transpose(parts, (0, 2, 1, 3)).reshape(devices, 1, depth, width // cuts)


def gather_parts(parts, heads):
    devices, each, depth, width = parts.shape
    if heads >= devices:
        return parts.reshape(heads, depth, width)
    cuts = devices // heads
    parts = parts.reshape(heads, cuts, depth, width)
    return jnp.transpose(parts, (0, 2, 1, 3)).reshape(heads, depth, cuts * width)


def swap(parts):
    return lax.all_to_all(parts, "ctx", split_axis=0, concat_axis=0, tiled=True)


def spread_totals(totals):
    devices, heads = lax.axis_size("ctx"), totals.shape[0]
    if heads >= devices:
        return spread(totals, devices)
    maps = jnp.repeat(totals[:, :, :DK], devices // heads, axis=0)[:, None]
    return jnp.concatenate([maps, spread(totals[:, :, DK:], devices)], axis=-1)


def run_chain_forward(held):
    return pl.pallas_call(
        chain_forward_kernel,
        out_shape=jax.ShapeDtypeStruct((*held.shape[:3], held.shape[3] - DK), BF16),
        interpret=INTERPRET,
        name="chain_forward",
    )(held)


def run_chain_backward(held, deltas):
    return pl.pallas_call(
        chain_backward_kernel,
        out_shape=jax.ShapeDtypeStruct(deltas.shape, BF16),
        interpret=INTERPRET,
        name="chain_backward",
    )(held, deltas)


def product(spec, a, b):
    return jnp.einsum(spec, a, b, preferred_element_type=F32)


def projection_kernel(
    inputs_ref,
    query_key_weight_ref,
    value_weight_ref,
    decay_beta_weight_ref,
    query_key_ref,
    value_ref,
    decay_beta_ref,
):
    inputs = inputs_ref[...]
    query_key_ref[0] = dot(inputs, query_key_weight_ref[0])
    query_key_ref[1] = dot(inputs, query_key_weight_ref[1])
    value_ref[...] = dot(inputs, value_weight_ref[0])

    @pl.when(pl.program_id(0) == 0)
    def _():
        decay_beta_ref[0] = dot(inputs, decay_beta_weight_ref[0])
        decay_beta_ref[1] = dot(inputs, decay_beta_weight_ref[1])


def run_projection(inputs, query_key_weight, value_gate_weight, decay_beta_weight):
    tokens, model = inputs.shape
    key_width, value_width = query_key_weight.shape[2], value_gate_weight.shape[2]
    heads = decay_beta_weight.shape[2]
    steps = 2
    keys, values = key_width // steps, value_width // steps
    return pl.pallas_call(
        projection_kernel,
        grid=(steps,),
        in_specs=[
            whole((tokens, model)),
            pl.BlockSpec((2, model, keys), lambda j: (0, 0, j)),
            pl.BlockSpec((1, model, values), lambda j: (0, 0, j)),
            whole((2, model, heads)),
        ],
        out_specs=[
            pl.BlockSpec((2, tokens, keys), lambda j: (0, 0, j)),
            pl.BlockSpec((tokens, values), lambda j: (0, j)),
            whole((2, tokens, heads)),
        ],
        out_shape=[
            jax.ShapeDtypeStruct((2, tokens, key_width), F32),
            jax.ShapeDtypeStruct((tokens, value_width), F32),
            jax.ShapeDtypeStruct((2, tokens, heads), F32),
        ],
        compiler_params=PARAMS,
        interpret=INTERPRET,
        name="projection",
    )(inputs, query_key_weight, value_gate_weight, decay_beta_weight)


def input_gradient_kernel(
    delta_query_key_ref,
    delta_value_ref,
    delta_gate_ref,
    query_key_weight_ref,
    value_gate_weight_ref,
    decay_beta_weight_ref,
    out_ref,
):
    rows = decay_beta_weight_ref.shape[1]
    heads = decay_beta_weight_ref.shape[2]
    packed = jnp.concatenate(
        [
            query_key_weight_ref[0],
            query_key_weight_ref[1],
            decay_beta_weight_ref[0],
            decay_beta_weight_ref[1],
            jnp.zeros((rows, LANES - 2 * heads), BF16),
        ],
        axis=1,
    )
    total = dot(delta_gate_ref[...], value_gate_weight_ref[1], NT)
    total += dot(delta_value_ref[...], value_gate_weight_ref[0], NT)
    total += dot(delta_query_key_ref[...], packed, NT)
    out_ref[...] = total.astype(BF16)


def run_input_gradient(
    delta_query_key, delta_value, delta_gate, query_key_weight, value_gate_weight, decay_beta_weight
):
    tokens, model = delta_value.shape[0], query_key_weight.shape[1]
    cut = 256

    def weight(array):
        return pl.BlockSpec((2, cut, array.shape[2]), lambda j: (0, j, 0))

    return pl.pallas_call(
        input_gradient_kernel,
        grid=(model // cut,),
        in_specs=[
            whole(delta_query_key.shape),
            whole(delta_value.shape),
            whole(delta_gate.shape),
            weight(query_key_weight),
            weight(value_gate_weight),
            weight(decay_beta_weight),
        ],
        out_specs=pl.BlockSpec((tokens, cut), lambda j: (0, j)),
        out_shape=jax.ShapeDtypeStruct((tokens, model), BF16),
        compiler_params=PARAMS,
        interpret=INTERPRET,
        name="input_gradient",
    )(delta_query_key, delta_value, delta_gate, query_key_weight, value_gate_weight, decay_beta_weight)


def together(*arrays):
    return lax.optimization_barrier(arrays)


def exchange(array, distance):
    devices = range(lax.axis_size("ctx"))
    return lax.ppermute(array, "ctx", [(i, i ^ distance) for i in devices])


def block_of(step, place, flip):
    x, y = (place // 2) % 2, place // 4
    core = lax.rem(place + flip, 2)
    across_x, across_y = 1 - step // 2, 1 - lax.rem(step, 2)
    target_x, target_y = lax.rem(x + across_x, 2), lax.rem(y + across_y, 2)
    return target_y * 4 + target_x * 2 + core


def send_kernel(place_ref, left_ref, delta_ref, out_ref):
    out_ref[...] = dot(left_ref[...], delta_ref[...], TN).astype(BF16)


def keep_kernel(
    place_ref, left_ref, delta_ref, arrived_ref, x_send_ref, x_keep_ref, y_send_ref, y_keep_ref
):
    step = pl.program_id(0)
    cut = x_send_ref.shape[2]
    total = dot(left_ref[...], delta_ref[...], TN) + arrived_ref[...].astype(F32)
    total = total.astype(BF16)

    @pl.when(step < 2)
    def _():
        x_send_ref[0] = total[:, :cut]

    @pl.when(step >= 2)
    def _():
        x_keep_ref[0] = total[:, :cut]

    @pl.when(lax.rem(step, 2) == 0)
    def _():
        y_send_ref[0] = total[:, cut:]

    @pl.when(lax.rem(step, 2) == 1)
    def _():
        y_keep_ref[0] = total[:, cut:]


def halving_start(place, left, delta):
    tokens, width = delta.shape
    rows = left.shape[1] // 8
    send = pl.pallas_call(
        send_kernel,
        grid_spec=pltpu.PrefetchScalarGridSpec(
            num_scalar_prefetch=1,
            grid=(4,),
            in_specs=[
                pl.BlockSpec((tokens, rows), lambda i, place: (0, block_of(i, place[0], 1))),
                pl.BlockSpec((tokens, width), lambda i, place: (0, 0)),
            ],
            out_specs=pl.BlockSpec((rows, width), lambda i, place: (i, 0)),
        ),
        out_shape=jax.ShapeDtypeStruct((4 * rows, width), BF16),
        compiler_params=PARAMS,
        interpret=INTERPRET,
        name="send_rows",
    )(place, left, delta)
    return exchange(send, 1)


def halving_keep(place, left, delta, arrived):
    tokens, width = delta.shape
    rows = left.shape[1] // 8
    cut = -(-(width // 2) // LANES) * LANES
    return pl.pallas_call(
        keep_kernel,
        grid_spec=pltpu.PrefetchScalarGridSpec(
            num_scalar_prefetch=1,
            grid=(4,),
            in_specs=[
                pl.BlockSpec((tokens, rows), lambda i, place: (0, block_of(i, place[0], 0))),
                pl.BlockSpec((tokens, width), lambda i, place: (0, 0)),
                pl.BlockSpec((rows, width), lambda i, place: (i, 0)),
            ],
            out_specs=[
                pl.BlockSpec((1, rows, cut), lambda i, place: (jnp.minimum(i, 1), 0, 0)),
                pl.BlockSpec((1, rows, cut), lambda i, place: (jnp.maximum(i - 2, 0), 0, 0)),
                pl.BlockSpec((1, rows, width - cut), lambda i, place: (i // 2, 0, 0)),
                pl.BlockSpec((1, rows, width - cut), lambda i, place: (i // 2, 0, 0)),
            ],
        ),
        out_shape=[
            jax.ShapeDtypeStruct((2, rows, cut), BF16),
            jax.ShapeDtypeStruct((2, rows, cut), BF16),
            jax.ShapeDtypeStruct((2, rows, width - cut), BF16),
            jax.ShapeDtypeStruct((2, rows, width - cut), BF16),
        ],
        compiler_params=PARAMS,
        interpret=INTERPRET,
        name="keep_rows",
    )(place, left, delta, arrived)


def halving_cross(x_send, x_keep, y_send, y_keep):
    return x_keep, exchange(x_send, 2), y_keep, exchange(y_send, 4)


def halving_last(a, a_arrived, b, b_arrived):
    a_send = (a[0].astype(F32) + a_arrived[0].astype(F32)).astype(BF16)
    b_send = (b[0].astype(F32) + b_arrived[0].astype(F32)).astype(BF16)
    return a[1], a_arrived[1], exchange(a_send, 4), b[1], b_arrived[1], exchange(b_send, 2)


def halving_sum(*pieces):
    a, a_near, a_far, b, b_near, b_far = [piece.astype(F32) for piece in pieces]
    return jnp.concatenate([a + a_near + a_far, b + b_near + b_far], axis=1)


def scatter(partial, axis, dimension):
    return lax.psum_scatter(partial.astype(BF16), axis, scatter_dimension=dimension, tiled=True)


def body(
    inputs,
    query_key_weight,
    value_gate_weight,
    decay_beta_weight,
    beta_bias,
    decay_scale,
    norm_gain,
    out_weight,
    boundaries,
    grad_mixed,
):
    tokens, heads = inputs.shape[0], beta_bias.shape[0]
    key_width = query_key_weight.shape[2]
    cubic = lax.axis_size("ctx") == 8
    query_key, value, decay_beta = run_projection(
        inputs, query_key_weight, value_gate_weight, decay_beta_weight
    )
    bias, scale = beta_bias.reshape(1, heads), decay_scale.reshape(1, heads)
    resets = boundaries.reshape(tokens // CHUNK, 1, CHUNK)
    solve, starts, reach, local, totals = run_forward(
        query_key, value, decay_beta, bias, scale, resets
    )

    held = swap(spread_totals(totals))
    gate = product("td,df->tf", inputs, value_gate_weight[1])
    held, gate = together(held, gate)
    states = swap(run_chain_forward(held))
    delta_hidden = product("td,fd->tf", grad_mixed, out_weight)
    states, delta_hidden = together(states, delta_hidden)
    state_in = gather_parts(states, heads)
    hidden, delta_gate, delta_out, delta_state = run_output(
        local, reach, gate, delta_hidden, state_in, norm_gain.reshape(1, DV)
    )

    deltas = swap(spread(delta_state, lax.axis_size("ctx")))
    partial_out = product("tf,fd->td", hidden, out_weight).astype(BF16)
    deltas, partial_out = together(deltas, partial_out)
    mixed = scatter(partial_out, "head", 1)
    finals = swap(run_chain_backward(held, deltas))
    if cubic:
        place = lax.axis_index("ctx").astype(jnp.int32).reshape(1)
        place, deltas = together(place, deltas)
        gate_sent = halving_start(place, inputs, delta_gate)
        out_sent = halving_start(place, grad_mixed, hidden)
        gate_cut = halving_keep(place, inputs, delta_gate, gate_sent)
        out_cut = halving_keep(place, grad_mixed, hidden, out_sent)
        finals, gate_cut, out_cut = together(finals, gate_cut, out_cut)
        gate_next, out_next = halving_cross(*gate_cut), halving_cross(*out_cut)
    delta_final = gather_parts(finals, heads)
    delta_query_key, delta_value = run_backward(
        query_key,
        value,
        decay_beta,
        bias,
        scale,
        resets,
        solve,
        starts,
        state_in,
        delta_out,
        delta_final,
    )
    if cubic:
        value_sent = halving_start(place, inputs, delta_value)
        query_key_sent = halving_start(place, inputs, delta_query_key)
        value_next = halving_cross(*halving_keep(place, inputs, delta_value, value_sent))
        query_key_next = halving_cross(
            *halving_keep(place, inputs, delta_query_key, query_key_sent)
        )
    grad_rows = run_input_gradient(
        delta_query_key,
        delta_value,
        delta_gate,
        query_key_weight,
        value_gate_weight,
        decay_beta_weight,
    )
    grad_inputs = scatter(grad_rows, "head", 1)
    if cubic:
        grad_gate = halving_sum(*halving_last(*gate_next))
        grad_out = halving_sum(*halving_last(*out_next)).T
        grad_value = halving_sum(*halving_last(*value_next))
        packed = halving_sum(*halving_last(*query_key_next))
    else:
        grad_gate = scatter(product("td,tf->df", inputs, delta_gate), "ctx", 0).astype(F32)
        grad_out = scatter(product("tf,td->fd", hidden, grad_mixed), "ctx", 1).astype(F32)
        grad_value = scatter(product("td,tf->df", inputs, delta_value), "ctx", 0).astype(F32)
        packed = scatter(product("td,tf->df", inputs, delta_query_key), "ctx", 0).astype(F32)
    rest = packed[:, 2 * key_width :]
    return (
        mixed,
        grad_inputs,
        jnp.stack([packed[:, :key_width], packed[:, key_width : 2 * key_width]]),
        jnp.stack([grad_value, grad_gate]),
        jnp.stack([rest[:, :heads], rest[:, heads : 2 * heads]]),
        grad_out,
    )


def solution(mesh):
    in_specs = (
        P("ctx", None),
        P(None, None, "head"),
        P(None, None, "head"),
        P(None, None, "head"),
        P("head"),
        P("head"),
        P(),
        P("head", None),
        P("ctx"),
        P("ctx", None),
    )
    out_specs = (
        P("ctx", "head"),
        P("ctx", "head"),
        P(None, "ctx", "head"),
        P(None, "ctx", "head"),
        P(None, "ctx", "head"),
        P("head", "ctx"),
    )
    return jax.shard_map(body, mesh=mesh, in_specs=in_specs, out_specs=out_specs, check_vma=False)
```

```python
import functools

import jax
import jax.numpy as jnp
from jax import lax
from jax.experimental import pallas as pl
from jax.experimental.pallas import tpu as pltpu
from jax.sharding import PartitionSpec as P

DK = 128
DV = 128
CHUNK = 128
EPS = 1e-06
QUERY_SCALE = DK ** (-0.5)
LANES = 128

F32 = jnp.float32
BF16 = jnp.bfloat16
NN = ((1,), (0,))
NT = ((1,), (1,))
TN = ((0,), (0,))


def dot(a, b, dims=NN):
    return lax.dot_general(
        a.astype(BF16), b.astype(BF16), (dims, ((), ())), preferred_element_type=F32
    )


def exact(a, b, dims=NN):
    return lax.dot_general(
        a, b, (dims, ((), ())), precision=lax.Precision.HIGHEST, preferred_element_type=F32
    )


def softplus(x):
    return jnp.maximum(x, 0.0) + jnp.log1p(jnp.exp(-jnp.abs(x)))


def sigmoid(x):
    return 1.0 / (1.0 + jnp.exp(-x))


def row_sum(x):
    return jnp.sum(x, axis=-1, keepdims=True)


def grid_of(size):
    row = lax.broadcasted_iota(jnp.int32, (size, size), 0)
    col = lax.broadcasted_iota(jnp.int32, (size, size), 1)
    return row, col


def decays(decay_beta_ref, bias_ref, scale_ref, resets_ref):
    row, col = grid_of(CHUNK)
    lower = (row >= col).astype(F32)
    heads = bias_ref.shape[1]
    decay_logit = decay_beta_ref[:, :heads]
    beta = sigmoid(decay_beta_ref[:, heads:] + bias_ref[...])
    log_decay = -scale_ref[...] * softplus(decay_logit)
    resets = jnp.broadcast_to(resets_ref[0].astype(F32), (8, CHUNK))
    doc_row = dot(resets, lower, NT)[0:1]
    doc_col = dot(lower, resets, NT)[:, 0:1]
    cum_col = exact(lower, log_decay)
    cum_row = exact(log_decay, lower, ((0,), (1,)))
    same = (doc_col == doc_row) & (row >= col)
    start = jnp.where(doc_col == 0.0, jnp.exp(cum_col), 0.0)
    last = CHUNK - 1
    end = jnp.where(
        doc_col == doc_col[last:],
        jnp.exp(jnp.minimum(cum_col[last:] - cum_col, 0.0)),
        0.0,
    )
    return beta, cum_col, cum_row, same, start, end, start[last:], resets


def pair_decay(cum_col, cum_row, same, h):
    gap = jnp.minimum(cum_col[:, h : h + 1] - cum_row[h : h + 1, :], 0.0)
    return jnp.where(same, jnp.exp(gap), 0.0)


def head(ref, index, h):
    return ref[index][:, h * DK : (h + 1) * DK]


def unit_rows(x):
    inverse = lax.rsqrt(row_sum(x * x) + EPS)
    return x * inverse, inverse


def forward_kernel(
    query_key_ref,
    value_ref,
    decay_beta_ref,
    bias_ref,
    scale_ref,
    resets_ref,
    solve_ref,
    start_ref,
    map_ref,
    local_ref,
    total_ref,
    state_ref,
):
    heads = state_ref.shape[0]
    key_heads = query_key_ref.shape[2] // DK
    repeat = heads // key_heads
    row, col = grid_of(CHUNK)

    @pl.when(pl.program_id(0) == 0)
    def _():
        first = jnp.concatenate([(row == col).astype(F32), jnp.zeros((DK, DV), F32)], axis=1)
        for h in range(heads):
            state_ref[h] = first

    beta, cum_col, cum_row, same, start, end, total, _ = decays(
        decay_beta_ref, bias_ref, scale_ref, resets_ref
    )
    strict = row > col
    differ = row ^ col
    keys, queries, systems, scores = [], [], [], []
    for g in range(key_heads):
        q = unit_rows(head(query_key_ref, 0, g))[0] * QUERY_SCALE
        k = unit_rows(head(query_key_ref, 1, g))[0]
        queries.append(q)
        keys.append(k)
        key_gram = dot(k, k, NT)
        query_gram = dot(q, k, NT)
        for h in range(g * repeat, (g + 1) * repeat):
            decay = pair_decay(cum_col, cum_row, same, h)
            scores.append((decay * query_gram).astype(BF16))
            systems.append(jnp.where(strict, beta[:, h : h + 1] * decay * key_gram, 0.0))
    identity = (row == col).astype(F32)
    inverse = [
        (identity - jnp.where(differ == 1, system, 0.0)).astype(BF16) for system in systems
    ]
    level = 1
    while (1 << level) < CHUNK:
        here = (differ >> level) == 1
        inner = [
            dot(jnp.where(here, system, 0.0), x).astype(BF16)
            for system, x in zip(systems, inverse)
        ]
        inverse = [x - dot(x, y).astype(BF16) for x, y in zip(inverse, inner)]
        level += 1
    weights = []
    for h in range(heads):
        k = keys[h // repeat]
        v = value_ref[:, h * DV : (h + 1) * DV]
        b = beta[:, h : h + 1]
        right = jnp.concatenate([(b * start[:, h : h + 1]) * k, b * v], axis=1)
        weights.append(dot(inverse[h], right))
        solve_ref[0, h] = inverse[h]
    values = []
    for h in range(heads):
        state = state_ref[h].astype(BF16)
        start_ref[0, h] = state
        solved = weights[h]
        base = jnp.concatenate([jnp.zeros((CHUNK, DK), F32), solved[:, DK:]], axis=1)
        values.append((base - dot(solved[:, :DK], state)).astype(BF16))
    for h in range(heads):
        k, q = keys[h // repeat], queries[h // repeat]
        state = state_ref[h]
        out = dot(start[:, h : h + 1] * q, state) + dot(scores[h], values[h])
        map_ref[:, h * DK : (h + 1) * DK] = out[:, :DK].astype(BF16)
        local_ref[:, h * DV : (h + 1) * DV] = out[:, DK:]
        state = total[:, h : h + 1] * state + dot(end[:, h : h + 1] * k, values[h], TN)
        state_ref[h] = state
        total_ref[h] = state.astype(BF16)


def output_kernel(
    local_ref,
    map_ref,
    gate_ref,
    delta_ref,
    state_ref,
    gain_ref,
    hidden_ref,
    delta_gate_ref,
    delta_out_ref,
    delta_state_ref,
    total_ref,
):
    heads = state_ref.shape[0]
    gain = gain_ref[...]

    @pl.when(pl.program_id(0) == 0)
    def _():
        total_ref[...] = jnp.zeros_like(total_ref)

    for h in range(heads):
        cols = slice(h * DV, (h + 1) * DV)
        reach = map_ref[:, cols]
        out = local_ref[:, cols] + dot(reach, state_ref[h])
        gate = gate_ref[:, cols]
        delta = delta_ref[:, cols]
        scale = lax.rsqrt(row_sum(out * out) * (1.0 / DV) + EPS)
        normed = out * scale
        share = sigmoid(gate)
        silu = gate * share
        scaled = normed * gain
        hidden_ref[:, cols] = (scaled * silu).astype(BF16)
        delta_gate_ref[:, cols] = (
            delta * scaled * (share * (1.0 + gate * (1.0 - share)))
        ).astype(BF16)
        delta_normed = delta * gain * silu
        delta_out = scale * (
            delta_normed - normed * (row_sum(normed * delta_normed) * (1.0 / DV))
        )
        delta_out = delta_out.astype(BF16)
        delta_out_ref[:, cols] = delta_out
        part = total_ref[h] + dot(reach, delta_out, TN)
        total_ref[h] = part
        delta_state_ref[h] = part.astype(BF16)


def backward_kernel(
    query_key_ref,
    value_ref,
    decay_beta_ref,
    bias_ref,
    scale_ref,
    resets_ref,
    solve_ref,
    start_ref,
    state_in_ref,
    delta_out_ref,
    delta_final_ref,
    delta_query_key_ref,
    delta_value_ref,
    carry_ref,
):
    heads = carry_ref.shape[0]
    key_heads = query_key_ref.shape[2] // DK
    repeat = heads // key_heads
    row, col = grid_of(CHUNK)

    @pl.when(pl.program_id(0) == 0)
    def _():
        carry_ref[...] = delta_final_ref[...].astype(F32)

    beta, cum_col, cum_row, same, start, end, total, resets = decays(
        decay_beta_ref, bias_ref, scale_ref, resets_ref
    )
    strict = row > col
    lane = lax.broadcasted_iota(jnp.int32, (CHUNK, heads), 1)
    lane_one = lax.broadcasted_iota(jnp.int32, (1, heads), 1)
    state_of, value_of, right_of = [], [], []
    qs, ks, q_inv, k_inv, grams = [], [], [], [], []
    for g in range(key_heads):
        q, qi = unit_rows(head(query_key_ref, 0, g))
        k, ki = unit_rows(head(query_key_ref, 1, g))
        q = q * QUERY_SCALE
        qs.append(q)
        ks.append(k)
        q_inv.append(qi)
        k_inv.append(ki)
        grams.append((dot(k, k, NT), dot(q, k, NT)))
    for h in range(heads):
        before = start_ref[0, h]
        state = dot(before[:, :DK], state_in_ref[h]) + before[:, DK:].astype(F32)
        state_of.append(state.astype(BF16))
    for h in range(heads):
        k = ks[h // repeat]
        v = value_ref[:, h * DV : (h + 1) * DV]
        seen = dot(k, state_of[h])
        right_of.append(beta[:, h : h + 1] * (v - start[:, h : h + 1] * seen))
    for h in range(heads):
        value_of.append(dot(solve_ref[0, h], right_of[h]).astype(BF16))
    decay_of, delta_value_of, delta_right_of = [], [], []
    for h in range(heads):
        decay = pair_decay(cum_col, cum_row, same, h)
        decay_of.append(decay)
        k = ks[h // repeat]
        delta_out = delta_out_ref[:, h * DV : (h + 1) * DV]
        carry = carry_ref[h].astype(BF16)
        delta_value_of.append(
            dot(decay * grams[h // repeat][1], delta_out, TN)
            + dot(end[:, h : h + 1] * k, carry)
        )
    for h in range(heads):
        delta_right_of.append(dot(solve_ref[0, h], delta_value_of[h], TN))
    sums = jnp.zeros((CHUNK, heads), F32)
    logits = jnp.zeros((CHUNK, heads), F32)
    tail = jnp.zeros((1, heads), F32)
    lower_rows = []
    for g in range(key_heads):
        q, k = qs[g], ks[g]
        key_gram, query_gram = grams[g]
        delta_q = jnp.zeros((CHUNK, DK), F32)
        delta_k = jnp.zeros((CHUNK, DK), F32)
        for h in range(g * repeat, (g + 1) * repeat):
            cols = slice(h * DV, (h + 1) * DV)
            b, s, e = beta[:, h : h + 1], start[:, h : h + 1], end[:, h : h + 1]
            delta_out = delta_out_ref[:, cols]
            delta_right = delta_right_of[h]
            delta_value_ref[:, cols] = (b * delta_right).astype(BF16)
            pseudo = value_of[h]
            both = jnp.concatenate([delta_out, delta_right.astype(BF16)], axis=0)
            carry = carry_ref[h]
            pairs = dot(both, pseudo, NT)
            states = dot(both, state_of[h], NT)
            decay = decay_of[h]
            pair_q = decay * pairs[:CHUNK]
            pair_k = jnp.where(strict, (-b) * decay * pairs[CHUNK:], 0.0)
            cross = pair_q * query_gram + pair_k * key_gram
            state_q = s * states[:CHUNK]
            state_k = (b * s) * states[CHUNK:]
            end_k = e * dot(pseudo, carry, NT)
            delta_q += dot(pair_q, k) + state_q
            delta_k += (
                dot(pair_k, k)
                + dot(
                    jnp.concatenate([pair_q, pair_k], axis=0),
                    jnp.concatenate([q, k], axis=0),
                    TN,
                )
                + end_k
                - state_k
            )
            ends = row_sum(end_k * k)
            column = row_sum(cross + state_q * q - state_k * k) - ends
            sums = jnp.where(lane == h, column, sums)
            lower_rows.append(jnp.sum(cross, axis=0, keepdims=True))
            held = total[:, h : h + 1] * jnp.sum(
                state_of[h].astype(F32) * carry, axis=(0, 1), keepdims=True
            )
            tail = jnp.where(lane_one == h, held + jnp.sum(ends, axis=0, keepdims=True), tail)
            logits = jnp.where(lane == h, row_sum(delta_right * pseudo.astype(F32)), logits)
            carry_ref[h] = total[:, h : h + 1] * carry + dot(
                jnp.concatenate([s * q, (-b * s) * k], axis=0), both, TN
            )
        delta_q = delta_q * QUERY_SCALE
        unit = q * (1.0 / QUERY_SCALE)
        delta_q = q_inv[g] * (delta_q - unit * row_sum(unit * delta_q))
        delta_k = k_inv[g] * (delta_k - k * row_sum(k * delta_k))
        delta_query_key_ref[:, g * DK : (g + 1) * DK] = delta_q.astype(BF16)
        delta_query_key_ref[:, (key_heads + g) * DK : (key_heads + g + 1) * DK] = (
            delta_k.astype(BF16)
        )
    upper = (row <= col).astype(F32)
    reset_col = dot((row == col).astype(F32), resets, NT)[:, 0:1]
    pad = -heads % 8
    if pad:
        lower_rows.append(jnp.zeros((pad, CHUNK), F32))
    below = jnp.concatenate(lower_rows, axis=0)
    delta_log = exact(upper, sums) - exact(upper, below, NT)[:, :heads] + tail
    delta_log = jnp.where(reset_col == 0.0, delta_log, 0.0)
    delta_decay = delta_log * (-scale_ref[...]) * sigmoid(decay_beta_ref[:, :heads])
    delta_beta = logits * (1.0 - beta)
    rest = jnp.zeros((CHUNK, LANES - 2 * heads), F32)
    delta_query_key_ref[:, 2 * key_heads * DK :] = jnp.concatenate(
        [delta_decay, delta_beta, rest], axis=1
    ).astype(BF16)


def chain_forward_kernel(totals_ref, states_ref):
    devices, heads = totals_ref.shape[0], totals_ref.shape[1]
    for h in range(heads):
        state = jnp.zeros(states_ref.shape[2:], F32)
        for i in range(devices):
            states_ref[i, h] = state.astype(BF16)
            if i < devices - 1:
                step = totals_ref[i, h]
                high = state.astype(BF16)
                low = state - high.astype(F32)
                state = (
                    dot(step[:, :DK], high) + dot(step[:, :DK], low) + step[:, DK:].astype(F32)
                )


def chain_backward_kernel(totals_ref, deltas_ref, states_ref):
    devices, heads = totals_ref.shape[0], totals_ref.shape[1]
    for h in range(heads):
        state = jnp.zeros(states_ref.shape[2:], F32)
        for i in reversed(range(devices)):
            states_ref[i, h] = state.astype(BF16)
            if i > 0:
                step = totals_ref[i, h]
                high = state.astype(BF16)
                low = state - high.astype(F32)
                state = (
                    dot(step[:, :DK], high, TN)
                    + dot(step[:, :DK], low, TN)
                    + deltas_ref[i, h].astype(F32)
                )


PARAMS = pltpu.CompilerParams(
    dimension_semantics=("arbitrary",), vmem_limit_bytes=56 * 1024 * 1024
)
INTERPRET = False


def whole(shape):
    return pl.BlockSpec(shape, lambda c: (0,) * len(shape))


def run_forward(query_key, value, decay_beta, bias, scale, resets):
    tokens, heads = query_key.shape[1], bias.shape[1]
    chunks = tokens // CHUNK
    key_width, value_width = query_key.shape[2], heads * DV
    return pl.pallas_call(
        forward_kernel,
        grid=(chunks,),
        in_specs=[
            pl.BlockSpec((2, CHUNK, key_width), lambda c: (0, c, 0)),
            pl.BlockSpec((CHUNK, value_width), lambda c: (c, 0)),
            pl.BlockSpec((CHUNK, 2 * heads), lambda c: (c, 0)),
            whole((1, heads)),
            whole((1, heads)),
            pl.BlockSpec((1, 1, CHUNK), lambda c: (c, 0, 0)),
        ],
        out_specs=[
            pl.BlockSpec((1, heads, CHUNK, CHUNK), lambda c: (c, 0, 0, 0)),
            pl.BlockSpec((1, heads, DK, DK + DV), lambda c: (c, 0, 0, 0)),
            pl.BlockSpec((CHUNK, value_width), lambda c: (c, 0)),
            pl.BlockSpec((CHUNK, value_width), lambda c: (c, 0)),
            whole((heads, DK, DK + DV)),
        ],
        out_shape=[
            jax.ShapeDtypeStruct((chunks, heads, CHUNK, CHUNK), BF16),
            jax.ShapeDtypeStruct((chunks, heads, DK, DK + DV), BF16),
            jax.ShapeDtypeStruct((tokens, value_width), BF16),
            jax.ShapeDtypeStruct((tokens, value_width), F32),
            jax.ShapeDtypeStruct((heads, DK, DK + DV), BF16),
        ],
        scratch_shapes=[pltpu.VMEM((heads, DK, DK + DV), F32)],
        compiler_params=PARAMS,
        interpret=INTERPRET,
        name="forward_blocks",
    )(query_key, value, decay_beta, bias, scale, resets)


def run_output(local, reach, gate, delta_hidden, state_in, gain):
    tokens, value_width = local.shape
    heads = value_width // DV
    chunks = tokens // CHUNK
    block = pl.BlockSpec((CHUNK, value_width), lambda c: (c, 0))
    return pl.pallas_call(
        output_kernel,
        grid=(chunks,),
        in_specs=[
            block,
            block,
            block,
            block,
            whole((heads, DK, DV)),
            whole((1, DV)),
        ],
        out_specs=[block, block, block, whole((heads, DK, DV))],
        out_shape=[
            jax.ShapeDtypeStruct((tokens, value_width), BF16),
            jax.ShapeDtypeStruct((tokens, value_width), BF16),
            jax.ShapeDtypeStruct((tokens, value_width), BF16),
            jax.ShapeDtypeStruct((heads, DK, DV), BF16),
        ],
        scratch_shapes=[pltpu.VMEM((heads, DK, DV), F32)],
        compiler_params=PARAMS,
        interpret=INTERPRET,
        name="gated_norm",
    )(local, reach, gate, delta_hidden, state_in, gain)


def run_backward(
    query_key, value, decay_beta, bias, scale, resets, solve, starts, state_in, delta_out, final
):
    tokens, heads = query_key.shape[1], bias.shape[1]
    chunks = tokens // CHUNK
    key_width, value_width = query_key.shape[2], heads * DV
    last = chunks - 1
    return pl.pallas_call(
        backward_kernel,
        grid=(chunks,),
        in_specs=[
            pl.BlockSpec((2, CHUNK, key_width), lambda c: (0, last - c, 0)),
            pl.BlockSpec((CHUNK, value_width), lambda c: (last - c, 0)),
            pl.BlockSpec((CHUNK, 2 * heads), lambda c: (last - c, 0)),
            whole((1, heads)),
            whole((1, heads)),
            pl.BlockSpec((1, 1, CHUNK), lambda c: (last - c, 0, 0)),
            pl.BlockSpec((1, heads, CHUNK, CHUNK), lambda c: (last - c, 0, 0, 0)),
            pl.BlockSpec((1, heads, DK, DK + DV), lambda c: (last - c, 0, 0, 0)),
            whole((heads, DK, DV)),
            pl.BlockSpec((CHUNK, value_width), lambda c: (last - c, 0)),
            whole((heads, DK, DV)),
        ],
        out_specs=[
            pl.BlockSpec((CHUNK, 2 * key_width + LANES), lambda c: (last - c, 0)),
            pl.BlockSpec((CHUNK, value_width), lambda c: (last - c, 0)),
        ],
        out_shape=[
            jax.ShapeDtypeStruct((tokens, 2 * key_width + LANES), BF16),
            jax.ShapeDtypeStruct((tokens, value_width), BF16),
        ],
        scratch_shapes=[pltpu.VMEM((heads, DK, DV), F32)],
        compiler_params=PARAMS,
        interpret=INTERPRET,
        name="backward_blocks",
    )(query_key, value, decay_beta, bias, scale, resets, solve, starts, state_in, delta_out, final)


def spread(array, devices):
    heads, depth, width = array.shape
    if heads >= devices:
        return array.reshape(devices, heads // devices, depth, width)
    cuts = devices // heads
    parts = array.reshape(heads, depth, cuts, width // cuts)
    return jnp.transpose(parts, (0, 2, 1, 3)).reshape(devices, 1, depth, width // cuts)


def gather_parts(parts, heads):
    devices, each, depth, width = parts.shape
    if heads >= devices:
        return parts.reshape(heads, depth, width)
    cuts = devices // heads
    parts = parts.reshape(heads, cuts, depth, width)
    return jnp.transpose(parts, (0, 2, 1, 3)).reshape(heads, depth, cuts * width)


def swap(parts):
    return lax.all_to_all(parts, "ctx", split_axis=0, concat_axis=0, tiled=True)


def spread_totals(totals):
    devices, heads = lax.axis_size("ctx"), totals.shape[0]
    if heads >= devices:
        return spread(totals, devices)
    maps = jnp.repeat(totals[:, :, :DK], devices // heads, axis=0)[:, None]
    return jnp.concatenate([maps, spread(totals[:, :, DK:], devices)], axis=-1)


def run_chain_forward(held):
    return pl.pallas_call(
        chain_forward_kernel,
        out_shape=jax.ShapeDtypeStruct((*held.shape[:3], held.shape[3] - DK), BF16),
        interpret=INTERPRET,
        name="chain_forward",
    )(held)


def run_chain_backward(held, deltas):
    return pl.pallas_call(
        chain_backward_kernel,
        out_shape=jax.ShapeDtypeStruct(deltas.shape, BF16),
        interpret=INTERPRET,
        name="chain_backward",
    )(held, deltas)


def product(spec, a, b):
    return jnp.einsum(spec, a, b, preferred_element_type=F32)


def rows_of(small_weight_ref):
    return jnp.concatenate([small_weight_ref[0].astype(F32), small_weight_ref[1].astype(F32)], axis=0)


def projection_kernel(
    inputs_ref,
    query_key_weight_ref,
    value_weight_ref,
    decay_beta_weight_ref,
    query_key_ref,
    value_ref,
    decay_beta_ref,
):
    inputs = inputs_ref[...]
    query_key_ref[0] = dot(inputs, query_key_weight_ref[0])
    value_ref[...] = dot(inputs, value_weight_ref[0])

    @pl.when(pl.program_id(0) == 0)
    def _():
        decay_beta_ref[...] = dot(inputs, rows_of(decay_beta_weight_ref), NT)


def run_projection(inputs, query_key_weight, value_gate_weight, decay_beta_weight):
    tokens, model = inputs.shape
    key_width, value_width = query_key_weight.shape[2], value_gate_weight.shape[2]
    heads = decay_beta_weight.shape[1]
    steps = 4
    keys, values = 2 * key_width // steps, value_width // steps
    return pl.pallas_call(
        projection_kernel,
        grid=(steps,),
        in_specs=[
            whole((tokens, model)),
            pl.BlockSpec((1, model, keys), lambda j: (j // 2, 0, j % 2)),
            pl.BlockSpec((1, model, values), lambda j: (0, 0, j)),
            whole((2, heads, model)),
        ],
        out_specs=[
            pl.BlockSpec((1, tokens, keys), lambda j: (j // 2, 0, j % 2)),
            pl.BlockSpec((tokens, values), lambda j: (0, j)),
            whole((tokens, 2 * heads)),
        ],
        out_shape=[
            jax.ShapeDtypeStruct((2, tokens, key_width), F32),
            jax.ShapeDtypeStruct((tokens, value_width), F32),
            jax.ShapeDtypeStruct((tokens, 2 * heads), F32),
        ],
        compiler_params=PARAMS,
        interpret=INTERPRET,
        name="projection",
    )(inputs, query_key_weight, value_gate_weight, decay_beta_weight)


def input_gradient_kernel(
    delta_query_key_ref,
    delta_value_ref,
    delta_gate_ref,
    query_key_weight_ref,
    value_gate_weight_ref,
    decay_beta_weight_ref,
    out_ref,
):
    width = query_key_weight_ref.shape[2]
    heads = decay_beta_weight_ref.shape[1]
    keys = jnp.concatenate([query_key_weight_ref[0], query_key_weight_ref[1]], axis=1)
    small = delta_query_key_ref[:, 2 * width : 2 * width + 2 * heads]
    total = dot(delta_gate_ref[...], value_gate_weight_ref[1], NT)
    total += dot(delta_value_ref[...], value_gate_weight_ref[0], NT)
    total += dot(delta_query_key_ref[:, : 2 * width], keys, NT)
    total += dot(small, rows_of(decay_beta_weight_ref))
    out_ref[...] = total.astype(BF16)


def run_input_gradient(
    delta_query_key, delta_value, delta_gate, query_key_weight, value_gate_weight, decay_beta_weight
):
    tokens, model = delta_value.shape[0], query_key_weight.shape[1]
    cut = 512

    def weight(array):
        return pl.BlockSpec((2, cut, array.shape[2]), lambda j: (0, j, 0))

    return pl.pallas_call(
        input_gradient_kernel,
        grid=(model // cut,),
        in_specs=[
            whole(delta_query_key.shape),
            whole(delta_value.shape),
            whole(delta_gate.shape),
            weight(query_key_weight),
            weight(value_gate_weight),
            pl.BlockSpec((2, decay_beta_weight.shape[1], cut), lambda j: (0, 0, j)),
        ],
        out_specs=pl.BlockSpec((tokens, cut), lambda j: (0, j)),
        out_shape=jax.ShapeDtypeStruct((tokens, model), BF16),
        compiler_params=PARAMS,
        interpret=INTERPRET,
        name="input_gradient",
    )(delta_query_key, delta_value, delta_gate, query_key_weight, value_gate_weight, decay_beta_weight)


def together(*arrays):
    return lax.optimization_barrier(arrays)


def exchange(array, distance):
    devices = range(lax.axis_size("ctx"))
    return lax.ppermute(array, "ctx", [(i, i ^ distance) for i in devices])


def block_of(step, place, flip):
    x, y = (place // 2) % 2, place // 4
    core = lax.rem(place + flip, 2)
    across_x, across_y = 1 - step // 2, 1 - lax.rem(step, 2)
    target_x, target_y = lax.rem(x + across_x, 2), lax.rem(y + across_y, 2)
    return target_y * 4 + target_x * 2 + core


def send_kernel(place_ref, left_a_ref, a_ref, left_b_ref, b_ref, a_out_ref, b_out_ref):
    a_out_ref[...] = dot(left_a_ref[...], a_ref[...], TN).astype(BF16)
    b_out_ref[...] = dot(left_b_ref[...], b_ref[...], TN).astype(BF16)


def keep_kernel(
    place_ref, left_a_ref, a_ref, left_b_ref, b_ref, a_arrived_ref, b_arrived_ref, *out_refs
):
    step = pl.program_id(0)
    a = dot(left_a_ref[...], a_ref[...], TN) + a_arrived_ref[...].astype(F32)
    b = dot(left_b_ref[...], b_ref[...], TN) + b_arrived_ref[...].astype(F32)
    for i in range(4):

        @pl.when(step == i)
        def _():
            out_refs[i][...] = a.astype(BF16)
            out_refs[4 + i][...] = b.astype(BF16)


def pair_specs(left_a, a, left_b, b, flip):
    def rows(left):
        return pl.BlockSpec(
            (left.shape[0], left.shape[1] // 8), lambda i, place: (0, block_of(i, place[0], flip))
        )

    def full(delta):
        return pl.BlockSpec(delta.shape, lambda i, place: (0, 0))

    return [rows(left_a), full(a), rows(left_b), full(b)]


def halving_start(place, left_a, a, left_b, b):
    rows = left_a.shape[1] // 8
    return pl.pallas_call(
        send_kernel,
        grid_spec=pltpu.PrefetchScalarGridSpec(
            num_scalar_prefetch=1,
            grid=(4,),
            in_specs=pair_specs(left_a, a, left_b, b, 1),
            out_specs=[
                pl.BlockSpec((rows, delta.shape[1]), lambda i, place: (i, 0)) for delta in (a, b)
            ],
        ),
        out_shape=[
            jax.ShapeDtypeStruct((4 * rows, delta.shape[1]), BF16) for delta in (a, b)
        ],
        compiler_params=PARAMS,
        interpret=INTERPRET,
        name="send_rows",
    )(place, left_a, a, left_b, b)


def halving_keep(place, left_a, a, left_b, b, a_arrived, b_arrived):
    rows = left_a.shape[1] // 8
    return pl.pallas_call(
        keep_kernel,
        grid_spec=pltpu.PrefetchScalarGridSpec(
            num_scalar_prefetch=1,
            grid=(4,),
            in_specs=pair_specs(left_a, a, left_b, b, 0)
            + [pl.BlockSpec((rows, delta.shape[1]), lambda i, place: (i, 0)) for delta in (a, b)],
            out_specs=[
                pl.BlockSpec((rows, delta.shape[1]), lambda i, place: (0, 0))
                for delta in (a, b)
                for _ in range(4)
            ],
        ),
        out_shape=[
            jax.ShapeDtypeStruct((rows, delta.shape[1]), BF16)
            for delta in (a, b)
            for _ in range(4)
        ],
        compiler_params=PARAMS,
        interpret=INTERPRET,
        name="keep_rows",
    )(place, left_a, a, left_b, b, a_arrived, b_arrived)


def summed(a, b):
    return (a.astype(F32) + b.astype(F32)).astype(BF16)


def halving_cross(pieces):
    a, b = pieces[:4], pieces[4:]
    return exchange(a[0], 2), exchange(b[0], 4), exchange(a[1], 2), exchange(b[2], 4)


def halving_last(pieces, arrived):
    a, b = pieces[:4], pieces[4:]
    return exchange(summed(a[2], arrived[0]), 4), exchange(summed(b[1], arrived[1]), 2)


def halving_sum(pieces, arrived, last):
    def total(own, near, far):
        return own.astype(F32) + near.astype(F32) + far.astype(F32)

    return total(pieces[3], arrived[2], last[0]), total(pieces[7], arrived[3], last[1])


def scatter(partial, axis, dimension):
    return lax.psum_scatter(partial.astype(BF16), axis, scatter_dimension=dimension, tiled=True)


def body(
    inputs,
    query_key_weight,
    value_gate_weight,
    decay_beta_weight,
    beta_bias,
    decay_scale,
    norm_gain,
    out_weight,
    boundaries,
    grad_mixed,
):
    tokens, heads = inputs.shape[0], beta_bias.shape[0]
    key_width = query_key_weight.shape[2]
    cubic = lax.axis_size("ctx") == 8
    small_weight = jnp.swapaxes(decay_beta_weight, 1, 2)
    query_key, value, decay_beta = run_projection(
        inputs, query_key_weight, value_gate_weight, small_weight
    )
    bias, scale = beta_bias.reshape(1, heads), decay_scale.reshape(1, heads)
    resets = boundaries.reshape(tokens // CHUNK, 1, CHUNK)
    solve, starts, reach, local, totals = run_forward(
        query_key, value, decay_beta, bias, scale, resets
    )

    held = swap(spread_totals(totals))
    gate = product("td,df->tf", inputs, value_gate_weight[1])
    held, gate = together(held, gate)
    states = swap(run_chain_forward(held))
    delta_hidden = product("td,fd->tf", grad_mixed, out_weight)
    states, delta_hidden = together(states, delta_hidden)
    state_in = gather_parts(states, heads)
    hidden, delta_gate, delta_out, delta_state = run_output(
        local, reach, gate, delta_hidden, state_in, norm_gain.reshape(1, DV)
    )

    deltas = swap(spread(delta_state, lax.axis_size("ctx")))
    partial_out = product("tf,fd->td", hidden, out_weight).astype(BF16)
    deltas, partial_out = together(deltas, partial_out)
    mixed = scatter(partial_out, "head", 1)
    finals = swap(run_chain_backward(held, deltas))
    if cubic:
        place = lax.axis_index("ctx").astype(jnp.int32).reshape(1)
        early = (place, inputs, delta_gate, grad_mixed, hidden)
        sent = halving_start(*early)
        arrived = [exchange(part, 1) for part in sent]
        early_pieces = halving_keep(*early, *arrived)
        finals, early_pieces = together(finals, early_pieces)
        early_arrived = halving_cross(early_pieces)
    delta_final = gather_parts(finals, heads)
    delta_query_key, delta_value = run_backward(
        query_key,
        value,
        decay_beta,
        bias,
        scale,
        resets,
        solve,
        starts,
        state_in,
        delta_out,
        delta_final,
    )
    if cubic:
        late = (place, inputs, delta_value, inputs, delta_query_key)
        sent = halving_start(*late)
        arrived = [exchange(part, 1) for part in sent]
    grad_rows = run_input_gradient(
        delta_query_key,
        delta_value,
        delta_gate,
        query_key_weight,
        value_gate_weight,
        small_weight,
    )
    if cubic:
        grad_rows, arrived = together(grad_rows, arrived)
    grad_inputs = scatter(grad_rows, "head", 1)
    if cubic:
        late_pieces = halving_keep(*late, *arrived)
        late_pieces, early_arrived = together(late_pieces, early_arrived)
        late_arrived = halving_cross(late_pieces)
        early_last = halving_last(early_pieces, early_arrived)
        late_last = halving_last(late_pieces, late_arrived)
        grad_gate, grad_out = halving_sum(early_pieces, early_arrived, early_last)
        grad_out = grad_out.T
        grad_value, packed = halving_sum(late_pieces, late_arrived, late_last)
    else:
        grad_gate = scatter(product("td,tf->df", inputs, delta_gate), "ctx", 0).astype(F32)
        grad_out = scatter(product("tf,td->fd", hidden, grad_mixed), "ctx", 1).astype(F32)
        grad_value = scatter(product("td,tf->df", inputs, delta_value), "ctx", 0).astype(F32)
        packed = scatter(product("td,tf->df", inputs, delta_query_key), "ctx", 0).astype(F32)
    rest = packed[:, 2 * key_width :]
    return (
        mixed,
        grad_inputs,
        jnp.stack([packed[:, :key_width], packed[:, key_width : 2 * key_width]]),
        jnp.stack([grad_value, grad_gate]),
        jnp.stack([rest[:, :heads], rest[:, heads : 2 * heads]]),
        grad_out,
    )


def solution(mesh):
    in_specs = (
        P("ctx", None),
        P(None, None, "head"),
        P(None, None, "head"),
        P(None, None, "head"),
        P("head"),
        P("head"),
        P(),
        P("head", None),
        P("ctx"),
        P("ctx", None),
    )
    out_specs = (
        P("ctx", "head"),
        P("ctx", "head"),
        P(None, "ctx", "head"),
        P(None, "ctx", "head"),
        P(None, "ctx", "head"),
        P("head", "ctx"),
    )
    return jax.shard_map(body, mesh=mesh, in_specs=in_specs, out_specs=out_specs, check_vma=False)
```

```python
import functools

import jax
import jax.numpy as jnp
from jax import lax
from jax.experimental import pallas as pl
from jax.experimental.pallas import tpu as pltpu
from jax.sharding import PartitionSpec as P

DK = 128
DV = 128
CHUNK = 128
EPS = 1e-06
QUERY_SCALE = DK ** (-0.5)
LANES = 128
FORWARD_SPANS = 2
BACKWARD_SPANS = 2

F32 = jnp.float32
BF16 = jnp.bfloat16
NN = ((1,), (0,))
NT = ((1,), (1,))
TN = ((0,), (0,))


def dot(a, b, dims=NN):
    return lax.dot_general(
        a.astype(BF16), b.astype(BF16), (dims, ((), ())), preferred_element_type=F32
    )


def exact(a, b, dims=NN):
    return lax.dot_general(
        a, b, (dims, ((), ())), precision=lax.Precision.HIGHEST, preferred_element_type=F32
    )


def softplus(x):
    return jnp.maximum(x, 0.0) + jnp.log1p(jnp.exp(-jnp.abs(x)))


def sigmoid(x):
    return 1.0 / (1.0 + jnp.exp(-x))


def row_sum(x):
    return jnp.sum(x, axis=-1, keepdims=True)


def grid_of(size):
    row = lax.broadcasted_iota(jnp.int32, (size, size), 0)
    col = lax.broadcasted_iota(jnp.int32, (size, size), 1)
    return row, col


def decays(decay_beta, bias_ref, scale_ref, resets):
    row, col = grid_of(CHUNK)
    lower = (row >= col).astype(F32)
    heads = bias_ref.shape[1]
    decay_logit = decay_beta[:, :heads]
    beta = sigmoid(decay_beta[:, heads:] + bias_ref[...])
    log_decay = -scale_ref[...] * softplus(decay_logit)
    resets = jnp.broadcast_to(resets.astype(F32), (8, CHUNK))
    doc_row = dot(resets, lower, NT)[0:1]
    doc_col = dot(lower, resets, NT)[:, 0:1]
    cum_col = exact(lower, log_decay)
    cum_row = exact(log_decay, lower, ((0,), (1,)))
    same = (doc_col == doc_row) & (row >= col)
    start = jnp.where(doc_col == 0.0, jnp.exp(cum_col), 0.0)
    last = CHUNK - 1
    end = jnp.where(
        doc_col == doc_col[last:],
        jnp.exp(jnp.minimum(cum_col[last:] - cum_col, 0.0)),
        0.0,
    )
    return beta, cum_col, cum_row, same, start, end, start[last:], resets


def pair_decay(cum_col, cum_row, same, h):
    gap = jnp.minimum(spread_column(cum_col, h) - cum_row[h : h + 1, :], 0.0)
    return jnp.where(same, jnp.exp(gap), 0.0)


def spread_column(columns, h):
    return jnp.broadcast_to(columns[:, h : h + 1], (columns.shape[0], LANES))


def unit_rows(x):
    inverse = lax.rsqrt(row_sum(x * x) + EPS)
    return x * inverse, inverse


def forward_kernel(
    query_key_ref,
    value_ref,
    decay_beta_ref,
    bias_ref,
    scale_ref,
    resets_ref,
    solve_ref,
    start_ref,
    map_ref,
    local_ref,
    total_ref,
    state_ref,
):
    heads = state_ref.shape[0]
    key_heads = query_key_ref.shape[2] // DK
    repeat = heads // key_heads
    spans = solve_ref.shape[0]
    row, col = grid_of(CHUNK)

    @pl.when(pl.program_id(0) == 0)
    def _():
        first = jnp.concatenate([(row == col).astype(F32), jnp.zeros((DK, DV), F32)], axis=1)
        for h in range(heads):
            state_ref[h] = first

    strict = row > col
    differ = row ^ col
    rows = [slice(c * CHUNK, (c + 1) * CHUNK) for c in range(spans)]
    each = [(c, h) for c in range(spans) for h in range(heads)]
    terms = [
        decays(decay_beta_ref[rows[c]], bias_ref, scale_ref, resets_ref[c]) for c in range(spans)
    ]
    keys, queries = {}, {}
    for c in range(spans):
        for g in range(key_heads):
            cols = slice(g * DK, (g + 1) * DK)
            queries[c, g] = unit_rows(query_key_ref[0, rows[c], cols])[0] * QUERY_SCALE
            keys[c, g] = unit_rows(query_key_ref[1, rows[c], cols])[0]
    grams = {p: (dot(keys[p], keys[p], NT), dot(queries[p], keys[p], NT)) for p in keys}
    scores, systems, betas, starts = {}, {}, {}, {}
    for c, h in each:
        beta, cum_col, cum_row, same, start = terms[c][:5]
        betas[c, h] = spread_column(beta, h)
        starts[c, h] = spread_column(start, h)
        decay = pair_decay(cum_col, cum_row, same, h)
        key_gram, query_gram = grams[c, h // repeat]
        scores[c, h] = (decay * query_gram).astype(BF16)
        systems[c, h] = jnp.where(strict, betas[c, h] * decay * key_gram, 0.0)
    identity = (row == col).astype(F32)
    inverse = {
        p: (identity - jnp.where(differ == 1, systems[p], 0.0)).astype(BF16) for p in each
    }
    level = 1
    while (1 << level) < CHUNK:
        here = (differ >> level) == 1
        inner = {
            p: dot(jnp.where(here, systems[p], 0.0), inverse[p]).astype(BF16) for p in each
        }
        inverse = {p: inverse[p] - dot(inverse[p], inner[p]).astype(BF16) for p in each}
        level += 1
    weights = {}
    for c, h in each:
        k = keys[c, h // repeat]
        v = value_ref[rows[c], h * DV : (h + 1) * DV]
        b = betas[c, h]
        right = jnp.concatenate([(b * starts[c, h]) * k, b * v], axis=1)
        weights[c, h] = dot(inverse[c, h], right)
        solve_ref[c, h] = inverse[c, h]
    for c in range(spans):
        end, total = terms[c][5:7]
        values = []
        for h in range(heads):
            state = state_ref[h].astype(BF16)
            start_ref[c, h] = state
            solved = weights[c, h]
            base = jnp.concatenate([jnp.zeros((CHUNK, DK), F32), solved[:, DK:]], axis=1)
            values.append((base - dot(solved[:, :DK], state)).astype(BF16))
        for h in range(heads):
            k, q = keys[c, h // repeat], queries[c, h // repeat]
            state = state_ref[h]
            out = dot(starts[c, h] * q, state) + dot(scores[c, h], values[h])
            map_ref[rows[c], h * DK : (h + 1) * DK] = out[:, :DK].astype(BF16)
            local_ref[rows[c], h * DV : (h + 1) * DV] = out[:, DK:]
            state = total[:, h : h + 1] * state + dot(spread_column(end, h) * k, values[h], TN)
            state_ref[h] = state
            total_ref[h] = state.astype(BF16)


def output_kernel(
    local_ref,
    map_ref,
    gate_ref,
    delta_ref,
    state_ref,
    gain_ref,
    hidden_ref,
    delta_gate_ref,
    delta_out_ref,
    delta_state_ref,
    total_ref,
):
    heads = state_ref.shape[0]
    gain = gain_ref[...]

    @pl.when(pl.program_id(0) == 0)
    def _():
        total_ref[...] = jnp.zeros_like(total_ref)

    outs, deltas = [], []
    for h in range(heads):
        cols = slice(h * DV, (h + 1) * DV)
        outs.append(local_ref[:, cols] + dot(map_ref[:, cols], state_ref[h]))
    for h in range(heads):
        cols = slice(h * DV, (h + 1) * DV)
        out = outs[h]
        gate = gate_ref[:, cols]
        delta = delta_ref[:, cols]
        scale = lax.rsqrt(row_sum(out * out) * (1.0 / DV) + EPS)
        normed = out * scale
        share = sigmoid(gate)
        silu = gate * share
        scaled = normed * gain
        hidden_ref[:, cols] = (scaled * silu).astype(BF16)
        delta_gate_ref[:, cols] = (
            delta * scaled * (share * (1.0 + gate * (1.0 - share)))
        ).astype(BF16)
        delta_normed = delta * gain * silu
        delta_out = scale * (
            delta_normed - normed * (row_sum(normed * delta_normed) * (1.0 / DV))
        )
        delta_out = delta_out.astype(BF16)
        delta_out_ref[:, cols] = delta_out
        deltas.append(delta_out)
    for h in range(heads):
        cols = slice(h * DV, (h + 1) * DV)
        part = total_ref[h] + dot(map_ref[:, cols], deltas[h], TN)
        total_ref[h] = part
        delta_state_ref[h] = part.astype(BF16)


def backward_kernel(
    query_key_ref,
    value_ref,
    decay_beta_ref,
    bias_ref,
    scale_ref,
    resets_ref,
    solve_ref,
    start_ref,
    state_in_ref,
    delta_out_ref,
    delta_final_ref,
    delta_query_key_ref,
    delta_value_ref,
    carry_ref,
):
    heads = carry_ref.shape[0]
    key_heads = query_key_ref.shape[2] // DK
    repeat = heads // key_heads
    spans = solve_ref.shape[0]
    row, col = grid_of(CHUNK)

    @pl.when(pl.program_id(0) == 0)
    def _():
        carry_ref[...] = delta_final_ref[...].astype(F32)

    strict = row > col
    upper = (row <= col).astype(F32)
    identity = (row == col).astype(F32)
    rows = [slice(c * CHUNK, (c + 1) * CHUNK) for c in range(spans)]
    cols = [slice(h * DV, (h + 1) * DV) for h in range(heads)]
    each = [(c, h) for c in reversed(range(spans)) for h in range(heads)]
    terms = [
        decays(decay_beta_ref[rows[c]], bias_ref, scale_ref, resets_ref[c]) for c in range(spans)
    ]
    half = lax.broadcasted_iota(jnp.int32, (2 * DK, 2 * heads), 0) // DK
    lane = lax.broadcasted_iota(jnp.int32, (2 * DK, 2 * heads), 1)
    lane_one = lax.broadcasted_iota(jnp.int32, (1, heads), 1)
    qs, ks, q_inv, k_inv = {}, {}, {}, {}
    for c in range(spans):
        for g in range(key_heads):
            at = slice(g * DK, (g + 1) * DK)
            q, q_inv[c, g] = unit_rows(query_key_ref[0, rows[c], at])
            qs[c, g] = q * QUERY_SCALE
            ks[c, g], k_inv[c, g] = unit_rows(query_key_ref[1, rows[c], at])
    grams = {p: (dot(ks[p], ks[p], NT), dot(qs[p], ks[p], NT)) for p in ks}
    state_of, value_of, right_of = {}, {}, {}
    betas, starts, ends = {}, {}, {}
    for c, h in each:
        before = start_ref[c, h]
        state = dot(before[:, :DK], state_in_ref[h]) + before[:, DK:].astype(F32)
        state_of[c, h] = state.astype(BF16)
    for c, h in each:
        beta, start, end = terms[c][0], terms[c][4], terms[c][5]
        seen = dot(ks[c, h // repeat], state_of[c, h])
        betas[c, h] = spread_column(beta, h)
        starts[c, h] = spread_column(start, h)
        ends[c, h] = spread_column(end, h)
        right_of[c, h] = betas[c, h] * (value_ref[rows[c], cols[h]] - starts[c, h] * seen)
    for c, h in each:
        value_of[c, h] = dot(solve_ref[c, h], right_of[c, h]).astype(BF16)
    decay_of, delta_value_of, delta_right_of = {}, {}, {}
    for c, h in each:
        decay_of[c, h] = pair_decay(terms[c][1], terms[c][2], terms[c][3], h)
        delta_value_of[c, h] = dot(
            decay_of[c, h] * grams[c, h // repeat][1], delta_out_ref[rows[c], cols[h]], TN
        )
    both_of, held_of, carry_of = {}, {}, {}
    for c in reversed(range(spans)):
        total = terms[c][6]
        for h in range(heads):
            carry_of[c, h] = carry_ref[h].astype(BF16)
            delta_value_of[c, h] += dot(ends[c, h] * ks[c, h // repeat], carry_of[c, h])
        for h in range(heads):
            delta_right_of[c, h] = dot(solve_ref[c, h], delta_value_of[c, h], TN)
        for h in range(heads):
            q, k = qs[c, h // repeat], ks[c, h // repeat]
            b, s = betas[c, h], starts[c, h]
            delta_right = delta_right_of[c, h]
            delta_value_ref[rows[c], cols[h]] = (b * delta_right).astype(BF16)
            both_of[c, h] = jnp.concatenate(
                [delta_out_ref[rows[c], cols[h]], delta_right.astype(BF16)], axis=0
            )
            carry = carry_ref[h]
            held_of[c, h] = total[:, h : h + 1] * row_sum(
                jnp.sum(state_of[c, h].astype(F32) * carry, axis=0, keepdims=True)
            )
            carry_ref[h] = total[:, h : h + 1] * carry + dot(
                jnp.concatenate([s * q, (-b * s) * k], axis=0), both_of[c, h], TN
            )
    pairs_of = {p: dot(both_of[p], value_of[p], NT) for p in each}
    states_of = {p: dot(both_of[p], state_of[p], NT) for p in each}
    ends_of = {p: ends[p] * dot(value_of[p], carry_of[p], NT) for p in each}
    pair_of, sum_of, tail_of, lower_of = {}, {}, {}, {}
    for c, h in each:
        q, k = qs[c, h // repeat], ks[c, h // repeat]
        key_gram, query_gram = grams[c, h // repeat]
        decay, b, s = decay_of[c, h], betas[c, h], starts[c, h]
        pair_q = decay * pairs_of[c, h][:CHUNK]
        pair_k = jnp.where(strict, (-b) * decay * pairs_of[c, h][CHUNK:], 0.0)
        cross = jnp.where(strict, pair_q * query_gram + pair_k * key_gram, 0.0).astype(BF16)
        pair_of[c, h] = (pair_q.astype(BF16), pair_k.astype(BF16))
        state_q = s * states_of[c, h][:CHUNK]
        state_k = (b * s) * states_of[c, h][CHUNK:]
        states_of[c, h] = (state_q, ends_of[c, h] - state_k)
        sum_of[c, h] = jnp.concatenate(
            [cross, (state_q * q - state_k * k).astype(BF16)], axis=1
        )
        tail_of[c, h] = jnp.concatenate(
            [ends_of[c, h] * k, delta_right_of[c, h] * value_of[c, h].astype(F32)], axis=1
        ).astype(BF16)
        lower_of[c, h] = jnp.sum(cross.astype(F32), axis=0, keepdims=True)
    for c in range(spans):
        for g in range(key_heads):
            q, k = qs[c, g], ks[c, g]
            both = jnp.concatenate([q, k], axis=0)
            delta_q = jnp.zeros((CHUNK, DK), F32)
            delta_k = jnp.zeros((CHUNK, DK), F32)
            for h in range(g * repeat, (g + 1) * repeat):
                pair_q, pair_k = pair_of[c, h]
                delta_q += dot(pair_q, k) + states_of[c, h][0]
                delta_k += (
                    dot(pair_k, k)
                    + dot(jnp.concatenate([pair_q, pair_k], axis=0), both, TN)
                    + states_of[c, h][1]
                )
            delta_q = delta_q * QUERY_SCALE
            unit = q * (1.0 / QUERY_SCALE)
            delta_q = q_inv[c, g] * (delta_q - unit * row_sum(unit * delta_q))
            delta_k = k_inv[c, g] * (delta_k - k * row_sum(k * delta_k))
            at, after = g * DK, (key_heads + g) * DK
            delta_query_key_ref[rows[c], at : at + DK] = delta_q.astype(BF16)
            delta_query_key_ref[rows[c], after : after + DK] = delta_k.astype(BF16)
    for c in range(spans):
        beta, resets = terms[c][0], terms[c][7]
        sums = jnp.zeros((CHUNK, 2 * heads), F32)
        tails = jnp.zeros((CHUNK, 2 * heads), F32)
        tail = jnp.zeros((1, heads), F32)
        for h in range(heads):
            sums += dot(sum_of[c, h], lane == h)
            tails += dot(tail_of[c, h], lane == h + heads * half)
            tail = jnp.where(lane_one == h, held_of[c, h], tail)
        below = [lower_of[c, h] for h in range(heads)]
        if heads % 8:
            below.append(jnp.zeros((-heads % 8, CHUNK), F32))
        below = exact(upper, jnp.concatenate(below, axis=0), NT)[:, :heads]
        ends_sum = tails[:, :heads]
        tail = tail + jnp.sum(ends_sum, axis=0, keepdims=True)
        delta_log = exact(upper, sums[:, :heads] - ends_sum) - below + tail
        reset_col = dot(identity, resets, NT)[:, 0:1]
        delta_log = jnp.where(reset_col == 0.0, delta_log, 0.0)
        logits = decay_beta_ref[rows[c], :heads]
        delta_decay = delta_log * (-scale_ref[...]) * sigmoid(logits)
        delta_beta = tails[:, heads:] * (1.0 - beta)
        rest = jnp.zeros((CHUNK, LANES - 2 * heads), F32)
        delta_query_key_ref[rows[c], 2 * key_heads * DK :] = jnp.concatenate(
            [delta_decay, delta_beta, rest], axis=1
        ).astype(BF16)


def chain_forward_kernel(totals_ref, states_ref):
    devices, heads = totals_ref.shape[0], totals_ref.shape[1]
    for h in range(heads):
        state = jnp.zeros(states_ref.shape[2:], F32)
        for i in range(devices):
            states_ref[i, h] = state.astype(BF16)
            if i < devices - 1:
                step = totals_ref[i, h]
                high = state.astype(BF16)
                low = state - high.astype(F32)
                state = (
                    dot(step[:, :DK], high) + dot(step[:, :DK], low) + step[:, DK:].astype(F32)
                )


def chain_backward_kernel(totals_ref, deltas_ref, states_ref):
    devices, heads = totals_ref.shape[0], totals_ref.shape[1]
    for h in range(heads):
        state = jnp.zeros(states_ref.shape[2:], F32)
        for i in reversed(range(devices)):
            states_ref[i, h] = state.astype(BF16)
            if i > 0:
                step = totals_ref[i, h]
                high = state.astype(BF16)
                low = state - high.astype(F32)
                state = (
                    dot(step[:, :DK], high, TN)
                    + dot(step[:, :DK], low, TN)
                    + deltas_ref[i, h].astype(F32)
                )


PARAMS = pltpu.CompilerParams(
    dimension_semantics=("arbitrary",), vmem_limit_bytes=56 * 1024 * 1024
)
INTERPRET = False


def whole(shape):
    return pl.BlockSpec(shape, lambda c: (0,) * len(shape))


def run_forward(query_key, value, decay_beta, bias, scale, resets):
    tokens, heads = query_key.shape[1], bias.shape[1]
    chunks = tokens // CHUNK
    spans = min(FORWARD_SPANS, chunks)
    step = spans * CHUNK
    key_width, value_width = query_key.shape[2], heads * DV
    return pl.pallas_call(
        forward_kernel,
        grid=(chunks // spans,),
        in_specs=[
            pl.BlockSpec((2, step, key_width), lambda c: (0, c, 0)),
            pl.BlockSpec((step, value_width), lambda c: (c, 0)),
            pl.BlockSpec((step, 2 * heads), lambda c: (c, 0)),
            whole((1, heads)),
            whole((1, heads)),
            pl.BlockSpec((spans, 1, CHUNK), lambda c: (c, 0, 0)),
        ],
        out_specs=[
            pl.BlockSpec((spans, heads, CHUNK, CHUNK), lambda c: (c, 0, 0, 0)),
            pl.BlockSpec((spans, heads, DK, DK + DV), lambda c: (c, 0, 0, 0)),
            pl.BlockSpec((step, value_width), lambda c: (c, 0)),
            pl.BlockSpec((step, value_width), lambda c: (c, 0)),
            whole((heads, DK, DK + DV)),
        ],
        out_shape=[
            jax.ShapeDtypeStruct((chunks, heads, CHUNK, CHUNK), BF16),
            jax.ShapeDtypeStruct((chunks, heads, DK, DK + DV), BF16),
            jax.ShapeDtypeStruct((tokens, value_width), BF16),
            jax.ShapeDtypeStruct((tokens, value_width), F32),
            jax.ShapeDtypeStruct((heads, DK, DK + DV), BF16),
        ],
        scratch_shapes=[pltpu.VMEM((heads, DK, DK + DV), F32)],
        compiler_params=PARAMS,
        interpret=INTERPRET,
        name="forward_blocks",
    )(query_key, value, decay_beta, bias, scale, resets)


def run_output(local, reach, gate, delta_hidden, state_in, gain):
    tokens, value_width = local.shape
    heads = value_width // DV
    chunks = tokens // CHUNK
    block = pl.BlockSpec((CHUNK, value_width), lambda c: (c, 0))
    return pl.pallas_call(
        output_kernel,
        grid=(chunks,),
        in_specs=[
            block,
            block,
            block,
            block,
            whole((heads, DK, DV)),
            whole((1, DV)),
        ],
        out_specs=[block, block, block, whole((heads, DK, DV))],
        out_shape=[
            jax.ShapeDtypeStruct((tokens, value_width), BF16),
            jax.ShapeDtypeStruct((tokens, value_width), BF16),
            jax.ShapeDtypeStruct((tokens, value_width), BF16),
            jax.ShapeDtypeStruct((heads, DK, DV), BF16),
        ],
        scratch_shapes=[pltpu.VMEM((heads, DK, DV), F32)],
        compiler_params=PARAMS,
        interpret=INTERPRET,
        name="gated_norm",
    )(local, reach, gate, delta_hidden, state_in, gain)


def run_backward(
    query_key, value, decay_beta, bias, scale, resets, solve, starts, state_in, delta_out, final
):
    tokens, heads = query_key.shape[1], bias.shape[1]
    chunks = tokens // CHUNK
    spans = min(BACKWARD_SPANS, chunks)
    step = spans * CHUNK
    key_width, value_width = query_key.shape[2], heads * DV
    last = chunks // spans - 1
    return pl.pallas_call(
        backward_kernel,
        grid=(chunks // spans,),
        in_specs=[
            pl.BlockSpec((2, step, key_width), lambda c: (0, last - c, 0)),
            pl.BlockSpec((step, value_width), lambda c: (last - c, 0)),
            pl.BlockSpec((step, 2 * heads), lambda c: (last - c, 0)),
            whole((1, heads)),
            whole((1, heads)),
            pl.BlockSpec((spans, 1, CHUNK), lambda c: (last - c, 0, 0)),
            pl.BlockSpec((spans, heads, CHUNK, CHUNK), lambda c: (last - c, 0, 0, 0)),
            pl.BlockSpec((spans, heads, DK, DK + DV), lambda c: (last - c, 0, 0, 0)),
            whole((heads, DK, DV)),
            pl.BlockSpec((step, value_width), lambda c: (last - c, 0)),
            whole((heads, DK, DV)),
        ],
        out_specs=[
            pl.BlockSpec((step, 2 * key_width + LANES), lambda c: (last - c, 0)),
            pl.BlockSpec((step, value_width), lambda c: (last - c, 0)),
        ],
        out_shape=[
            jax.ShapeDtypeStruct((tokens, 2 * key_width + LANES), BF16),
            jax.ShapeDtypeStruct((tokens, value_width), BF16),
        ],
        scratch_shapes=[pltpu.VMEM((heads, DK, DV), F32)],
        compiler_params=PARAMS,
        interpret=INTERPRET,
        name="backward_blocks",
    )(query_key, value, decay_beta, bias, scale, resets, solve, starts, state_in, delta_out, final)


def spread(array, devices):
    heads, depth, width = array.shape
    if heads >= devices:
        return array.reshape(devices, heads // devices, depth, width)
    cuts = devices // heads
    parts = array.reshape(heads, depth, cuts, width // cuts)
    return jnp.transpose(parts, (0, 2, 1, 3)).reshape(devices, 1, depth, width // cuts)


def gather_parts(parts, heads):
    devices, each, depth, width = parts.shape
    if heads >= devices:
        return parts.reshape(heads, depth, width)
    cuts = devices // heads
    parts = parts.reshape(heads, cuts, depth, width)
    return jnp.transpose(parts, (0, 2, 1, 3)).reshape(heads, depth, cuts * width)


def swap(parts):
    return lax.all_to_all(parts, "ctx", split_axis=0, concat_axis=0, tiled=True)


def spread_totals(totals):
    devices, heads = lax.axis_size("ctx"), totals.shape[0]
    if heads >= devices:
        return spread(totals, devices)
    maps = jnp.repeat(totals[:, :, :DK], devices // heads, axis=0)[:, None]
    return jnp.concatenate([maps, spread(totals[:, :, DK:], devices)], axis=-1)


def run_chain_forward(held):
    return pl.pallas_call(
        chain_forward_kernel,
        out_shape=jax.ShapeDtypeStruct((*held.shape[:3], held.shape[3] - DK), BF16),
        interpret=INTERPRET,
        name="chain_forward",
    )(held)


def run_chain_backward(held, deltas):
    return pl.pallas_call(
        chain_backward_kernel,
        out_shape=jax.ShapeDtypeStruct(deltas.shape, BF16),
        interpret=INTERPRET,
        name="chain_backward",
    )(held, deltas)


def product(spec, a, b):
    return jnp.einsum(spec, a, b, preferred_element_type=F32)


def rows_of(small_weight_ref):
    return jnp.concatenate([small_weight_ref[0].astype(F32), small_weight_ref[1].astype(F32)], axis=0)


def projection_kernel(
    inputs_ref,
    query_key_weight_ref,
    value_weight_ref,
    decay_beta_weight_ref,
    query_key_ref,
    value_ref,
    decay_beta_ref,
):
    inputs = inputs_ref[...]
    query_key_ref[0] = dot(inputs, query_key_weight_ref[0])
    value_ref[...] = dot(inputs, value_weight_ref[0])

    @pl.when(pl.program_id(0) == 0)
    def _():
        decay_beta_ref[...] = dot(inputs, rows_of(decay_beta_weight_ref), NT)


def run_projection(inputs, query_key_weight, value_gate_weight, decay_beta_weight):
    tokens, model = inputs.shape
    key_width, value_width = query_key_weight.shape[2], value_gate_weight.shape[2]
    heads = decay_beta_weight.shape[1]
    steps = 4
    keys, values = 2 * key_width // steps, value_width // steps
    return pl.pallas_call(
        projection_kernel,
        grid=(steps,),
        in_specs=[
            whole((tokens, model)),
            pl.BlockSpec((1, model, keys), lambda j: (j // 2, 0, j % 2)),
            pl.BlockSpec((1, model, values), lambda j: (0, 0, j)),
            whole((2, heads, model)),
        ],
        out_specs=[
            pl.BlockSpec((1, tokens, keys), lambda j: (j // 2, 0, j % 2)),
            pl.BlockSpec((tokens, values), lambda j: (0, j)),
            whole((tokens, 2 * heads)),
        ],
        out_shape=[
            jax.ShapeDtypeStruct((2, tokens, key_width), F32),
            jax.ShapeDtypeStruct((tokens, value_width), F32),
            jax.ShapeDtypeStruct((tokens, 2 * heads), F32),
        ],
        compiler_params=PARAMS,
        interpret=INTERPRET,
        name="projection",
    )(inputs, query_key_weight, value_gate_weight, decay_beta_weight)


def input_gradient_kernel(
    delta_query_key_ref,
    delta_value_ref,
    delta_gate_ref,
    query_key_weight_ref,
    value_gate_weight_ref,
    decay_beta_weight_ref,
    out_ref,
):
    width = query_key_weight_ref.shape[2]
    heads = decay_beta_weight_ref.shape[1]
    keys = jnp.concatenate([query_key_weight_ref[0], query_key_weight_ref[1]], axis=1)
    small = delta_query_key_ref[:, 2 * width : 2 * width + 2 * heads]
    total = dot(delta_gate_ref[...], value_gate_weight_ref[1], NT)
    total += dot(delta_value_ref[...], value_gate_weight_ref[0], NT)
    total += dot(delta_query_key_ref[:, : 2 * width], keys, NT)
    total += dot(small, rows_of(decay_beta_weight_ref))
    out_ref[...] = total.astype(BF16)


def run_input_gradient(
    delta_query_key, delta_value, delta_gate, query_key_weight, value_gate_weight, decay_beta_weight
):
    tokens, model = delta_value.shape[0], query_key_weight.shape[1]
    cut = 512

    def weight(array):
        return pl.BlockSpec((2, cut, array.shape[2]), lambda j: (0, j, 0))

    return pl.pallas_call(
        input_gradient_kernel,
        grid=(model // cut,),
        in_specs=[
            whole(delta_query_key.shape),
            whole(delta_value.shape),
            whole(delta_gate.shape),
            weight(query_key_weight),
            weight(value_gate_weight),
            pl.BlockSpec((2, decay_beta_weight.shape[1], cut), lambda j: (0, 0, j)),
        ],
        out_specs=pl.BlockSpec((tokens, cut), lambda j: (0, j)),
        out_shape=jax.ShapeDtypeStruct((tokens, model), BF16),
        compiler_params=PARAMS,
        interpret=INTERPRET,
        name="input_gradient",
    )(delta_query_key, delta_value, delta_gate, query_key_weight, value_gate_weight, decay_beta_weight)


def together(*arrays):
    return lax.optimization_barrier(arrays)


def exchange(array, distance):
    devices = range(lax.axis_size("ctx"))
    return lax.ppermute(array, "ctx", [(i, i ^ distance) for i in devices])


def block_of(step, place, flip):
    x, y = (place // 2) % 2, place // 4
    core = lax.rem(place + flip, 2)
    across_x, across_y = 1 - step // 2, 1 - lax.rem(step, 2)
    target_x, target_y = lax.rem(x + across_x, 2), lax.rem(y + across_y, 2)
    return target_y * 4 + target_x * 2 + core


def send_kernel(place_ref, left_a_ref, a_ref, left_b_ref, b_ref, out_ref):
    width = a_ref.shape[1]
    out_ref[:, :width] = dot(left_a_ref[...], a_ref[...], TN).astype(BF16)
    out_ref[:, width:] = dot(left_b_ref[...], b_ref[...], TN).astype(BF16)


def keep_kernel(place_ref, left_a_ref, a_ref, left_b_ref, b_ref, arrived_ref, *out_refs):
    step = pl.program_id(0)
    width = a_ref.shape[1]
    a = dot(left_a_ref[...], a_ref[...], TN) + arrived_ref[:, :width].astype(F32)
    b = dot(left_b_ref[...], b_ref[...], TN) + arrived_ref[:, width:].astype(F32)
    for i in range(4):

        @pl.when(step == i)
        def _():
            out_refs[i][...] = a.astype(BF16)
            out_refs[4 + i][...] = b.astype(BF16)


def pair_specs(left_a, a, left_b, b, flip):
    def rows(left):
        return pl.BlockSpec(
            (left.shape[0], left.shape[1] // 8), lambda i, place: (0, block_of(i, place[0], flip))
        )

    def full(delta):
        return pl.BlockSpec(delta.shape, lambda i, place: (0, 0))

    return [rows(left_a), full(a), rows(left_b), full(b)]


def halving_start(place, left_a, a, left_b, b):
    rows, width = left_a.shape[1] // 8, a.shape[1] + b.shape[1]
    return pl.pallas_call(
        send_kernel,
        grid_spec=pltpu.PrefetchScalarGridSpec(
            num_scalar_prefetch=1,
            grid=(4,),
            in_specs=pair_specs(left_a, a, left_b, b, 1),
            out_specs=pl.BlockSpec((rows, width), lambda i, place: (i, 0)),
        ),
        out_shape=jax.ShapeDtypeStruct((4 * rows, width), BF16),
        compiler_params=PARAMS,
        interpret=INTERPRET,
        name="send_rows",
    )(place, left_a, a, left_b, b)


def halving_keep(place, left_a, a, left_b, b, arrived):
    rows = left_a.shape[1] // 8
    return pl.pallas_call(
        keep_kernel,
        grid_spec=pltpu.PrefetchScalarGridSpec(
            num_scalar_prefetch=1,
            grid=(4,),
            in_specs=pair_specs(left_a, a, left_b, b, 0)
            + [pl.BlockSpec((rows, arrived.shape[1]), lambda i, place: (i, 0))],
            out_specs=[
                pl.BlockSpec((rows, delta.shape[1]), lambda i, place: (0, 0))
                for delta in (a, b)
                for _ in range(4)
            ],
        ),
        out_shape=[
            jax.ShapeDtypeStruct((rows, delta.shape[1]), BF16)
            for delta in (a, b)
            for _ in range(4)
        ],
        compiler_params=PARAMS,
        interpret=INTERPRET,
        name="keep_rows",
    )(place, left_a, a, left_b, b, arrived)


def summed(a, b):
    return (a.astype(F32) + b.astype(F32)).astype(BF16)


def halving_cross(pieces):
    a, b = pieces[:4], pieces[4:]
    return exchange(a[0], 2), exchange(b[0], 4), exchange(a[1], 2), exchange(b[2], 4)


def halving_onward(pieces, arrived):
    return summed(pieces[2], arrived[0]), summed(pieces[5], arrived[1])


def halving_last(onward):
    return exchange(onward[0], 4), exchange(onward[1], 2)


def halving_sum(pieces, arrived, last):
    def total(own, near, far):
        return own.astype(F32) + near.astype(F32) + far.astype(F32)

    return total(pieces[3], arrived[2], last[0]), total(pieces[7], arrived[3], last[1])


def scatter(partial, axis, dimension):
    return lax.psum_scatter(partial.astype(BF16), axis, scatter_dimension=dimension, tiled=True)


def body(
    inputs,
    query_key_weight,
    value_gate_weight,
    decay_beta_weight,
    beta_bias,
    decay_scale,
    norm_gain,
    out_weight,
    boundaries,
    grad_mixed,
):
    tokens, heads = inputs.shape[0], beta_bias.shape[0]
    key_width = query_key_weight.shape[2]
    cubic = lax.axis_size("ctx") == 8
    small_weight = jnp.swapaxes(decay_beta_weight, 1, 2)
    query_key, value, decay_beta = run_projection(
        inputs, query_key_weight, value_gate_weight, small_weight
    )
    bias, scale = beta_bias.reshape(1, heads), decay_scale.reshape(1, heads)
    resets = boundaries.reshape(tokens // CHUNK, 1, CHUNK)
    solve, starts, reach, local, totals = run_forward(
        query_key, value, decay_beta, bias, scale, resets
    )

    held = swap(spread_totals(totals))
    gate = product("td,df->tf", inputs, value_gate_weight[1])
    held, gate = together(held, gate)
    states = swap(run_chain_forward(held))
    delta_hidden = product("td,fd->tf", grad_mixed, out_weight)
    states, delta_hidden = together(states, delta_hidden)
    state_in = gather_parts(states, heads)
    hidden, delta_gate, delta_out, delta_state = run_output(
        local, reach, gate, delta_hidden, state_in, norm_gain.reshape(1, DV)
    )

    deltas = swap(spread(delta_state, lax.axis_size("ctx")))
    partial_out = product("tf,fd->td", hidden, out_weight).astype(BF16)
    deltas, partial_out = together(deltas, partial_out)
    mixed = scatter(partial_out, "head", 1)
    finals = swap(run_chain_backward(held, deltas))
    if cubic:
        place = lax.axis_index("ctx").astype(jnp.int32).reshape(1)
        early = (place, inputs, delta_gate, grad_mixed, hidden)
        early_pieces = halving_keep(*early, exchange(halving_start(*early), 1))
        finals, early_pieces = together(finals, early_pieces)
        early_arrived = halving_cross(early_pieces)
    delta_final = gather_parts(finals, heads)
    delta_query_key, delta_value = run_backward(
        query_key,
        value,
        decay_beta,
        bias,
        scale,
        resets,
        solve,
        starts,
        state_in,
        delta_out,
        delta_final,
    )
    if cubic:
        late = (place, inputs, delta_value, inputs, delta_query_key)
        arrived = exchange(halving_start(*late), 1)
        early_onward = halving_onward(early_pieces, early_arrived)
        delta_gate, early_onward = together(delta_gate, early_onward)
        early_last = halving_last(early_onward)
    grad_rows = run_input_gradient(
        delta_query_key,
        delta_value,
        delta_gate,
        query_key_weight,
        value_gate_weight,
        small_weight,
    )
    if cubic:
        grad_rows, arrived = together(grad_rows, arrived)
    grad_inputs = scatter(grad_rows, "head", 1)
    if cubic:
        late_pieces = halving_keep(*late, arrived)
        late_arrived = halving_cross(late_pieces)
        late_last = halving_last(halving_onward(late_pieces, late_arrived))
        grad_gate, grad_out = halving_sum(early_pieces, early_arrived, early_last)
        grad_out = grad_out.T
        grad_value, packed = halving_sum(late_pieces, late_arrived, late_last)
    else:
        grad_gate = scatter(product("td,tf->df", inputs, delta_gate), "ctx", 0).astype(F32)
        grad_out = scatter(product("tf,td->fd", hidden, grad_mixed), "ctx", 1).astype(F32)
        grad_value = scatter(product("td,tf->df", inputs, delta_value), "ctx", 0).astype(F32)
        packed = scatter(product("td,tf->df", inputs, delta_query_key), "ctx", 0).astype(F32)
    rest = packed[:, 2 * key_width :]
    return (
        mixed,
        grad_inputs,
        jnp.stack([packed[:, :key_width], packed[:, key_width : 2 * key_width]]),
        jnp.stack([grad_value, grad_gate]),
        jnp.stack([rest[:, :heads], rest[:, heads : 2 * heads]]),
        grad_out,
    )


def solution(mesh):
    in_specs = (
        P("ctx", None),
        P(None, None, "head"),
        P(None, None, "head"),
        P(None, None, "head"),
        P("head"),
        P("head"),
        P(),
        P("head", None),
        P("ctx"),
        P("ctx", None),
    )
    out_specs = (
        P("ctx", "head"),
        P("ctx", "head"),
        P(None, "ctx", "head"),
        P(None, "ctx", "head"),
        P(None, "ctx", "head"),
        P("head", "ctx"),
    )
    return jax.shard_map(body, mesh=mesh, in_specs=in_specs, out_specs=out_specs, check_vma=False)
```

```python
import functools

import jax
import jax.numpy as jnp
from jax import lax
from jax.experimental import pallas as pl
from jax.experimental.pallas import tpu as pltpu
from jax.sharding import PartitionSpec as P

DK = 128
DV = 128
CHUNK = 128
EPS = 1e-06
QUERY_SCALE = DK ** (-0.5)
LANES = 128
FORWARD_SPANS = 2
BACKWARD_SPANS = 2

F32 = jnp.float32
BF16 = jnp.bfloat16
NN = ((1,), (0,))
NT = ((1,), (1,))
TN = ((0,), (0,))


def dot(a, b, dims=NN):
    return lax.dot_general(
        a.astype(BF16), b.astype(BF16), (dims, ((), ())), preferred_element_type=F32
    )


def exact(a, b, dims=NN):
    return lax.dot_general(
        a, b, (dims, ((), ())), precision=lax.Precision.HIGHEST, preferred_element_type=F32
    )


def softplus(x):
    return jnp.maximum(x, 0.0) + jnp.log1p(jnp.exp(-jnp.abs(x)))


def sigmoid(x):
    return 1.0 / (1.0 + jnp.exp(-x))


def row_sum(x):
    return jnp.sum(x, axis=-1, keepdims=True)


def grid_of(size):
    row = lax.broadcasted_iota(jnp.int32, (size, size), 0)
    col = lax.broadcasted_iota(jnp.int32, (size, size), 1)
    return row, col


def decays(decay_beta, bias_ref, scale_ref, resets):
    row, col = grid_of(CHUNK)
    lower = (row >= col).astype(F32)
    heads = bias_ref.shape[1]
    decay_logit = decay_beta[:, :heads]
    beta = sigmoid(decay_beta[:, heads:] + bias_ref[...])
    log_decay = -scale_ref[...] * softplus(decay_logit)
    resets = jnp.broadcast_to(resets.astype(F32), (8, CHUNK))
    doc_row = dot(resets, lower, NT)[0:1]
    doc_col = dot(lower, resets, NT)[:, 0:1]
    cum_col = exact(lower, log_decay)
    cum_row = exact(log_decay, lower, ((0,), (1,)))
    same = (doc_col == doc_row) & (row >= col)
    start = jnp.where(doc_col == 0.0, jnp.exp(cum_col), 0.0)
    last = CHUNK - 1
    end = jnp.where(
        doc_col == doc_col[last:],
        jnp.exp(jnp.minimum(cum_col[last:] - cum_col, 0.0)),
        0.0,
    )
    return beta, cum_col, cum_row, same, start, end, start[last:], resets


def pair_decay(cum_col, cum_row, same, h):
    gap = jnp.minimum(spread_column(cum_col, h) - cum_row[h : h + 1, :], 0.0)
    return jnp.where(same, jnp.exp(gap), 0.0)


def spread_column(columns, h):
    return jnp.broadcast_to(columns[:, h : h + 1], (columns.shape[0], LANES))


def unit_rows(x):
    inverse = lax.rsqrt(row_sum(x * x) + EPS)
    return x * inverse, inverse


def forward_kernel(
    query_key_ref,
    value_ref,
    decay_beta_ref,
    bias_ref,
    scale_ref,
    resets_ref,
    solve_ref,
    start_ref,
    map_ref,
    local_ref,
    total_ref,
    state_ref,
):
    heads = state_ref.shape[0]
    key_heads = query_key_ref.shape[2] // DK
    repeat = heads // key_heads
    spans = solve_ref.shape[0]
    row, col = grid_of(CHUNK)

    @pl.when(pl.program_id(0) == 0)
    def _():
        first = jnp.concatenate([(row == col).astype(F32), jnp.zeros((DK, DV), F32)], axis=1)
        for h in range(heads):
            state_ref[h] = first

    strict = row > col
    differ = row ^ col
    rows = [slice(c * CHUNK, (c + 1) * CHUNK) for c in range(spans)]
    each = [(c, h) for c in range(spans) for h in range(heads)]
    terms = [
        decays(decay_beta_ref[rows[c]], bias_ref, scale_ref, resets_ref[c]) for c in range(spans)
    ]
    keys, queries = {}, {}
    for c in range(spans):
        for g in range(key_heads):
            cols = slice(g * DK, (g + 1) * DK)
            queries[c, g] = unit_rows(query_key_ref[0, rows[c], cols])[0] * QUERY_SCALE
            keys[c, g] = unit_rows(query_key_ref[1, rows[c], cols])[0]
    grams = {p: (dot(keys[p], keys[p], NT), dot(queries[p], keys[p], NT)) for p in keys}
    scores, systems, betas, starts = {}, {}, {}, {}
    for c, h in each:
        beta, cum_col, cum_row, same, start = terms[c][:5]
        betas[c, h] = spread_column(beta, h)
        starts[c, h] = spread_column(start, h)
        decay = pair_decay(cum_col, cum_row, same, h)
        key_gram, query_gram = grams[c, h // repeat]
        scores[c, h] = (decay * query_gram).astype(BF16)
        systems[c, h] = jnp.where(strict, betas[c, h] * decay * key_gram, 0.0)
    identity = (row == col).astype(F32)
    inverse = {
        p: (identity - jnp.where(differ == 1, systems[p], 0.0)).astype(BF16) for p in each
    }
    level = 1
    while (1 << level) < CHUNK:
        here = (differ >> level) == 1
        inner = {
            p: dot(jnp.where(here, systems[p], 0.0), inverse[p]).astype(BF16) for p in each
        }
        inverse = {p: inverse[p] - dot(inverse[p], inner[p]).astype(BF16) for p in each}
        level += 1
    weights = {}
    for c, h in each:
        k = keys[c, h // repeat]
        v = value_ref[rows[c], h * DV : (h + 1) * DV]
        b = betas[c, h]
        right = jnp.concatenate([(b * starts[c, h]) * k, b * v], axis=1)
        weights[c, h] = dot(inverse[c, h], right)
        solve_ref[c, h] = inverse[c, h]
    for c in range(spans):
        end, total = terms[c][5:7]
        values = []
        for h in range(heads):
            state = state_ref[h].astype(BF16)
            start_ref[c, h] = state
            solved = weights[c, h]
            base = jnp.concatenate([jnp.zeros((CHUNK, DK), F32), solved[:, DK:]], axis=1)
            values.append((base - dot(solved[:, :DK], state)).astype(BF16))
        for h in range(heads):
            k, q = keys[c, h // repeat], queries[c, h // repeat]
            state = state_ref[h]
            out = dot(starts[c, h] * q, state) + dot(scores[c, h], values[h])
            map_ref[rows[c], h * DK : (h + 1) * DK] = out[:, :DK].astype(BF16)
            local_ref[rows[c], h * DV : (h + 1) * DV] = out[:, DK:]
            state = total[:, h : h + 1] * state + dot(spread_column(end, h) * k, values[h], TN)
            state_ref[h] = state
            total_ref[h] = state.astype(BF16)


def output_kernel(
    local_ref,
    map_ref,
    gate_ref,
    delta_ref,
    state_ref,
    gain_ref,
    hidden_ref,
    delta_gate_ref,
    delta_out_ref,
    delta_state_ref,
    total_ref,
):
    heads = state_ref.shape[0]
    gain = gain_ref[...]

    @pl.when(pl.program_id(0) == 0)
    def _():
        total_ref[...] = jnp.zeros_like(total_ref)

    outs, deltas = [], []
    for h in range(heads):
        cols = slice(h * DV, (h + 1) * DV)
        outs.append(local_ref[:, cols] + dot(map_ref[:, cols], state_ref[h]))
    for h in range(heads):
        cols = slice(h * DV, (h + 1) * DV)
        out = outs[h]
        gate = gate_ref[:, cols]
        delta = delta_ref[:, cols]
        scale = lax.rsqrt(row_sum(out * out) * (1.0 / DV) + EPS)
        normed = out * scale
        share = sigmoid(gate)
        silu = gate * share
        scaled = normed * gain
        hidden_ref[:, cols] = (scaled * silu).astype(BF16)
        delta_gate_ref[:, cols] = (
            delta * scaled * (share * (1.0 + gate * (1.0 - share)))
        ).astype(BF16)
        delta_normed = delta * gain * silu
        delta_out = scale * (
            delta_normed - normed * (row_sum(normed * delta_normed) * (1.0 / DV))
        )
        delta_out = delta_out.astype(BF16)
        delta_out_ref[:, cols] = delta_out
        deltas.append(delta_out)
    for h in range(heads):
        cols = slice(h * DV, (h + 1) * DV)
        part = total_ref[h] + dot(map_ref[:, cols], deltas[h], TN)
        total_ref[h] = part
        delta_state_ref[h] = part.astype(BF16)


def backward_kernel(
    query_key_ref,
    value_ref,
    decay_beta_ref,
    bias_ref,
    scale_ref,
    resets_ref,
    solve_ref,
    start_ref,
    state_in_ref,
    delta_out_ref,
    delta_final_ref,
    delta_query_key_ref,
    delta_value_ref,
    carry_ref,
):
    heads = carry_ref.shape[0]
    key_heads = query_key_ref.shape[2] // DK
    repeat = heads // key_heads
    spans = solve_ref.shape[0]
    row, col = grid_of(CHUNK)

    @pl.when(pl.program_id(0) == 0)
    def _():
        carry_ref[...] = delta_final_ref[...].astype(F32)

    strict = row > col
    upper = (row <= col).astype(F32)
    identity = (row == col).astype(F32)
    rows = [slice(c * CHUNK, (c + 1) * CHUNK) for c in range(spans)]
    cols = [slice(h * DV, (h + 1) * DV) for h in range(heads)]
    each = [(c, h) for c in reversed(range(spans)) for h in range(heads)]
    terms = [
        decays(decay_beta_ref[rows[c]], bias_ref, scale_ref, resets_ref[c]) for c in range(spans)
    ]
    half = lax.broadcasted_iota(jnp.int32, (2 * DK, 2 * heads), 0) // DK
    lane = lax.broadcasted_iota(jnp.int32, (2 * DK, 2 * heads), 1)
    lane_one = lax.broadcasted_iota(jnp.int32, (1, heads), 1)
    qs, ks, q_inv, k_inv = {}, {}, {}, {}
    for c in range(spans):
        for g in range(key_heads):
            at = slice(g * DK, (g + 1) * DK)
            q, q_inv[c, g] = unit_rows(query_key_ref[0, rows[c], at])
            qs[c, g] = q * QUERY_SCALE
            ks[c, g], k_inv[c, g] = unit_rows(query_key_ref[1, rows[c], at])
    grams = {p: (dot(ks[p], ks[p], NT), dot(qs[p], ks[p], NT)) for p in ks}
    state_of, value_of, right_of = {}, {}, {}
    betas, starts, ends = {}, {}, {}
    for c, h in each:
        before = start_ref[c, h]
        state = dot(before[:, :DK], state_in_ref[h]) + before[:, DK:].astype(F32)
        state_of[c, h] = state.astype(BF16)
    for c, h in each:
        beta, start, end = terms[c][0], terms[c][4], terms[c][5]
        seen = dot(ks[c, h // repeat], state_of[c, h])
        betas[c, h] = spread_column(beta, h)
        starts[c, h] = spread_column(start, h)
        ends[c, h] = spread_column(end, h)
        right_of[c, h] = betas[c, h] * (value_ref[rows[c], cols[h]] - starts[c, h] * seen)
    for c, h in each:
        value_of[c, h] = dot(solve_ref[c, h], right_of[c, h]).astype(BF16)
    decay_of, delta_value_of, delta_right_of = {}, {}, {}
    for c, h in each:
        decay_of[c, h] = pair_decay(terms[c][1], terms[c][2], terms[c][3], h)
        delta_value_of[c, h] = dot(
            decay_of[c, h] * grams[c, h // repeat][1], delta_out_ref[rows[c], cols[h]], TN
        )
    both_of, held_of, carry_of = {}, {}, {}
    for c in reversed(range(spans)):
        total = terms[c][6]
        for h in range(heads):
            carry_of[c, h] = carry_ref[h].astype(BF16)
            delta_value_of[c, h] += dot(ends[c, h] * ks[c, h // repeat], carry_of[c, h])
        for h in range(heads):
            delta_right_of[c, h] = dot(solve_ref[c, h], delta_value_of[c, h], TN)
        for h in range(heads):
            q, k = qs[c, h // repeat], ks[c, h // repeat]
            b, s = betas[c, h], starts[c, h]
            delta_right = delta_right_of[c, h]
            delta_value_ref[rows[c], cols[h]] = (b * delta_right).astype(BF16)
            both_of[c, h] = jnp.concatenate(
                [delta_out_ref[rows[c], cols[h]], delta_right.astype(BF16)], axis=0
            )
            carry = carry_ref[h]
            held_of[c, h] = total[:, h : h + 1] * row_sum(
                jnp.sum(state_of[c, h].astype(F32) * carry, axis=0, keepdims=True)
            )
            carry_ref[h] = total[:, h : h + 1] * carry + dot(
                jnp.concatenate([s * q, (-b * s) * k], axis=0), both_of[c, h], TN
            )
    pairs_of = {p: dot(both_of[p], value_of[p], NT) for p in each}
    states_of = {p: dot(both_of[p], state_of[p], NT) for p in each}
    ends_of = {p: ends[p] * dot(value_of[p], carry_of[p], NT) for p in each}
    pair_of, sum_of, tail_of, lower_of = {}, {}, {}, {}
    for c, h in each:
        q, k = qs[c, h // repeat], ks[c, h // repeat]
        key_gram, query_gram = grams[c, h // repeat]
        decay, b, s = decay_of[c, h], betas[c, h], starts[c, h]
        pair_q = decay * pairs_of[c, h][:CHUNK]
        pair_k = jnp.where(strict, (-b) * decay * pairs_of[c, h][CHUNK:], 0.0)
        cross = jnp.where(strict, pair_q * query_gram + pair_k * key_gram, 0.0).astype(BF16)
        pair_of[c, h] = (pair_q.astype(BF16), pair_k.astype(BF16))
        state_q = s * states_of[c, h][:CHUNK]
        state_k = (b * s) * states_of[c, h][CHUNK:]
        states_of[c, h] = (state_q, ends_of[c, h] - state_k)
        sum_of[c, h] = jnp.concatenate(
            [cross, (state_q * q - state_k * k).astype(BF16)], axis=1
        )
        tail_of[c, h] = jnp.concatenate(
            [ends_of[c, h] * k, delta_right_of[c, h] * value_of[c, h].astype(F32)], axis=1
        ).astype(BF16)
        lower_of[c, h] = jnp.sum(cross.astype(F32), axis=0, keepdims=True)
    for c in range(spans):
        for g in range(key_heads):
            q, k = qs[c, g], ks[c, g]
            both = jnp.concatenate([q, k], axis=0)
            delta_q = jnp.zeros((CHUNK, DK), F32)
            delta_k = jnp.zeros((CHUNK, DK), F32)
            for h in range(g * repeat, (g + 1) * repeat):
                pair_q, pair_k = pair_of[c, h]
                delta_q += dot(pair_q, k) + states_of[c, h][0]
                delta_k += (
                    dot(pair_k, k)
                    + dot(jnp.concatenate([pair_q, pair_k], axis=0), both, TN)
                    + states_of[c, h][1]
                )
            delta_q = delta_q * QUERY_SCALE
            unit = q * (1.0 / QUERY_SCALE)
            delta_q = q_inv[c, g] * (delta_q - unit * row_sum(unit * delta_q))
            delta_k = k_inv[c, g] * (delta_k - k * row_sum(k * delta_k))
            at, after = g * DK, (key_heads + g) * DK
            delta_query_key_ref[rows[c], at : at + DK] = delta_q.astype(BF16)
            delta_query_key_ref[rows[c], after : after + DK] = delta_k.astype(BF16)
    for c in range(spans):
        beta, resets = terms[c][0], terms[c][7]
        sums = jnp.zeros((CHUNK, 2 * heads), F32)
        tails = jnp.zeros((CHUNK, 2 * heads), F32)
        tail = jnp.zeros((1, heads), F32)
        for h in range(heads):
            sums += dot(sum_of[c, h], lane == h)
            tails += dot(tail_of[c, h], lane == h + heads * half)
            tail = jnp.where(lane_one == h, held_of[c, h], tail)
        below = [lower_of[c, h] for h in range(heads)]
        if heads % 8:
            below.append(jnp.zeros((-heads % 8, CHUNK), F32))
        below = exact(upper, jnp.concatenate(below, axis=0), NT)[:, :heads]
        ends_sum = tails[:, :heads]
        tail = tail + jnp.sum(ends_sum, axis=0, keepdims=True)
        delta_log = exact(upper, sums[:, :heads] - ends_sum) - below + tail
        reset_col = dot(identity, resets, NT)[:, 0:1]
        delta_log = jnp.where(reset_col == 0.0, delta_log, 0.0)
        logits = decay_beta_ref[rows[c], :heads]
        delta_decay = delta_log * (-scale_ref[...]) * sigmoid(logits)
        delta_beta = tails[:, heads:] * (1.0 - beta)
        rest = jnp.zeros((CHUNK, LANES - 2 * heads), F32)
        delta_query_key_ref[rows[c], 2 * key_heads * DK :] = jnp.concatenate(
            [delta_decay, delta_beta, rest], axis=1
        ).astype(BF16)


def chain_forward_kernel(totals_ref, states_ref):
    devices, heads = totals_ref.shape[0], totals_ref.shape[1]
    for h in range(heads):
        state = jnp.zeros(states_ref.shape[2:], F32)
        for i in range(devices):
            states_ref[i, h] = state.astype(BF16)
            if i < devices - 1:
                step = totals_ref[i, h]
                high = state.astype(BF16)
                low = state - high.astype(F32)
                state = (
                    dot(step[:, :DK], high) + dot(step[:, :DK], low) + step[:, DK:].astype(F32)
                )


def chain_backward_kernel(totals_ref, deltas_ref, states_ref):
    devices, heads = totals_ref.shape[0], totals_ref.shape[1]
    for h in range(heads):
        state = jnp.zeros(states_ref.shape[2:], F32)
        for i in reversed(range(devices)):
            states_ref[i, h] = state.astype(BF16)
            if i > 0:
                step = totals_ref[i, h]
                high = state.astype(BF16)
                low = state - high.astype(F32)
                state = (
                    dot(step[:, :DK], high, TN)
                    + dot(step[:, :DK], low, TN)
                    + deltas_ref[i, h].astype(F32)
                )


PARAMS = pltpu.CompilerParams(
    dimension_semantics=("arbitrary",), vmem_limit_bytes=56 * 1024 * 1024
)
INTERPRET = False


def cost(microseconds):
    return pl.CostEstimate(
        flops=int(microseconds * 1e9),
        bytes_accessed=int(microseconds * 3.6e6),
        transcendentals=0,
    )


def whole(shape):
    return pl.BlockSpec(shape, lambda c: (0,) * len(shape))


def run_forward(query_key, value, decay_beta, bias, scale, resets):
    tokens, heads = query_key.shape[1], bias.shape[1]
    chunks = tokens // CHUNK
    spans = min(FORWARD_SPANS, chunks)
    step = spans * CHUNK
    key_width, value_width = query_key.shape[2], heads * DV
    return pl.pallas_call(
        forward_kernel,
        grid=(chunks // spans,),
        in_specs=[
            pl.BlockSpec((2, step, key_width), lambda c: (0, c, 0)),
            pl.BlockSpec((step, value_width), lambda c: (c, 0)),
            pl.BlockSpec((step, 2 * heads), lambda c: (c, 0)),
            whole((1, heads)),
            whole((1, heads)),
            pl.BlockSpec((spans, 1, CHUNK), lambda c: (c, 0, 0)),
        ],
        out_specs=[
            pl.BlockSpec((spans, heads, CHUNK, CHUNK), lambda c: (c, 0, 0, 0)),
            pl.BlockSpec((spans, heads, DK, DK + DV), lambda c: (c, 0, 0, 0)),
            pl.BlockSpec((step, value_width), lambda c: (c, 0)),
            pl.BlockSpec((step, value_width), lambda c: (c, 0)),
            whole((heads, DK, DK + DV)),
        ],
        out_shape=[
            jax.ShapeDtypeStruct((chunks, heads, CHUNK, CHUNK), BF16),
            jax.ShapeDtypeStruct((chunks, heads, DK, DK + DV), BF16),
            jax.ShapeDtypeStruct((tokens, value_width), BF16),
            jax.ShapeDtypeStruct((tokens, value_width), F32),
            jax.ShapeDtypeStruct((heads, DK, DK + DV), BF16),
        ],
        scratch_shapes=[pltpu.VMEM((heads, DK, DK + DV), F32)],
        compiler_params=PARAMS,
        interpret=INTERPRET,
        cost_estimate=cost(13),
        name="forward_blocks",
    )(query_key, value, decay_beta, bias, scale, resets)


def run_output(local, reach, gate, delta_hidden, state_in, gain):
    tokens, value_width = local.shape
    heads = value_width // DV
    chunks = tokens // CHUNK
    block = pl.BlockSpec((CHUNK, value_width), lambda c: (c, 0))
    return pl.pallas_call(
        output_kernel,
        grid=(chunks,),
        in_specs=[
            block,
            block,
            block,
            block,
            whole((heads, DK, DV)),
            whole((1, DV)),
        ],
        out_specs=[block, block, block, whole((heads, DK, DV))],
        out_shape=[
            jax.ShapeDtypeStruct((tokens, value_width), BF16),
            jax.ShapeDtypeStruct((tokens, value_width), BF16),
            jax.ShapeDtypeStruct((tokens, value_width), BF16),
            jax.ShapeDtypeStruct((heads, DK, DV), BF16),
        ],
        scratch_shapes=[pltpu.VMEM((heads, DK, DV), F32)],
        compiler_params=PARAMS,
        interpret=INTERPRET,
        cost_estimate=cost(7),
        name="gated_norm",
    )(local, reach, gate, delta_hidden, state_in, gain)


def run_backward(
    query_key, value, decay_beta, bias, scale, resets, solve, starts, state_in, delta_out, final
):
    tokens, heads = query_key.shape[1], bias.shape[1]
    chunks = tokens // CHUNK
    spans = min(BACKWARD_SPANS, chunks)
    step = spans * CHUNK
    key_width, value_width = query_key.shape[2], heads * DV
    last = chunks // spans - 1
    return pl.pallas_call(
        backward_kernel,
        grid=(chunks // spans,),
        in_specs=[
            pl.BlockSpec((2, step, key_width), lambda c: (0, last - c, 0)),
            pl.BlockSpec((step, value_width), lambda c: (last - c, 0)),
            pl.BlockSpec((step, 2 * heads), lambda c: (last - c, 0)),
            whole((1, heads)),
            whole((1, heads)),
            pl.BlockSpec((spans, 1, CHUNK), lambda c: (last - c, 0, 0)),
            pl.BlockSpec((spans, heads, CHUNK, CHUNK), lambda c: (last - c, 0, 0, 0)),
            pl.BlockSpec((spans, heads, DK, DK + DV), lambda c: (last - c, 0, 0, 0)),
            whole((heads, DK, DV)),
            pl.BlockSpec((step, value_width), lambda c: (last - c, 0)),
            whole((heads, DK, DV)),
        ],
        out_specs=[
            pl.BlockSpec((step, 2 * key_width + LANES), lambda c: (last - c, 0)),
            pl.BlockSpec((step, value_width), lambda c: (last - c, 0)),
        ],
        out_shape=[
            jax.ShapeDtypeStruct((tokens, 2 * key_width + LANES), BF16),
            jax.ShapeDtypeStruct((tokens, value_width), BF16),
        ],
        scratch_shapes=[pltpu.VMEM((heads, DK, DV), F32)],
        compiler_params=PARAMS,
        interpret=INTERPRET,
        cost_estimate=cost(17),
        name="backward_blocks",
    )(query_key, value, decay_beta, bias, scale, resets, solve, starts, state_in, delta_out, final)


def spread(array, devices):
    heads, depth, width = array.shape
    if heads >= devices:
        return array.reshape(devices, heads // devices, depth, width)
    cuts = devices // heads
    parts = array.reshape(heads, depth, cuts, width // cuts)
    return jnp.transpose(parts, (0, 2, 1, 3)).reshape(devices, 1, depth, width // cuts)


def gather_parts(parts, heads):
    devices, each, depth, width = parts.shape
    if heads >= devices:
        return parts.reshape(heads, depth, width)
    cuts = devices // heads
    parts = parts.reshape(heads, cuts, depth, width)
    return jnp.transpose(parts, (0, 2, 1, 3)).reshape(heads, depth, cuts * width)


def swap(parts):
    return lax.all_to_all(parts, "ctx", split_axis=0, concat_axis=0, tiled=True)


def spread_totals(totals):
    devices, heads = lax.axis_size("ctx"), totals.shape[0]
    if heads >= devices:
        return spread(totals, devices)
    maps = jnp.repeat(totals[:, :, :DK], devices // heads, axis=0)[:, None]
    return jnp.concatenate([maps, spread(totals[:, :, DK:], devices)], axis=-1)


def run_chain_forward(held):
    return pl.pallas_call(
        chain_forward_kernel,
        out_shape=jax.ShapeDtypeStruct((*held.shape[:3], held.shape[3] - DK), BF16),
        interpret=INTERPRET,
        cost_estimate=cost(3),
        name="chain_forward",
    )(held)


def run_chain_backward(held, deltas):
    return pl.pallas_call(
        chain_backward_kernel,
        out_shape=jax.ShapeDtypeStruct(deltas.shape, BF16),
        interpret=INTERPRET,
        cost_estimate=cost(3),
        name="chain_backward",
    )(held, deltas)


def product(spec, a, b):
    return jnp.einsum(spec, a, b, preferred_element_type=F32)


def rows_of(small_weight_ref):
    return jnp.concatenate([small_weight_ref[0].astype(F32), small_weight_ref[1].astype(F32)], axis=0)


def projection_kernel(
    inputs_ref,
    query_key_weight_ref,
    value_weight_ref,
    decay_beta_weight_ref,
    query_key_ref,
    value_ref,
    decay_beta_ref,
):
    inputs = inputs_ref[...]
    query_key_ref[0] = dot(inputs, query_key_weight_ref[0])
    value_ref[...] = dot(inputs, value_weight_ref[0])

    @pl.when(pl.program_id(0) == 0)
    def _():
        decay_beta_ref[...] = dot(inputs, rows_of(decay_beta_weight_ref), NT)


def run_projection(inputs, query_key_weight, value_gate_weight, decay_beta_weight):
    tokens, model = inputs.shape
    key_width, value_width = query_key_weight.shape[2], value_gate_weight.shape[2]
    heads = decay_beta_weight.shape[1]
    steps = 4
    keys, values = 2 * key_width // steps, value_width // steps
    return pl.pallas_call(
        projection_kernel,
        grid=(steps,),
        in_specs=[
            whole((tokens, model)),
            pl.BlockSpec((1, model, keys), lambda j: (j // 2, 0, j % 2)),
            pl.BlockSpec((1, model, values), lambda j: (0, 0, j)),
            whole((2, heads, model)),
        ],
        out_specs=[
            pl.BlockSpec((1, tokens, keys), lambda j: (j // 2, 0, j % 2)),
            pl.BlockSpec((tokens, values), lambda j: (0, j)),
            whole((tokens, 2 * heads)),
        ],
        out_shape=[
            jax.ShapeDtypeStruct((2, tokens, key_width), F32),
            jax.ShapeDtypeStruct((tokens, value_width), F32),
            jax.ShapeDtypeStruct((tokens, 2 * heads), F32),
        ],
        compiler_params=PARAMS,
        interpret=INTERPRET,
        cost_estimate=cost(10),
        name="projection",
    )(inputs, query_key_weight, value_gate_weight, decay_beta_weight)


def input_gradient_kernel(
    delta_query_key_ref,
    delta_value_ref,
    delta_gate_ref,
    query_key_weight_ref,
    value_gate_weight_ref,
    decay_beta_weight_ref,
    first_ref,
    second_ref,
):
    width = query_key_weight_ref.shape[2]
    heads = decay_beta_weight_ref.shape[1]
    keys = jnp.concatenate([query_key_weight_ref[0], query_key_weight_ref[1]], axis=1)
    small = delta_query_key_ref[:, 2 * width : 2 * width + 2 * heads]
    total = dot(delta_gate_ref[...], value_gate_weight_ref[1], NT)
    total += dot(delta_value_ref[...], value_gate_weight_ref[0], NT)
    total += dot(delta_query_key_ref[:, : 2 * width], keys, NT)
    total += dot(small, rows_of(decay_beta_weight_ref))
    total = total.astype(BF16)
    cut = first_ref.shape[0]
    first_ref[...] = total[:cut]
    second_ref[...] = total[cut:]


def run_input_gradient(
    delta_query_key, delta_value, delta_gate, query_key_weight, value_gate_weight, decay_beta_weight
):
    tokens, model = delta_value.shape[0], query_key_weight.shape[1]
    cut = 512

    def weight(array):
        return pl.BlockSpec((2, cut, array.shape[2]), lambda j: (0, j, 0))

    return pl.pallas_call(
        input_gradient_kernel,
        grid=(model // cut,),
        in_specs=[
            whole(delta_query_key.shape),
            whole(delta_value.shape),
            whole(delta_gate.shape),
            weight(query_key_weight),
            weight(value_gate_weight),
            pl.BlockSpec((2, decay_beta_weight.shape[1], cut), lambda j: (0, 0, j)),
        ],
        out_specs=[pl.BlockSpec((tokens // 2, cut), lambda j: (0, j))] * 2,
        out_shape=[jax.ShapeDtypeStruct((tokens // 2, model), BF16)] * 2,
        compiler_params=PARAMS,
        interpret=INTERPRET,
        cost_estimate=cost(11),
        name="input_gradient",
    )(delta_query_key, delta_value, delta_gate, query_key_weight, value_gate_weight, decay_beta_weight)


def together(*arrays):
    return lax.optimization_barrier(arrays)


def exchange(array, distance):
    devices = range(lax.axis_size("ctx"))
    return lax.ppermute(array, "ctx", [(i, i ^ distance) for i in devices])


def block_of(step, place, flip):
    x, y = (place // 2) % 2, place // 4
    core = lax.rem(place + flip, 2)
    across_x, across_y = 1 - step // 2, 1 - lax.rem(step, 2)
    target_x, target_y = lax.rem(x + across_x, 2), lax.rem(y + across_y, 2)
    return target_y * 4 + target_x * 2 + core


def send_kernel(place_ref, left_a_ref, a_ref, left_b_ref, b_ref, out_ref):
    width = a_ref.shape[1]
    out_ref[:, :width] = dot(left_a_ref[...], a_ref[...], TN).astype(BF16)
    out_ref[:, width:] = dot(left_b_ref[...], b_ref[...], TN).astype(BF16)


def keep_kernel(place_ref, left_a_ref, a_ref, left_b_ref, b_ref, arrived_ref, *out_refs):
    step = pl.program_id(0)
    width = a_ref.shape[1]
    a = dot(left_a_ref[...], a_ref[...], TN) + arrived_ref[:, :width].astype(F32)
    b = dot(left_b_ref[...], b_ref[...], TN) + arrived_ref[:, width:].astype(F32)
    for i in range(4):

        @pl.when(step == i)
        def _():
            out_refs[i][...] = a.astype(BF16)
            out_refs[4 + i][...] = b.astype(BF16)


def pair_specs(left_a, a, left_b, b, flip):
    def rows(left):
        return pl.BlockSpec(
            (left.shape[0], left.shape[1] // 8), lambda i, place: (0, block_of(i, place[0], flip))
        )

    def full(delta):
        return pl.BlockSpec(delta.shape, lambda i, place: (0, 0))

    return [rows(left_a), full(a), rows(left_b), full(b)]


def halving_start(place, left_a, a, left_b, b):
    rows, width = left_a.shape[1] // 8, a.shape[1] + b.shape[1]
    return pl.pallas_call(
        send_kernel,
        grid_spec=pltpu.PrefetchScalarGridSpec(
            num_scalar_prefetch=1,
            grid=(4,),
            in_specs=pair_specs(left_a, a, left_b, b, 1),
            out_specs=pl.BlockSpec((rows, width), lambda i, place: (i, 0)),
        ),
        out_shape=jax.ShapeDtypeStruct((4 * rows, width), BF16),
        compiler_params=PARAMS,
        interpret=INTERPRET,
        cost_estimate=cost(6),
        name="send_rows",
    )(place, left_a, a, left_b, b)


def halving_keep(place, left_a, a, left_b, b, arrived):
    rows = left_a.shape[1] // 8
    return pl.pallas_call(
        keep_kernel,
        grid_spec=pltpu.PrefetchScalarGridSpec(
            num_scalar_prefetch=1,
            grid=(4,),
            in_specs=pair_specs(left_a, a, left_b, b, 0)
            + [pl.BlockSpec((rows, arrived.shape[1]), lambda i, place: (i, 0))],
            out_specs=[
                pl.BlockSpec((rows, delta.shape[1]), lambda i, place: (0, 0))
                for delta in (a, b)
                for _ in range(4)
            ],
        ),
        out_shape=[
            jax.ShapeDtypeStruct((rows, delta.shape[1]), BF16)
            for delta in (a, b)
            for _ in range(4)
        ],
        compiler_params=PARAMS,
        interpret=INTERPRET,
        cost_estimate=cost(8),
        name="keep_rows",
    )(place, left_a, a, left_b, b, arrived)


def summed(a, b):
    return (a.astype(F32) + b.astype(F32)).astype(BF16)


def halving_cross(pieces):
    return exchange(pieces[0], 2), exchange(pieces[4], 4)


def halving_stay(pieces):
    return exchange(pieces[1], 2), exchange(pieces[6], 4)


def halving_onward(pieces, arrived):
    return summed(pieces[2], arrived[0]), summed(pieces[5], arrived[1])


def halving_last(onward):
    return exchange(onward[0], 4), exchange(onward[1], 2)


def halving_sum(pieces, arrived, last):
    def total(own, near, far):
        return own.astype(F32) + near.astype(F32) + far.astype(F32)

    return total(pieces[3], arrived[0], last[0]), total(pieces[7], arrived[1], last[1])


def line_hop(step, partial, received):
    devices = lax.axis_size("head")
    place = lax.axis_index("head")

    def send(block, arrived, route):
        part = line_block(partial, jnp.clip(block, 0, devices - 1))
        if arrived is not None:
            part = summed(part, arrived)
        return lax.ppermute(part, "head", route)

    up = [(i, i + 1) for i in range(step)]
    down = [(i, i - 1) for i in range(devices - step, devices)]
    return (
        send(devices - step + place, received[0], up),
        send(place - devices + step, received[1], down),
    )


def line_block(partial, block):
    width = partial.shape[1] // lax.axis_size("head")
    return lax.dynamic_slice_in_dim(partial, block * width, width, 1)


def line_sum(partial, received):
    own = line_block(partial, lax.axis_index("head")).astype(F32)
    return (own + received[0].astype(F32) + received[1].astype(F32)).astype(BF16)


def scatter(partial, axis, dimension):
    return lax.psum_scatter(partial.astype(BF16), axis, scatter_dimension=dimension, tiled=True)


def body(
    inputs,
    query_key_weight,
    value_gate_weight,
    decay_beta_weight,
    beta_bias,
    decay_scale,
    norm_gain,
    out_weight,
    boundaries,
    grad_mixed,
):
    tokens, heads = inputs.shape[0], beta_bias.shape[0]
    key_width = query_key_weight.shape[2]
    cubic = lax.axis_size("ctx") == 8
    small_weight = jnp.swapaxes(decay_beta_weight, 1, 2)
    query_key, value, decay_beta = run_projection(
        inputs, query_key_weight, value_gate_weight, small_weight
    )
    bias, scale = beta_bias.reshape(1, heads), decay_scale.reshape(1, heads)
    resets = boundaries.reshape(tokens // CHUNK, 1, CHUNK)
    solve, starts, reach, local, totals = run_forward(
        query_key, value, decay_beta, bias, scale, resets
    )

    held = swap(spread_totals(totals))
    gate = product("td,df->tf", inputs, value_gate_weight[1])
    held, gate = together(held, gate)
    states = swap(run_chain_forward(held))
    delta_hidden = product("td,fd->tf", grad_mixed, out_weight)
    states, delta_hidden = together(states, delta_hidden)
    state_in = gather_parts(states, heads)
    hidden, delta_gate, delta_out, delta_state = run_output(
        local, reach, gate, delta_hidden, state_in, norm_gain.reshape(1, DV)
    )

    deltas = swap(spread(delta_state, lax.axis_size("ctx")))
    partial_out = product("tf,fd->td", hidden, out_weight).astype(BF16)
    deltas, partial_out = together(deltas, partial_out)
    line = cubic and lax.axis_size("head") == 4
    if line:
        hop = line_hop(1, partial_out, (None, None))
    else:
        mixed = scatter(partial_out, "head", 1)
    finals = swap(run_chain_backward(held, deltas))
    if cubic:
        place = lax.axis_index("ctx").astype(jnp.int32).reshape(1)
        early = (place, inputs, delta_gate, grad_mixed, hidden)
        early_pieces = halving_keep(*early, exchange(halving_start(*early), 1))
        finals, early_pieces = together(finals, early_pieces)
        if line:
            finals, hop = together(finals, hop)
            hop = line_hop(2, partial_out, hop)
        early_arrived = halving_cross(early_pieces)
    delta_final = gather_parts(finals, heads)
    delta_query_key, delta_value = run_backward(
        query_key,
        value,
        decay_beta,
        bias,
        scale,
        resets,
        solve,
        starts,
        state_in,
        delta_out,
        delta_final,
    )
    if cubic:
        delta_value, early_arrived, early_pieces = together(
            delta_value, early_arrived, early_pieces
        )
        if line:
            delta_value, hop = together(delta_value, hop)
            hop = line_hop(3, partial_out, hop)
        early_last = halving_last(halving_onward(early_pieces, early_arrived))
        early_stay = halving_stay(early_pieces)
        late = (place, inputs, delta_value, inputs, delta_query_key)
        arrived = exchange(halving_start(*late), 1)
    grad_rows = run_input_gradient(
        delta_query_key,
        delta_value,
        delta_gate,
        query_key_weight,
        value_gate_weight,
        small_weight,
    )
    if cubic:
        grad_rows, arrived, early_last = together(grad_rows, arrived, early_last)
        if line:
            arrived, hop = together(arrived, hop)
            mixed = line_sum(partial_out, hop)
    grad_inputs = jnp.concatenate([scatter(part, "head", 1) for part in grad_rows], axis=0)
    if cubic:
        late_pieces = halving_keep(*late, arrived)
        late_pieces, early_stay = together(late_pieces, early_stay)
        late_arrived = halving_cross(late_pieces)
        late_stay = halving_stay(late_pieces)
        late_last = halving_last(halving_onward(late_pieces, late_arrived))
        grad_gate, grad_out = halving_sum(early_pieces, early_stay, early_last)
        grad_out = grad_out.T
        grad_value, packed = halving_sum(late_pieces, late_stay, late_last)
    else:
        grad_gate = scatter(product("td,tf->df", inputs, delta_gate), "ctx", 0).astype(F32)
        grad_out = scatter(product("tf,td->fd", hidden, grad_mixed), "ctx", 1).astype(F32)
        grad_value = scatter(product("td,tf->df", inputs, delta_value), "ctx", 0).astype(F32)
        packed = scatter(product("td,tf->df", inputs, delta_query_key), "ctx", 0).astype(F32)
    rest = packed[:, 2 * key_width :]
    return (
        mixed,
        grad_inputs,
        jnp.stack([packed[:, :key_width], packed[:, key_width : 2 * key_width]]),
        jnp.stack([grad_value, grad_gate]),
        jnp.stack([rest[:, :heads], rest[:, heads : 2 * heads]]),
        grad_out,
    )


def solution(mesh):
    in_specs = (
        P("ctx", None),
        P(None, None, "head"),
        P(None, None, "head"),
        P(None, None, "head"),
        P("head"),
        P("head"),
        P(),
        P("head", None),
        P("ctx"),
        P("ctx", None),
    )
    out_specs = (
        P("ctx", "head"),
        P("ctx", "head"),
        P(None, "ctx", "head"),
        P(None, "ctx", "head"),
        P(None, "ctx", "head"),
        P("head", "ctx"),
    )
    return jax.shard_map(body, mesh=mesh, in_specs=in_specs, out_specs=out_specs, check_vma=False)
```

```python
import functools

import jax
import jax.numpy as jnp
from jax import lax
from jax.experimental import pallas as pl
from jax.experimental.pallas import tpu as pltpu
from jax.sharding import PartitionSpec as P

DK = 128
DV = 128
CHUNK = 128
EPS = 1e-06
QUERY_SCALE = DK ** (-0.5)
LANES = 128
FORWARD_SPANS = 2
BACKWARD_SPANS = 2

F32 = jnp.float32
BF16 = jnp.bfloat16
NN = ((1,), (0,))
NT = ((1,), (1,))
TN = ((0,), (0,))


def dot(a, b, dims=NN):
    return lax.dot_general(
        a.astype(BF16), b.astype(BF16), (dims, ((), ())), preferred_element_type=F32
    )


def exact(a, b, dims=NN):
    return lax.dot_general(
        a, b, (dims, ((), ())), precision=lax.Precision.HIGHEST, preferred_element_type=F32
    )


def softplus(x):
    return jnp.maximum(x, 0.0) + jnp.log1p(jnp.exp(-jnp.abs(x)))


def sigmoid(x):
    return 1.0 / (1.0 + jnp.exp(-x))


def row_sum(x):
    return jnp.sum(x, axis=-1, keepdims=True)


def grid_of(size):
    row = lax.broadcasted_iota(jnp.int32, (size, size), 0)
    col = lax.broadcasted_iota(jnp.int32, (size, size), 1)
    return row, col


def decays(decay_beta, bias_ref, scale_ref, resets):
    row, col = grid_of(CHUNK)
    lower = (row >= col).astype(F32)
    heads = bias_ref.shape[1]
    decay_logit = decay_beta[:, :heads]
    beta = sigmoid(decay_beta[:, heads:] + bias_ref[...])
    log_decay = -scale_ref[...] * softplus(decay_logit)
    resets = jnp.broadcast_to(resets.astype(F32), (8, CHUNK))
    doc_row = dot(resets, lower, NT)[0:1]
    doc_col = dot(lower, resets, NT)[:, 0:1]
    cum_col = exact(lower, log_decay)
    cum_row = exact(log_decay, lower, ((0,), (1,)))
    same = (doc_col == doc_row) & (row >= col)
    start = jnp.where(doc_col == 0.0, jnp.exp(cum_col), 0.0)
    last = CHUNK - 1
    end = jnp.where(
        doc_col == doc_col[last:],
        jnp.exp(jnp.minimum(cum_col[last:] - cum_col, 0.0)),
        0.0,
    )
    return beta, cum_col, cum_row, same, start, end, start[last:], resets


def pair_decay(cum_col, cum_row, same, h):
    gap = jnp.minimum(spread_column(cum_col, h) - cum_row[h : h + 1, :], 0.0)
    return jnp.where(same, jnp.exp(gap), 0.0)


def spread_column(columns, h):
    return jnp.broadcast_to(columns[:, h : h + 1], (columns.shape[0], LANES))


def unit_rows(x):
    inverse = lax.rsqrt(row_sum(x * x) + EPS)
    return x * inverse, inverse


def forward_kernel(
    query_key_ref,
    value_ref,
    decay_beta_ref,
    bias_ref,
    scale_ref,
    resets_ref,
    solve_ref,
    start_ref,
    map_ref,
    local_ref,
    total_ref,
    state_ref,
):
    heads = state_ref.shape[0]
    key_heads = query_key_ref.shape[2] // DK
    repeat = heads // key_heads
    spans = solve_ref.shape[0]
    row, col = grid_of(CHUNK)

    @pl.when(pl.program_id(0) == 0)
    def _():
        first = jnp.concatenate([(row == col).astype(F32), jnp.zeros((DK, DV), F32)], axis=1)
        for h in range(heads):
            state_ref[h] = first

    strict = row > col
    differ = row ^ col
    rows = [slice(c * CHUNK, (c + 1) * CHUNK) for c in range(spans)]
    each = [(c, h) for c in range(spans) for h in range(heads)]
    terms = [
        decays(decay_beta_ref[rows[c]], bias_ref, scale_ref, resets_ref[c]) for c in range(spans)
    ]
    keys, queries = {}, {}
    for c in range(spans):
        for g in range(key_heads):
            cols = slice(g * DK, (g + 1) * DK)
            queries[c, g] = unit_rows(query_key_ref[0, rows[c], cols])[0] * QUERY_SCALE
            keys[c, g] = unit_rows(query_key_ref[1, rows[c], cols])[0]
    grams = {p: (dot(keys[p], keys[p], NT), dot(queries[p], keys[p], NT)) for p in keys}
    scores, systems, betas, starts = {}, {}, {}, {}
    for c, h in each:
        beta, cum_col, cum_row, same, start = terms[c][:5]
        betas[c, h] = spread_column(beta, h)
        starts[c, h] = spread_column(start, h)
        decay = pair_decay(cum_col, cum_row, same, h)
        key_gram, query_gram = grams[c, h // repeat]
        scores[c, h] = (decay * query_gram).astype(BF16)
        systems[c, h] = jnp.where(strict, betas[c, h] * decay * key_gram, 0.0)
    identity = (row == col).astype(F32)
    inverse = {
        p: (identity - jnp.where(differ == 1, systems[p], 0.0)).astype(BF16) for p in each
    }
    level = 1
    while (1 << level) < CHUNK:
        here = (differ >> level) == 1
        inner = {
            p: dot(jnp.where(here, systems[p], 0.0), inverse[p]).astype(BF16) for p in each
        }
        inverse = {p: inverse[p] - dot(inverse[p], inner[p]).astype(BF16) for p in each}
        level += 1
    weights = {}
    for c, h in each:
        k = keys[c, h // repeat]
        v = value_ref[rows[c], h * DV : (h + 1) * DV]
        b = betas[c, h]
        right = jnp.concatenate([(b * starts[c, h]) * k, b * v], axis=1)
        weights[c, h] = dot(inverse[c, h], right)
        solve_ref[c, h] = inverse[c, h]
    for c in range(spans):
        end, total = terms[c][5:7]
        values = []
        for h in range(heads):
            state = state_ref[h].astype(BF16)
            start_ref[c, h] = state
            solved = weights[c, h]
            base = jnp.concatenate([jnp.zeros((CHUNK, DK), F32), solved[:, DK:]], axis=1)
            values.append((base - dot(solved[:, :DK], state)).astype(BF16))
        for h in range(heads):
            k, q = keys[c, h // repeat], queries[c, h // repeat]
            state = state_ref[h]
            out = dot(starts[c, h] * q, state) + dot(scores[c, h], values[h])
            map_ref[rows[c], h * DK : (h + 1) * DK] = out[:, :DK].astype(BF16)
            local_ref[rows[c], h * DV : (h + 1) * DV] = out[:, DK:]
            state = total[:, h : h + 1] * state + dot(spread_column(end, h) * k, values[h], TN)
            state_ref[h] = state
            total_ref[h] = state.astype(BF16)


def output_kernel(
    local_ref,
    map_ref,
    gate_ref,
    delta_ref,
    state_ref,
    gain_ref,
    hidden_ref,
    delta_gate_ref,
    delta_out_ref,
    delta_state_ref,
    total_ref,
):
    heads = state_ref.shape[0]
    gain = gain_ref[...]

    @pl.when(pl.program_id(0) == 0)
    def _():
        total_ref[...] = jnp.zeros_like(total_ref)

    outs, deltas = [], []
    for h in range(heads):
        cols = slice(h * DV, (h + 1) * DV)
        outs.append(local_ref[:, cols] + dot(map_ref[:, cols], state_ref[h]))
    for h in range(heads):
        cols = slice(h * DV, (h + 1) * DV)
        out = outs[h]
        gate = gate_ref[:, cols]
        delta = delta_ref[:, cols]
        scale = lax.rsqrt(row_sum(out * out) * (1.0 / DV) + EPS)
        normed = out * scale
        share = sigmoid(gate)
        silu = gate * share
        scaled = normed * gain
        hidden_ref[:, cols] = (scaled * silu).astype(BF16)
        delta_gate_ref[:, cols] = (
            delta * scaled * (share * (1.0 + gate * (1.0 - share)))
        ).astype(BF16)
        delta_normed = delta * gain * silu
        delta_out = scale * (
            delta_normed - normed * (row_sum(normed * delta_normed) * (1.0 / DV))
        )
        delta_out = delta_out.astype(BF16)
        delta_out_ref[:, cols] = delta_out
        deltas.append(delta_out)
    for h in range(heads):
        cols = slice(h * DV, (h + 1) * DV)
        part = total_ref[h] + dot(map_ref[:, cols], deltas[h], TN)
        total_ref[h] = part
        delta_state_ref[h] = part.astype(BF16)


def backward_kernel(
    query_key_ref,
    value_ref,
    decay_beta_ref,
    bias_ref,
    scale_ref,
    resets_ref,
    solve_ref,
    start_ref,
    state_in_ref,
    delta_out_ref,
    delta_final_ref,
    delta_query_key_ref,
    delta_value_ref,
    carry_ref,
):
    heads = carry_ref.shape[0]
    key_heads = query_key_ref.shape[2] // DK
    repeat = heads // key_heads
    spans = solve_ref.shape[0]
    row, col = grid_of(CHUNK)

    @pl.when(pl.program_id(0) == 0)
    def _():
        carry_ref[...] = delta_final_ref[...].astype(F32)

    strict = row > col
    upper = (row <= col).astype(F32)
    identity = (row == col).astype(F32)
    rows = [slice(c * CHUNK, (c + 1) * CHUNK) for c in range(spans)]
    cols = [slice(h * DV, (h + 1) * DV) for h in range(heads)]
    each = [(c, h) for c in reversed(range(spans)) for h in range(heads)]
    terms = [
        decays(decay_beta_ref[rows[c]], bias_ref, scale_ref, resets_ref[c]) for c in range(spans)
    ]
    half = lax.broadcasted_iota(jnp.int32, (2 * DK, 2 * heads), 0) // DK
    lane = lax.broadcasted_iota(jnp.int32, (2 * DK, 2 * heads), 1)
    lane_one = lax.broadcasted_iota(jnp.int32, (1, heads), 1)
    qs, ks, q_inv, k_inv = {}, {}, {}, {}
    for c in range(spans):
        for g in range(key_heads):
            at = slice(g * DK, (g + 1) * DK)
            q, q_inv[c, g] = unit_rows(query_key_ref[0, rows[c], at])
            qs[c, g] = q * QUERY_SCALE
            ks[c, g], k_inv[c, g] = unit_rows(query_key_ref[1, rows[c], at])
    grams = {p: (dot(ks[p], ks[p], NT), dot(qs[p], ks[p], NT)) for p in ks}
    state_of, value_of, right_of = {}, {}, {}
    betas, starts, ends = {}, {}, {}
    for c, h in each:
        before = start_ref[c, h]
        state = dot(before[:, :DK], state_in_ref[h]) + before[:, DK:].astype(F32)
        state_of[c, h] = state.astype(BF16)
    for c, h in each:
        beta, start, end = terms[c][0], terms[c][4], terms[c][5]
        seen = dot(ks[c, h // repeat], state_of[c, h])
        betas[c, h] = spread_column(beta, h)
        starts[c, h] = spread_column(start, h)
        ends[c, h] = spread_column(end, h)
        right_of[c, h] = betas[c, h] * (value_ref[rows[c], cols[h]] - starts[c, h] * seen)
    for c, h in each:
        value_of[c, h] = dot(solve_ref[c, h], right_of[c, h]).astype(BF16)
    decay_of, delta_value_of, delta_right_of = {}, {}, {}
    for c, h in each:
        decay_of[c, h] = pair_decay(terms[c][1], terms[c][2], terms[c][3], h)
        delta_value_of[c, h] = dot(
            decay_of[c, h] * grams[c, h // repeat][1], delta_out_ref[rows[c], cols[h]], TN
        )
    both_of, held_of, carry_of = {}, {}, {}
    for c in reversed(range(spans)):
        total = terms[c][6]
        for h in range(heads):
            carry_of[c, h] = carry_ref[h].astype(BF16)
            delta_value_of[c, h] += dot(ends[c, h] * ks[c, h // repeat], carry_of[c, h])
        for h in range(heads):
            delta_right_of[c, h] = dot(solve_ref[c, h], delta_value_of[c, h], TN)
        for h in range(heads):
            q, k = qs[c, h // repeat], ks[c, h // repeat]
            b, s = betas[c, h], starts[c, h]
            delta_right = delta_right_of[c, h]
            delta_value_ref[rows[c], cols[h]] = (b * delta_right).astype(BF16)
            both_of[c, h] = jnp.concatenate(
                [delta_out_ref[rows[c], cols[h]], delta_right.astype(BF16)], axis=0
            )
            carry = carry_ref[h]
            held_of[c, h] = total[:, h : h + 1] * row_sum(
                jnp.sum(state_of[c, h].astype(F32) * carry, axis=0, keepdims=True)
            )
            carry_ref[h] = total[:, h : h + 1] * carry + dot(
                jnp.concatenate([s * q, (-b * s) * k], axis=0), both_of[c, h], TN
            )
    pairs_of = {p: dot(both_of[p], value_of[p], NT) for p in each}
    states_of = {p: dot(both_of[p], state_of[p], NT) for p in each}
    ends_of = {p: ends[p] * dot(value_of[p], carry_of[p], NT) for p in each}
    pair_of, sum_of, tail_of, lower_of = {}, {}, {}, {}
    for c, h in each:
        q, k = qs[c, h // repeat], ks[c, h // repeat]
        key_gram, query_gram = grams[c, h // repeat]
        decay, b, s = decay_of[c, h], betas[c, h], starts[c, h]
        pair_q = decay * pairs_of[c, h][:CHUNK]
        pair_k = jnp.where(strict, (-b) * decay * pairs_of[c, h][CHUNK:], 0.0)
        cross = jnp.where(strict, pair_q * query_gram + pair_k * key_gram, 0.0).astype(BF16)
        pair_of[c, h] = (pair_q.astype(BF16), pair_k.astype(BF16))
        state_q = s * states_of[c, h][:CHUNK]
        state_k = (b * s) * states_of[c, h][CHUNK:]
        states_of[c, h] = (state_q, ends_of[c, h] - state_k)
        sum_of[c, h] = jnp.concatenate(
            [cross, (state_q * q - state_k * k).astype(BF16)], axis=1
        )
        tail_of[c, h] = jnp.concatenate(
            [ends_of[c, h] * k, delta_right_of[c, h] * value_of[c, h].astype(F32)], axis=1
        ).astype(BF16)
        lower_of[c, h] = jnp.sum(cross.astype(F32), axis=0, keepdims=True)
    for c in range(spans):
        for g in range(key_heads):
            q, k = qs[c, g], ks[c, g]
            both = jnp.concatenate([q, k], axis=0)
            delta_q = jnp.zeros((CHUNK, DK), F32)
            delta_k = jnp.zeros((CHUNK, DK), F32)
            for h in range(g * repeat, (g + 1) * repeat):
                pair_q, pair_k = pair_of[c, h]
                delta_q += dot(pair_q, k) + states_of[c, h][0]
                delta_k += (
                    dot(pair_k, k)
                    + dot(jnp.concatenate([pair_q, pair_k], axis=0), both, TN)
                    + states_of[c, h][1]
                )
            delta_q = delta_q * QUERY_SCALE
            unit = q * (1.0 / QUERY_SCALE)
            delta_q = q_inv[c, g] * (delta_q - unit * row_sum(unit * delta_q))
            delta_k = k_inv[c, g] * (delta_k - k * row_sum(k * delta_k))
            at, after = g * DK, (key_heads + g) * DK
            delta_query_key_ref[rows[c], at : at + DK] = delta_q.astype(BF16)
            delta_query_key_ref[rows[c], after : after + DK] = delta_k.astype(BF16)
    for c in range(spans):
        beta, resets = terms[c][0], terms[c][7]
        sums = jnp.zeros((CHUNK, 2 * heads), F32)
        tails = jnp.zeros((CHUNK, 2 * heads), F32)
        tail = jnp.zeros((1, heads), F32)
        for h in range(heads):
            sums += dot(sum_of[c, h], lane == h)
            tails += dot(tail_of[c, h], lane == h + heads * half)
            tail = jnp.where(lane_one == h, held_of[c, h], tail)
        below = [lower_of[c, h] for h in range(heads)]
        if heads % 8:
            below.append(jnp.zeros((-heads % 8, CHUNK), F32))
        below = exact(upper, jnp.concatenate(below, axis=0), NT)[:, :heads]
        ends_sum = tails[:, :heads]
        tail = tail + jnp.sum(ends_sum, axis=0, keepdims=True)
        delta_log = exact(upper, sums[:, :heads] - ends_sum) - below + tail
        reset_col = dot(identity, resets, NT)[:, 0:1]
        delta_log = jnp.where(reset_col == 0.0, delta_log, 0.0)
        logits = decay_beta_ref[rows[c], :heads]
        delta_decay = delta_log * (-scale_ref[...]) * sigmoid(logits)
        delta_beta = tails[:, heads:] * (1.0 - beta)
        rest = jnp.zeros((CHUNK, LANES - 2 * heads), F32)
        delta_query_key_ref[rows[c], 2 * key_heads * DK :] = jnp.concatenate(
            [delta_decay, delta_beta, rest], axis=1
        ).astype(BF16)


def chain_forward_kernel(totals_ref, states_ref):
    devices, heads = totals_ref.shape[0], totals_ref.shape[1]
    for h in range(heads):
        state = jnp.zeros(states_ref.shape[2:], F32)
        for i in range(devices):
            states_ref[i, h] = state.astype(BF16)
            if i < devices - 1:
                step = totals_ref[i, h]
                high = state.astype(BF16)
                low = state - high.astype(F32)
                state = (
                    dot(step[:, :DK], high) + dot(step[:, :DK], low) + step[:, DK:].astype(F32)
                )


def chain_backward_kernel(totals_ref, deltas_ref, states_ref):
    devices, heads = totals_ref.shape[0], totals_ref.shape[1]
    for h in range(heads):
        state = jnp.zeros(states_ref.shape[2:], F32)
        for i in reversed(range(devices)):
            states_ref[i, h] = state.astype(BF16)
            if i > 0:
                step = totals_ref[i, h]
                high = state.astype(BF16)
                low = state - high.astype(F32)
                state = (
                    dot(step[:, :DK], high, TN)
                    + dot(step[:, :DK], low, TN)
                    + deltas_ref[i, h].astype(F32)
                )


PARAMS = pltpu.CompilerParams(
    dimension_semantics=("arbitrary",), vmem_limit_bytes=56 * 1024 * 1024
)
INTERPRET = False


def whole(shape):
    return pl.BlockSpec(shape, lambda c: (0,) * len(shape))


def run_forward(query_key, value, decay_beta, bias, scale, resets):
    tokens, heads = query_key.shape[1], bias.shape[1]
    chunks = tokens // CHUNK
    spans = min(FORWARD_SPANS, chunks)
    step = spans * CHUNK
    key_width, value_width = query_key.shape[2], heads * DV
    return pl.pallas_call(
        forward_kernel,
        grid=(chunks // spans,),
        in_specs=[
            pl.BlockSpec((2, step, key_width), lambda c: (0, c, 0)),
            pl.BlockSpec((step, value_width), lambda c: (c, 0)),
            pl.BlockSpec((step, 2 * heads), lambda c: (c, 0)),
            whole((1, heads)),
            whole((1, heads)),
            pl.BlockSpec((spans, 1, CHUNK), lambda c: (c, 0, 0)),
        ],
        out_specs=[
            pl.BlockSpec((spans, heads, CHUNK, CHUNK), lambda c: (c, 0, 0, 0)),
            pl.BlockSpec((spans, heads, DK, DK + DV), lambda c: (c, 0, 0, 0)),
            pl.BlockSpec((step, value_width), lambda c: (c, 0)),
            pl.BlockSpec((step, value_width), lambda c: (c, 0)),
            whole((heads, DK, DK + DV)),
        ],
        out_shape=[
            jax.ShapeDtypeStruct((chunks, heads, CHUNK, CHUNK), BF16),
            jax.ShapeDtypeStruct((chunks, heads, DK, DK + DV), BF16),
            jax.ShapeDtypeStruct((tokens, value_width), BF16),
            jax.ShapeDtypeStruct((tokens, value_width), F32),
            jax.ShapeDtypeStruct((heads, DK, DK + DV), BF16),
        ],
        scratch_shapes=[pltpu.VMEM((heads, DK, DK + DV), F32)],
        compiler_params=PARAMS,
        interpret=INTERPRET,
        name="forward_blocks",
    )(query_key, value, decay_beta, bias, scale, resets)


def run_output(local, reach, gate, delta_hidden, state_in, gain):
    tokens, value_width = local.shape
    heads = value_width // DV
    chunks = tokens // CHUNK
    block = pl.BlockSpec((CHUNK, value_width), lambda c: (c, 0))
    return pl.pallas_call(
        output_kernel,
        grid=(chunks,),
        in_specs=[
            block,
            block,
            block,
            block,
            whole((heads, DK, DV)),
            whole((1, DV)),
        ],
        out_specs=[block, block, block, whole((heads, DK, DV))],
        out_shape=[
            jax.ShapeDtypeStruct((tokens, value_width), BF16),
            jax.ShapeDtypeStruct((tokens, value_width), BF16),
            jax.ShapeDtypeStruct((tokens, value_width), BF16),
            jax.ShapeDtypeStruct((heads, DK, DV), BF16),
        ],
        scratch_shapes=[pltpu.VMEM((heads, DK, DV), F32)],
        compiler_params=PARAMS,
        interpret=INTERPRET,
        name="gated_norm",
    )(local, reach, gate, delta_hidden, state_in, gain)


def run_backward(
    query_key, value, decay_beta, bias, scale, resets, solve, starts, state_in, delta_out, final
):
    tokens, heads = query_key.shape[1], bias.shape[1]
    chunks = tokens // CHUNK
    spans = min(BACKWARD_SPANS, chunks)
    step = spans * CHUNK
    key_width, value_width = query_key.shape[2], heads * DV
    last = chunks // spans - 1
    return pl.pallas_call(
        backward_kernel,
        grid=(chunks // spans,),
        in_specs=[
            pl.BlockSpec((2, step, key_width), lambda c: (0, last - c, 0)),
            pl.BlockSpec((step, value_width), lambda c: (last - c, 0)),
            pl.BlockSpec((step, 2 * heads), lambda c: (last - c, 0)),
            whole((1, heads)),
            whole((1, heads)),
            pl.BlockSpec((spans, 1, CHUNK), lambda c: (last - c, 0, 0)),
            pl.BlockSpec((spans, heads, CHUNK, CHUNK), lambda c: (last - c, 0, 0, 0)),
            pl.BlockSpec((spans, heads, DK, DK + DV), lambda c: (last - c, 0, 0, 0)),
            whole((heads, DK, DV)),
            pl.BlockSpec((step, value_width), lambda c: (last - c, 0)),
            whole((heads, DK, DV)),
        ],
        out_specs=[
            pl.BlockSpec((step, 2 * key_width + LANES), lambda c: (last - c, 0)),
            pl.BlockSpec((step, value_width), lambda c: (last - c, 0)),
        ],
        out_shape=[
            jax.ShapeDtypeStruct((tokens, 2 * key_width + LANES), BF16),
            jax.ShapeDtypeStruct((tokens, value_width), BF16),
        ],
        scratch_shapes=[pltpu.VMEM((heads, DK, DV), F32)],
        compiler_params=PARAMS,
        interpret=INTERPRET,
        name="backward_blocks",
    )(query_key, value, decay_beta, bias, scale, resets, solve, starts, state_in, delta_out, final)


def spread(array, devices):
    heads, depth, width = array.shape
    if heads >= devices:
        return array.reshape(devices, heads // devices, depth, width)
    cuts = devices // heads
    parts = array.reshape(heads, depth, cuts, width // cuts)
    return jnp.transpose(parts, (0, 2, 1, 3)).reshape(devices, 1, depth, width // cuts)


def gather_parts(parts, heads):
    devices, each, depth, width = parts.shape
    if heads >= devices:
        return parts.reshape(heads, depth, width)
    cuts = devices // heads
    parts = parts.reshape(heads, cuts, depth, width)
    return jnp.transpose(parts, (0, 2, 1, 3)).reshape(heads, depth, cuts * width)


def swap(parts):
    return lax.all_to_all(parts, "ctx", split_axis=0, concat_axis=0, tiled=True)


def spread_totals(totals):
    devices, heads = lax.axis_size("ctx"), totals.shape[0]
    if heads >= devices:
        return spread(totals, devices)
    maps = jnp.repeat(totals[:, :, :DK], devices // heads, axis=0)[:, None]
    return jnp.concatenate([maps, spread(totals[:, :, DK:], devices)], axis=-1)


def run_chain_forward(held):
    return pl.pallas_call(
        chain_forward_kernel,
        out_shape=jax.ShapeDtypeStruct((*held.shape[:3], held.shape[3] - DK), BF16),
        interpret=INTERPRET,
        name="chain_forward",
    )(held)


def run_chain_backward(held, deltas):
    return pl.pallas_call(
        chain_backward_kernel,
        out_shape=jax.ShapeDtypeStruct(deltas.shape, BF16),
        interpret=INTERPRET,
        name="chain_backward",
    )(held, deltas)


def product(spec, a, b):
    return jnp.einsum(spec, a, b, preferred_element_type=F32)


def rows_of(small_weight_ref):
    return jnp.concatenate([small_weight_ref[0].astype(F32), small_weight_ref[1].astype(F32)], axis=0)


def projection_kernel(
    inputs_ref,
    query_key_weight_ref,
    value_weight_ref,
    decay_beta_weight_ref,
    query_key_ref,
    value_ref,
    decay_beta_ref,
):
    inputs = inputs_ref[...]
    query_key_ref[0] = dot(inputs, query_key_weight_ref[0])
    value_ref[...] = dot(inputs, value_weight_ref[0])

    @pl.when(pl.program_id(0) == 0)
    def _():
        decay_beta_ref[...] = dot(inputs, rows_of(decay_beta_weight_ref), NT)


def run_projection(inputs, query_key_weight, value_gate_weight, decay_beta_weight):
    tokens, model = inputs.shape
    key_width, value_width = query_key_weight.shape[2], value_gate_weight.shape[2]
    heads = decay_beta_weight.shape[1]
    steps = 4
    keys, values = 2 * key_width // steps, value_width // steps
    return pl.pallas_call(
        projection_kernel,
        grid=(steps,),
        in_specs=[
            whole((tokens, model)),
            pl.BlockSpec((1, model, keys), lambda j: (j // 2, 0, j % 2)),
            pl.BlockSpec((1, model, values), lambda j: (0, 0, j)),
            whole((2, heads, model)),
        ],
        out_specs=[
            pl.BlockSpec((1, tokens, keys), lambda j: (j // 2, 0, j % 2)),
            pl.BlockSpec((tokens, values), lambda j: (0, j)),
            whole((tokens, 2 * heads)),
        ],
        out_shape=[
            jax.ShapeDtypeStruct((2, tokens, key_width), F32),
            jax.ShapeDtypeStruct((tokens, value_width), F32),
            jax.ShapeDtypeStruct((tokens, 2 * heads), F32),
        ],
        compiler_params=PARAMS,
        interpret=INTERPRET,
        name="projection",
    )(inputs, query_key_weight, value_gate_weight, decay_beta_weight)


def input_gradient_kernel(
    delta_query_key_ref,
    delta_value_ref,
    delta_gate_ref,
    query_key_weight_ref,
    value_gate_weight_ref,
    decay_beta_weight_ref,
    out_ref,
):
    width = query_key_weight_ref.shape[2]
    heads = decay_beta_weight_ref.shape[1]
    keys = jnp.concatenate([query_key_weight_ref[0], query_key_weight_ref[1]], axis=1)
    small = delta_query_key_ref[:, 2 * width : 2 * width + 2 * heads]
    total = dot(delta_gate_ref[...], value_gate_weight_ref[1], NT)
    total += dot(delta_value_ref[...], value_gate_weight_ref[0], NT)
    total += dot(delta_query_key_ref[:, : 2 * width], keys, NT)
    total += dot(small, rows_of(decay_beta_weight_ref))
    out_ref[...] = total.astype(BF16)


def run_input_gradient(
    delta_query_key, delta_value, delta_gate, query_key_weight, value_gate_weight, decay_beta_weight
):
    tokens, model = delta_value.shape[0], query_key_weight.shape[1]
    cut = 512

    def weight(array):
        return pl.BlockSpec((2, cut, array.shape[2]), lambda j: (0, j, 0))

    return pl.pallas_call(
        input_gradient_kernel,
        grid=(model // cut,),
        in_specs=[
            whole(delta_query_key.shape),
            whole(delta_value.shape),
            whole(delta_gate.shape),
            weight(query_key_weight),
            weight(value_gate_weight),
            pl.BlockSpec((2, decay_beta_weight.shape[1], cut), lambda j: (0, 0, j)),
        ],
        out_specs=pl.BlockSpec((tokens, cut), lambda j: (0, j)),
        out_shape=jax.ShapeDtypeStruct((tokens, model), BF16),
        compiler_params=PARAMS,
        interpret=INTERPRET,
        name="input_gradient",
    )(delta_query_key, delta_value, delta_gate, query_key_weight, value_gate_weight, decay_beta_weight)


def together(*arrays):
    return lax.optimization_barrier(arrays)


def exchange(array, distance):
    devices = range(lax.axis_size("ctx"))
    return lax.ppermute(array, "ctx", [(i, i ^ distance) for i in devices])


def block_of(step, place, flip):
    x, y = (place // 2) % 2, place // 4
    core = lax.rem(place + flip, 2)
    across_x, across_y = 1 - step // 2, 1 - lax.rem(step, 2)
    target_x, target_y = lax.rem(x + across_x, 2), lax.rem(y + across_y, 2)
    return target_y * 4 + target_x * 2 + core


def send_kernel(place_ref, left_a_ref, a_ref, left_b_ref, b_ref, a_out_ref, b_out_ref):
    a_out_ref[...] = dot(left_a_ref[...], a_ref[...], TN).astype(BF16)
    b_out_ref[...] = dot(left_b_ref[...], b_ref[...], TN).astype(BF16)


def keep_kernel(
    place_ref, left_a_ref, a_ref, left_b_ref, b_ref, a_arrived_ref, b_arrived_ref, *out_refs
):
    step = pl.program_id(0)
    a = dot(left_a_ref[...], a_ref[...], TN) + a_arrived_ref[...].astype(F32)
    b = dot(left_b_ref[...], b_ref[...], TN) + b_arrived_ref[...].astype(F32)
    for i in range(4):

        @pl.when(step == i)
        def _():
            out_refs[i][...] = a.astype(BF16)
            out_refs[4 + i][...] = b.astype(BF16)


def pair_specs(left_a, a, left_b, b, flip):
    def rows(left):
        return pl.BlockSpec(
            (left.shape[0], left.shape[1] // 8), lambda i, place: (0, block_of(i, place[0], flip))
        )

    def full(delta):
        return pl.BlockSpec(delta.shape, lambda i, place: (0, 0))

    return [rows(left_a), full(a), rows(left_b), full(b)]


def halving_start(place, left_a, a, left_b, b):
    rows = left_a.shape[1] // 8
    return pl.pallas_call(
        send_kernel,
        grid_spec=pltpu.PrefetchScalarGridSpec(
            num_scalar_prefetch=1,
            grid=(4,),
            in_specs=pair_specs(left_a, a, left_b, b, 1),
            out_specs=[
                pl.BlockSpec((rows, delta.shape[1]), lambda i, place: (i, 0)) for delta in (a, b)
            ],
        ),
        out_shape=[
            jax.ShapeDtypeStruct((4 * rows, delta.shape[1]), BF16) for delta in (a, b)
        ],
        compiler_params=PARAMS,
        interpret=INTERPRET,
        name="send_rows",
    )(place, left_a, a, left_b, b)


def halving_keep(place, left_a, a, left_b, b, a_arrived, b_arrived):
    rows = left_a.shape[1] // 8
    return pl.pallas_call(
        keep_kernel,
        grid_spec=pltpu.PrefetchScalarGridSpec(
            num_scalar_prefetch=1,
            grid=(4,),
            in_specs=pair_specs(left_a, a, left_b, b, 0)
            + [pl.BlockSpec((rows, delta.shape[1]), lambda i, place: (i, 0)) for delta in (a, b)],
            out_specs=[
                pl.BlockSpec((rows, delta.shape[1]), lambda i, place: (0, 0))
                for delta in (a, b)
                for _ in range(4)
            ],
        ),
        out_shape=[
            jax.ShapeDtypeStruct((rows, delta.shape[1]), BF16)
            for delta in (a, b)
            for _ in range(4)
        ],
        compiler_params=PARAMS,
        interpret=INTERPRET,
        name="keep_rows",
    )(place, left_a, a, left_b, b, a_arrived, b_arrived)


def summed(a, b):
    return (a.astype(F32) + b.astype(F32)).astype(BF16)


def halving_cross(pieces):
    return exchange(pieces[0], 2), exchange(pieces[4], 4)


def halving_stay(pieces):
    return exchange(pieces[1], 2), exchange(pieces[6], 4)


def halving_last(pieces, arrived):
    a, b = pieces[:4], pieces[4:]
    return exchange(summed(a[2], arrived[0]), 4), exchange(summed(b[1], arrived[1]), 2)


def halving_sum(pieces, arrived, last):
    def total(own, near, far):
        return own.astype(F32) + near.astype(F32) + far.astype(F32)

    return total(pieces[3], arrived[0], last[0]), total(pieces[7], arrived[1], last[1])


def scatter(partial, axis, dimension):
    return lax.psum_scatter(partial.astype(BF16), axis, scatter_dimension=dimension, tiled=True)


def body(
    inputs,
    query_key_weight,
    value_gate_weight,
    decay_beta_weight,
    beta_bias,
    decay_scale,
    norm_gain,
    out_weight,
    boundaries,
    grad_mixed,
):
    tokens, heads = inputs.shape[0], beta_bias.shape[0]
    key_width = query_key_weight.shape[2]
    cubic = lax.axis_size("ctx") == 8
    small_weight = jnp.swapaxes(decay_beta_weight, 1, 2)
    query_key, value, decay_beta = run_projection(
        inputs, query_key_weight, value_gate_weight, small_weight
    )
    bias, scale = beta_bias.reshape(1, heads), decay_scale.reshape(1, heads)
    resets = boundaries.reshape(tokens // CHUNK, 1, CHUNK)
    solve, starts, reach, local, totals = run_forward(
        query_key, value, decay_beta, bias, scale, resets
    )

    held = swap(spread_totals(totals))
    gate = product("td,df->tf", inputs, value_gate_weight[1])
    held, gate = together(held, gate)
    states = swap(run_chain_forward(held))
    delta_hidden = product("td,fd->tf", grad_mixed, out_weight)
    states, delta_hidden = together(states, delta_hidden)
    state_in = gather_parts(states, heads)
    hidden, delta_gate, delta_out, delta_state = run_output(
        local, reach, gate, delta_hidden, state_in, norm_gain.reshape(1, DV)
    )

    deltas = swap(spread(delta_state, lax.axis_size("ctx")))
    partial_out = product("tf,fd->td", hidden, out_weight).astype(BF16)
    deltas, partial_out = together(deltas, partial_out)
    mixed = scatter(partial_out, "head", 1)
    finals = swap(run_chain_backward(held, deltas))
    if cubic:
        place = lax.axis_index("ctx").astype(jnp.int32).reshape(1)
        early = (place, inputs, delta_gate, grad_mixed, hidden)
        sent = halving_start(*early)
        arrived = [exchange(part, 1) for part in sent]
        early_pieces = halving_keep(*early, *arrived)
        finals, early_pieces = together(finals, early_pieces)
        early_arrived = halving_cross(early_pieces)
        early_stay = halving_stay(early_pieces)
    delta_final = gather_parts(finals, heads)
    delta_query_key, delta_value = run_backward(
        query_key,
        value,
        decay_beta,
        bias,
        scale,
        resets,
        solve,
        starts,
        state_in,
        delta_out,
        delta_final,
    )
    if cubic:
        delta_value, early_arrived = together(delta_value, early_arrived)
        early_last = halving_last(early_pieces, early_arrived)
        late = (place, inputs, delta_value, inputs, delta_query_key)
        sent = halving_start(*late)
        sent, early_stay = together(sent, early_stay)
        arrived = [exchange(part, 1) for part in sent]
    grad_rows = run_input_gradient(
        delta_query_key,
        delta_value,
        delta_gate,
        query_key_weight,
        value_gate_weight,
        small_weight,
    )
    if cubic:
        grad_rows, arrived, early_last = together(grad_rows, arrived, early_last)
    grad_inputs = scatter(grad_rows, "head", 1)
    if cubic:
        late_pieces = halving_keep(*late, *arrived)
        late_arrived = halving_cross(late_pieces)
        late_stay = halving_stay(late_pieces)
        late_last = halving_last(late_pieces, late_arrived)
        grad_gate, grad_out = halving_sum(early_pieces, early_stay, early_last)
        grad_out = grad_out.T
        grad_value, packed = halving_sum(late_pieces, late_stay, late_last)
    else:
        grad_gate = scatter(product("td,tf->df", inputs, delta_gate), "ctx", 0).astype(F32)
        grad_out = scatter(product("tf,td->fd", hidden, grad_mixed), "ctx", 1).astype(F32)
        grad_value = scatter(product("td,tf->df", inputs, delta_value), "ctx", 0).astype(F32)
        packed = scatter(product("td,tf->df", inputs, delta_query_key), "ctx", 0).astype(F32)
    rest = packed[:, 2 * key_width :]
    return (
        mixed,
        grad_inputs,
        jnp.stack([packed[:, :key_width], packed[:, key_width : 2 * key_width]]),
        jnp.stack([grad_value, grad_gate]),
        jnp.stack([rest[:, :heads], rest[:, heads : 2 * heads]]),
        grad_out,
    )


def solution(mesh):
    in_specs = (
        P("ctx", None),
        P(None, None, "head"),
        P(None, None, "head"),
        P(None, None, "head"),
        P("head"),
        P("head"),
        P(),
        P("head", None),
        P("ctx"),
        P("ctx", None),
    )
    out_specs = (
        P("ctx", "head"),
        P("ctx", "head"),
        P(None, "ctx", "head"),
        P(None, "ctx", "head"),
        P(None, "ctx", "head"),
        P("head", "ctx"),
    )
    return jax.shard_map(body, mesh=mesh, in_specs=in_specs, out_specs=out_specs, check_vma=False)
```

```python
import functools

import jax
import jax.numpy as jnp
from jax import lax
from jax.experimental import pallas as pl
from jax.experimental.pallas import tpu as pltpu
from jax.sharding import PartitionSpec as P

DK = 128
DV = 128
CHUNK = 128
EPS = 1e-06
QUERY_SCALE = DK ** (-0.5)
LANES = 128
FORWARD_SPANS = 2
BACKWARD_SPANS = 2

F32 = jnp.float32
BF16 = jnp.bfloat16
NN = ((1,), (0,))
NT = ((1,), (1,))
TN = ((0,), (0,))


def dot(a, b, dims=NN):
    return lax.dot_general(
        a.astype(BF16), b.astype(BF16), (dims, ((), ())), preferred_element_type=F32
    )


def exact(a, b, dims=NN):
    return lax.dot_general(
        a, b, (dims, ((), ())), precision=lax.Precision.HIGHEST, preferred_element_type=F32
    )


def softplus(x):
    return jnp.maximum(x, 0.0) + jnp.log1p(jnp.exp(-jnp.abs(x)))


def sigmoid(x):
    return 1.0 / (1.0 + jnp.exp(-x))


def row_sum(x):
    return jnp.sum(x, axis=-1, keepdims=True)


def grid_of(size):
    row = lax.broadcasted_iota(jnp.int32, (size, size), 0)
    col = lax.broadcasted_iota(jnp.int32, (size, size), 1)
    return row, col


def decays(decay_beta, bias_ref, scale_ref, resets):
    row, col = grid_of(CHUNK)
    lower = (row >= col).astype(F32)
    heads = bias_ref.shape[1]
    decay_logit = decay_beta[:, :heads]
    beta = sigmoid(decay_beta[:, heads:] + bias_ref[...])
    log_decay = -scale_ref[...] * softplus(decay_logit)
    resets = jnp.broadcast_to(resets.astype(F32), (8, CHUNK))
    doc_row = dot(resets, lower, NT)[0:1]
    doc_col = dot(lower, resets, NT)[:, 0:1]
    cum_col = exact(lower, log_decay)
    cum_row = exact(log_decay, lower, ((0,), (1,)))
    same = (doc_col == doc_row) & (row >= col)
    start = jnp.where(doc_col == 0.0, jnp.exp(cum_col), 0.0)
    last = CHUNK - 1
    end = jnp.where(
        doc_col == doc_col[last:],
        jnp.exp(jnp.minimum(cum_col[last:] - cum_col, 0.0)),
        0.0,
    )
    return beta, cum_col, cum_row, same, start, end, start[last:], resets


def pair_decay(cum_col, cum_row, same, h):
    gap = jnp.minimum(spread_column(cum_col, h) - cum_row[h : h + 1, :], 0.0)
    return jnp.where(same, jnp.exp(gap), 0.0)


def spread_column(columns, h):
    return jnp.broadcast_to(columns[:, h : h + 1], (columns.shape[0], LANES))


def unit_rows(x):
    inverse = lax.rsqrt(row_sum(x * x) + EPS)
    return x * inverse, inverse


def forward_kernel(
    query_key_ref,
    value_ref,
    decay_beta_ref,
    bias_ref,
    scale_ref,
    resets_ref,
    solve_ref,
    start_ref,
    map_ref,
    local_ref,
    total_ref,
    state_ref,
):
    heads = state_ref.shape[0]
    key_heads = query_key_ref.shape[2] // DK
    repeat = heads // key_heads
    spans = solve_ref.shape[0]
    row, col = grid_of(CHUNK)

    @pl.when(pl.program_id(0) == 0)
    def _():
        first = jnp.concatenate([(row == col).astype(F32), jnp.zeros((DK, DV), F32)], axis=1)
        for h in range(heads):
            state_ref[h] = first

    strict = row > col
    differ = row ^ col
    rows = [slice(c * CHUNK, (c + 1) * CHUNK) for c in range(spans)]
    each = [(c, h) for c in range(spans) for h in range(heads)]
    terms = [
        decays(decay_beta_ref[rows[c]], bias_ref, scale_ref, resets_ref[c]) for c in range(spans)
    ]
    keys, queries = {}, {}
    for c in range(spans):
        for g in range(key_heads):
            cols = slice(g * DK, (g + 1) * DK)
            queries[c, g] = unit_rows(query_key_ref[0, rows[c], cols])[0] * QUERY_SCALE
            keys[c, g] = unit_rows(query_key_ref[1, rows[c], cols])[0]
    grams = {p: (dot(keys[p], keys[p], NT), dot(queries[p], keys[p], NT)) for p in keys}
    scores, systems, betas, starts = {}, {}, {}, {}
    for c, h in each:
        beta, cum_col, cum_row, same, start = terms[c][:5]
        betas[c, h] = spread_column(beta, h)
        starts[c, h] = spread_column(start, h)
        decay = pair_decay(cum_col, cum_row, same, h)
        key_gram, query_gram = grams[c, h // repeat]
        scores[c, h] = (decay * query_gram).astype(BF16)
        systems[c, h] = jnp.where(strict, betas[c, h] * decay * key_gram, 0.0)
    identity = (row == col).astype(F32)
    inverse = {
        p: (identity - jnp.where(differ == 1, systems[p], 0.0)).astype(BF16) for p in each
    }
    level = 1
    while (1 << level) < CHUNK:
        here = (differ >> level) == 1
        inner = {
            p: dot(jnp.where(here, systems[p], 0.0), inverse[p]).astype(BF16) for p in each
        }
        inverse = {p: inverse[p] - dot(inverse[p], inner[p]).astype(BF16) for p in each}
        level += 1
    weights = {}
    for c, h in each:
        k = keys[c, h // repeat]
        v = value_ref[rows[c], h * DV : (h + 1) * DV]
        b = betas[c, h]
        right = jnp.concatenate([(b * starts[c, h]) * k, b * v], axis=1)
        weights[c, h] = dot(inverse[c, h], right)
        solve_ref[c, h] = inverse[c, h]
    for c in range(spans):
        end, total = terms[c][5:7]
        values = []
        for h in range(heads):
            state = state_ref[h].astype(BF16)
            start_ref[c, h] = state
            solved = weights[c, h]
            base = jnp.concatenate([jnp.zeros((CHUNK, DK), F32), solved[:, DK:]], axis=1)
            values.append((base - dot(solved[:, :DK], state)).astype(BF16))
        for h in range(heads):
            k, q = keys[c, h // repeat], queries[c, h // repeat]
            state = state_ref[h]
            out = dot(starts[c, h] * q, state) + dot(scores[c, h], values[h])
            map_ref[rows[c], h * DK : (h + 1) * DK] = out[:, :DK].astype(BF16)
            local_ref[rows[c], h * DV : (h + 1) * DV] = out[:, DK:]
            state = total[:, h : h + 1] * state + dot(spread_column(end, h) * k, values[h], TN)
            state_ref[h] = state
            total_ref[h] = state.astype(BF16)


def output_kernel(
    local_ref,
    map_ref,
    gate_ref,
    delta_ref,
    state_ref,
    gain_ref,
    hidden_ref,
    delta_gate_ref,
    delta_out_ref,
    delta_state_ref,
    total_ref,
):
    heads = state_ref.shape[0]
    gain = gain_ref[...]

    @pl.when(pl.program_id(0) == 0)
    def _():
        total_ref[...] = jnp.zeros_like(total_ref)

    outs, deltas = [], []
    for h in range(heads):
        cols = slice(h * DV, (h + 1) * DV)
        outs.append(local_ref[:, cols] + dot(map_ref[:, cols], state_ref[h]))
    for h in range(heads):
        cols = slice(h * DV, (h + 1) * DV)
        out = outs[h]
        gate = gate_ref[:, cols].astype(F32)
        delta = delta_ref[:, cols].astype(F32)
        scale = lax.rsqrt(row_sum(out * out) * (1.0 / DV) + EPS)
        normed = out * scale
        share = sigmoid(gate)
        silu = gate * share
        scaled = normed * gain
        hidden_ref[:, cols] = (scaled * silu).astype(BF16)
        delta_gate_ref[:, cols] = (
            delta * scaled * (share * (1.0 + gate * (1.0 - share)))
        ).astype(BF16)
        delta_normed = delta * gain * silu
        delta_out = scale * (
            delta_normed - normed * (row_sum(normed * delta_normed) * (1.0 / DV))
        )
        delta_out = delta_out.astype(BF16)
        delta_out_ref[:, cols] = delta_out
        deltas.append(delta_out)
    for h in range(heads):
        cols = slice(h * DV, (h + 1) * DV)
        part = total_ref[h] + dot(map_ref[:, cols], deltas[h], TN)
        total_ref[h] = part
        delta_state_ref[h] = part.astype(BF16)


def backward_kernel(
    query_key_ref,
    value_ref,
    decay_beta_ref,
    bias_ref,
    scale_ref,
    resets_ref,
    solve_ref,
    start_ref,
    state_in_ref,
    delta_out_ref,
    delta_final_ref,
    delta_query_key_ref,
    delta_value_ref,
    carry_ref,
):
    heads = carry_ref.shape[0]
    key_heads = query_key_ref.shape[2] // DK
    repeat = heads // key_heads
    spans = solve_ref.shape[0]
    row, col = grid_of(CHUNK)

    @pl.when(pl.program_id(0) == 0)
    def _():
        carry_ref[...] = delta_final_ref[...].astype(F32)

    strict = row > col
    upper = (row <= col).astype(F32)
    identity = (row == col).astype(F32)
    rows = [slice(c * CHUNK, (c + 1) * CHUNK) for c in range(spans)]
    cols = [slice(h * DV, (h + 1) * DV) for h in range(heads)]
    each = [(c, h) for c in reversed(range(spans)) for h in range(heads)]
    terms = [
        decays(decay_beta_ref[rows[c]], bias_ref, scale_ref, resets_ref[c]) for c in range(spans)
    ]
    half = lax.broadcasted_iota(jnp.int32, (2 * DK, 2 * heads), 0) // DK
    lane = lax.broadcasted_iota(jnp.int32, (2 * DK, 2 * heads), 1)
    lane_one = lax.broadcasted_iota(jnp.int32, (1, heads), 1)
    qs, ks, q_inv, k_inv = {}, {}, {}, {}
    for c in range(spans):
        for g in range(key_heads):
            at = slice(g * DK, (g + 1) * DK)
            q, q_inv[c, g] = unit_rows(query_key_ref[0, rows[c], at])
            qs[c, g] = q * QUERY_SCALE
            ks[c, g], k_inv[c, g] = unit_rows(query_key_ref[1, rows[c], at])
    grams = {p: (dot(ks[p], ks[p], NT), dot(qs[p], ks[p], NT)) for p in ks}
    state_of, value_of, right_of = {}, {}, {}
    betas, starts, ends = {}, {}, {}
    for c, h in each:
        before = start_ref[c, h]
        state = dot(before[:, :DK], state_in_ref[h]) + before[:, DK:].astype(F32)
        state_of[c, h] = state.astype(BF16)
    for c, h in each:
        beta, start, end = terms[c][0], terms[c][4], terms[c][5]
        seen = dot(ks[c, h // repeat], state_of[c, h])
        betas[c, h] = spread_column(beta, h)
        starts[c, h] = spread_column(start, h)
        ends[c, h] = spread_column(end, h)
        right_of[c, h] = betas[c, h] * (value_ref[rows[c], cols[h]] - starts[c, h] * seen)
    for c, h in each:
        value_of[c, h] = dot(solve_ref[c, h], right_of[c, h]).astype(BF16)
    decay_of, delta_value_of, delta_right_of = {}, {}, {}
    for c, h in each:
        decay_of[c, h] = pair_decay(terms[c][1], terms[c][2], terms[c][3], h)
        delta_value_of[c, h] = dot(
            decay_of[c, h] * grams[c, h // repeat][1], delta_out_ref[rows[c], cols[h]], TN
        )
    both_of, held_of, carry_of = {}, {}, {}
    for c in reversed(range(spans)):
        total = terms[c][6]
        for h in range(heads):
            carry_of[c, h] = carry_ref[h].astype(BF16)
            delta_value_of[c, h] += dot(ends[c, h] * ks[c, h // repeat], carry_of[c, h])
        for h in range(heads):
            delta_right_of[c, h] = dot(solve_ref[c, h], delta_value_of[c, h], TN)
        for h in range(heads):
            q, k = qs[c, h // repeat], ks[c, h // repeat]
            b, s = betas[c, h], starts[c, h]
            delta_right = delta_right_of[c, h]
            delta_value_ref[rows[c], cols[h]] = (b * delta_right).astype(BF16)
            both_of[c, h] = jnp.concatenate(
                [delta_out_ref[rows[c], cols[h]], delta_right.astype(BF16)], axis=0
            )
            carry = carry_ref[h]
            held_of[c, h] = total[:, h : h + 1] * row_sum(
                jnp.sum(state_of[c, h].astype(F32) * carry, axis=0, keepdims=True)
            )
            carry_ref[h] = total[:, h : h + 1] * carry + dot(
                jnp.concatenate([s * q, (-b * s) * k], axis=0), both_of[c, h], TN
            )
    pairs_of = {p: dot(both_of[p], value_of[p], NT) for p in each}
    states_of = {p: dot(both_of[p], state_of[p], NT) for p in each}
    ends_of = {p: ends[p] * dot(value_of[p], carry_of[p], NT) for p in each}
    pair_of, sum_of, tail_of, lower_of = {}, {}, {}, {}
    for c, h in each:
        q, k = qs[c, h // repeat], ks[c, h // repeat]
        key_gram, query_gram = grams[c, h // repeat]
        decay, b, s = decay_of[c, h], betas[c, h], starts[c, h]
        pair_q = decay * pairs_of[c, h][:CHUNK]
        pair_k = jnp.where(strict, (-b) * decay * pairs_of[c, h][CHUNK:], 0.0)
        cross = jnp.where(strict, pair_q * query_gram + pair_k * key_gram, 0.0).astype(BF16)
        pair_of[c, h] = (pair_q.astype(BF16), pair_k.astype(BF16))
        state_q = s * states_of[c, h][:CHUNK]
        state_k = (b * s) * states_of[c, h][CHUNK:]
        states_of[c, h] = (state_q, ends_of[c, h] - state_k)
        sum_of[c, h] = jnp.concatenate(
            [cross, (state_q * q - state_k * k).astype(BF16)], axis=1
        )
        tail_of[c, h] = jnp.concatenate(
            [ends_of[c, h] * k, delta_right_of[c, h] * value_of[c, h].astype(F32)], axis=1
        ).astype(BF16)
        lower_of[c, h] = jnp.sum(cross.astype(F32), axis=0, keepdims=True)
    for c in range(spans):
        for g in range(key_heads):
            q, k = qs[c, g], ks[c, g]
            both = jnp.concatenate([q, k], axis=0)
            delta_q = jnp.zeros((CHUNK, DK), F32)
            delta_k = jnp.zeros((CHUNK, DK), F32)
            for h in range(g * repeat, (g + 1) * repeat):
                pair_q, pair_k = pair_of[c, h]
                delta_q += dot(pair_q, k) + states_of[c, h][0]
                delta_k += (
                    dot(pair_k, k)
                    + dot(jnp.concatenate([pair_q, pair_k], axis=0), both, TN)
                    + states_of[c, h][1]
                )
            delta_q = delta_q * QUERY_SCALE
            unit = q * (1.0 / QUERY_SCALE)
            delta_q = q_inv[c, g] * (delta_q - unit * row_sum(unit * delta_q))
            delta_k = k_inv[c, g] * (delta_k - k * row_sum(k * delta_k))
            at, after = g * DK, (key_heads + g) * DK
            delta_query_key_ref[rows[c], at : at + DK] = delta_q.astype(BF16)
            delta_query_key_ref[rows[c], after : after + DK] = delta_k.astype(BF16)
    for c in range(spans):
        beta, resets = terms[c][0], terms[c][7]
        sums = jnp.zeros((CHUNK, 2 * heads), F32)
        tails = jnp.zeros((CHUNK, 2 * heads), F32)
        tail = jnp.zeros((1, heads), F32)
        for h in range(heads):
            sums += dot(sum_of[c, h], lane == h)
            tails += dot(tail_of[c, h], lane == h + heads * half)
            tail = jnp.where(lane_one == h, held_of[c, h], tail)
        below = [lower_of[c, h] for h in range(heads)]
        if heads % 8:
            below.append(jnp.zeros((-heads % 8, CHUNK), F32))
        below = exact(upper, jnp.concatenate(below, axis=0), NT)[:, :heads]
        ends_sum = tails[:, :heads]
        tail = tail + jnp.sum(ends_sum, axis=0, keepdims=True)
        delta_log = exact(upper, sums[:, :heads] - ends_sum) - below + tail
        reset_col = dot(identity, resets, NT)[:, 0:1]
        delta_log = jnp.where(reset_col == 0.0, delta_log, 0.0)
        logits = decay_beta_ref[rows[c], :heads]
        delta_decay = delta_log * (-scale_ref[...]) * sigmoid(logits)
        delta_beta = tails[:, heads:] * (1.0 - beta)
        rest = jnp.zeros((CHUNK, LANES - 2 * heads), F32)
        delta_query_key_ref[rows[c], 2 * key_heads * DK :] = jnp.concatenate(
            [delta_decay, delta_beta, rest], axis=1
        ).astype(BF16)


def chain_forward_kernel(totals_ref, states_ref):
    devices, heads = totals_ref.shape[0], totals_ref.shape[1]
    for h in range(heads):
        state = jnp.zeros(states_ref.shape[2:], F32)
        for i in range(devices):
            states_ref[i, h] = state.astype(BF16)
            if i < devices - 1:
                step = totals_ref[i, h]
                high = state.astype(BF16)
                low = state - high.astype(F32)
                state = (
                    dot(step[:, :DK], high) + dot(step[:, :DK], low) + step[:, DK:].astype(F32)
                )


def chain_backward_kernel(totals_ref, deltas_ref, states_ref):
    devices, heads = totals_ref.shape[0], totals_ref.shape[1]
    for h in range(heads):
        state = jnp.zeros(states_ref.shape[2:], F32)
        for i in reversed(range(devices)):
            states_ref[i, h] = state.astype(BF16)
            if i > 0:
                step = totals_ref[i, h]
                high = state.astype(BF16)
                low = state - high.astype(F32)
                state = (
                    dot(step[:, :DK], high, TN)
                    + dot(step[:, :DK], low, TN)
                    + deltas_ref[i, h].astype(F32)
                )


PARAMS = pltpu.CompilerParams(
    dimension_semantics=("arbitrary",), vmem_limit_bytes=56 * 1024 * 1024
)
INTERPRET = False


def whole(shape):
    return pl.BlockSpec(shape, lambda c: (0,) * len(shape))


def run_forward(query_key, value, decay_beta, bias, scale, resets):
    tokens, heads = query_key.shape[1], bias.shape[1]
    chunks = tokens // CHUNK
    spans = min(FORWARD_SPANS, chunks)
    step = spans * CHUNK
    key_width, value_width = query_key.shape[2], heads * DV
    return pl.pallas_call(
        forward_kernel,
        grid=(chunks // spans,),
        in_specs=[
            pl.BlockSpec((2, step, key_width), lambda c: (0, c, 0)),
            pl.BlockSpec((step, value_width), lambda c: (c, 0)),
            pl.BlockSpec((step, 2 * heads), lambda c: (c, 0)),
            whole((1, heads)),
            whole((1, heads)),
            pl.BlockSpec((spans, 1, CHUNK), lambda c: (c, 0, 0)),
        ],
        out_specs=[
            pl.BlockSpec((spans, heads, CHUNK, CHUNK), lambda c: (c, 0, 0, 0)),
            pl.BlockSpec((spans, heads, DK, DK + DV), lambda c: (c, 0, 0, 0)),
            pl.BlockSpec((step, value_width), lambda c: (c, 0)),
            pl.BlockSpec((step, value_width), lambda c: (c, 0)),
            whole((heads, DK, DK + DV)),
        ],
        out_shape=[
            jax.ShapeDtypeStruct((chunks, heads, CHUNK, CHUNK), BF16),
            jax.ShapeDtypeStruct((chunks, heads, DK, DK + DV), BF16),
            jax.ShapeDtypeStruct((tokens, value_width), BF16),
            jax.ShapeDtypeStruct((tokens, value_width), F32),
            jax.ShapeDtypeStruct((heads, DK, DK + DV), BF16),
        ],
        scratch_shapes=[pltpu.VMEM((heads, DK, DK + DV), F32)],
        compiler_params=PARAMS,
        interpret=INTERPRET,
        name="forward_blocks",
    )(query_key, value, decay_beta, bias, scale, resets)


def run_output(local, reach, gate, delta_hidden, state_in, gain):
    tokens, value_width = local.shape
    heads = value_width // DV
    chunks = tokens // CHUNK
    block = pl.BlockSpec((CHUNK, value_width), lambda c: (c, 0))
    return pl.pallas_call(
        output_kernel,
        grid=(chunks,),
        in_specs=[
            block,
            block,
            block,
            block,
            whole((heads, DK, DV)),
            whole((1, DV)),
        ],
        out_specs=[block, block, block, whole((heads, DK, DV))],
        out_shape=[
            jax.ShapeDtypeStruct((tokens, value_width), BF16),
            jax.ShapeDtypeStruct((tokens, value_width), BF16),
            jax.ShapeDtypeStruct((tokens, value_width), BF16),
            jax.ShapeDtypeStruct((heads, DK, DV), BF16),
        ],
        scratch_shapes=[pltpu.VMEM((heads, DK, DV), F32)],
        compiler_params=PARAMS,
        interpret=INTERPRET,
        name="gated_norm",
    )(local, reach, gate, delta_hidden, state_in, gain)


def run_backward(
    query_key, value, decay_beta, bias, scale, resets, solve, starts, state_in, delta_out, final
):
    tokens, heads = query_key.shape[1], bias.shape[1]
    chunks = tokens // CHUNK
    spans = min(BACKWARD_SPANS, chunks)
    step = spans * CHUNK
    key_width, value_width = query_key.shape[2], heads * DV
    last = chunks // spans - 1
    return pl.pallas_call(
        backward_kernel,
        grid=(chunks // spans,),
        in_specs=[
            pl.BlockSpec((2, step, key_width), lambda c: (0, last - c, 0)),
            pl.BlockSpec((step, value_width), lambda c: (last - c, 0)),
            pl.BlockSpec((step, 2 * heads), lambda c: (last - c, 0)),
            whole((1, heads)),
            whole((1, heads)),
            pl.BlockSpec((spans, 1, CHUNK), lambda c: (last - c, 0, 0)),
            pl.BlockSpec((spans, heads, CHUNK, CHUNK), lambda c: (last - c, 0, 0, 0)),
            pl.BlockSpec((spans, heads, DK, DK + DV), lambda c: (last - c, 0, 0, 0)),
            whole((heads, DK, DV)),
            pl.BlockSpec((step, value_width), lambda c: (last - c, 0)),
            whole((heads, DK, DV)),
        ],
        out_specs=[
            pl.BlockSpec((step, 2 * key_width + LANES), lambda c: (last - c, 0)),
            pl.BlockSpec((step, value_width), lambda c: (last - c, 0)),
        ],
        out_shape=[
            jax.ShapeDtypeStruct((tokens, 2 * key_width + LANES), BF16),
            jax.ShapeDtypeStruct((tokens, value_width), BF16),
        ],
        scratch_shapes=[pltpu.VMEM((heads, DK, DV), F32)],
        compiler_params=PARAMS,
        interpret=INTERPRET,
        name="backward_blocks",
    )(query_key, value, decay_beta, bias, scale, resets, solve, starts, state_in, delta_out, final)


def spread(array, devices):
    heads, depth, width = array.shape
    if heads >= devices:
        return array.reshape(devices, heads // devices, depth, width)
    cuts = devices // heads
    parts = array.reshape(heads, depth, cuts, width // cuts)
    return jnp.transpose(parts, (0, 2, 1, 3)).reshape(devices, 1, depth, width // cuts)


def gather_parts(parts, heads):
    devices, each, depth, width = parts.shape
    if heads >= devices:
        return parts.reshape(heads, depth, width)
    cuts = devices // heads
    parts = parts.reshape(heads, cuts, depth, width)
    return jnp.transpose(parts, (0, 2, 1, 3)).reshape(heads, depth, cuts * width)


def swap(parts):
    return lax.all_to_all(parts, "ctx", split_axis=0, concat_axis=0, tiled=True)


def spread_totals(totals):
    devices, heads = lax.axis_size("ctx"), totals.shape[0]
    if heads >= devices:
        return spread(totals, devices)
    maps = jnp.repeat(totals[:, :, :DK], devices // heads, axis=0)[:, None]
    return jnp.concatenate([maps, spread(totals[:, :, DK:], devices)], axis=-1)


def run_chain_forward(held):
    return pl.pallas_call(
        chain_forward_kernel,
        out_shape=jax.ShapeDtypeStruct((*held.shape[:3], held.shape[3] - DK), BF16),
        interpret=INTERPRET,
        name="chain_forward",
    )(held)


def run_chain_backward(held, deltas):
    return pl.pallas_call(
        chain_backward_kernel,
        out_shape=jax.ShapeDtypeStruct(deltas.shape, BF16),
        interpret=INTERPRET,
        name="chain_backward",
    )(held, deltas)


def product(spec, a, b):
    return jnp.einsum(spec, a, b, preferred_element_type=F32)


def rows_of(small_weight_ref):
    return jnp.concatenate([small_weight_ref[0].astype(F32), small_weight_ref[1].astype(F32)], axis=0)


def projection_kernel(
    inputs_ref,
    query_key_weight_ref,
    value_weight_ref,
    decay_beta_weight_ref,
    query_key_ref,
    value_ref,
    decay_beta_ref,
):
    inputs = inputs_ref[...]
    query_key_ref[0] = dot(inputs, query_key_weight_ref[0])
    value_ref[...] = dot(inputs, value_weight_ref[0])

    @pl.when(pl.program_id(0) == 0)
    def _():
        decay_beta_ref[...] = dot(inputs, rows_of(decay_beta_weight_ref), NT)


def run_projection(inputs, query_key_weight, value_gate_weight, decay_beta_weight):
    tokens, model = inputs.shape
    key_width, value_width = query_key_weight.shape[2], value_gate_weight.shape[2]
    heads = decay_beta_weight.shape[1]
    steps = 4
    keys, values = 2 * key_width // steps, value_width // steps
    return pl.pallas_call(
        projection_kernel,
        grid=(steps,),
        in_specs=[
            whole((tokens, model)),
            pl.BlockSpec((1, model, keys), lambda j: (j // 2, 0, j % 2)),
            pl.BlockSpec((1, model, values), lambda j: (0, 0, j)),
            whole((2, heads, model)),
        ],
        out_specs=[
            pl.BlockSpec((1, tokens, keys), lambda j: (j // 2, 0, j % 2)),
            pl.BlockSpec((tokens, values), lambda j: (0, j)),
            whole((tokens, 2 * heads)),
        ],
        out_shape=[
            jax.ShapeDtypeStruct((2, tokens, key_width), F32),
            jax.ShapeDtypeStruct((tokens, value_width), F32),
            jax.ShapeDtypeStruct((tokens, 2 * heads), F32),
        ],
        compiler_params=PARAMS,
        interpret=INTERPRET,
        name="projection",
    )(inputs, query_key_weight, value_gate_weight, decay_beta_weight)


def input_gradient_kernel(
    delta_query_key_ref,
    delta_value_ref,
    delta_gate_ref,
    query_key_weight_ref,
    value_gate_weight_ref,
    decay_beta_weight_ref,
    out_ref,
):
    width = query_key_weight_ref.shape[2]
    heads = decay_beta_weight_ref.shape[1]
    keys = jnp.concatenate([query_key_weight_ref[0], query_key_weight_ref[1]], axis=1)
    small = delta_query_key_ref[:, 2 * width : 2 * width + 2 * heads]
    total = dot(delta_gate_ref[...], value_gate_weight_ref[1], NT)
    total += dot(delta_value_ref[...], value_gate_weight_ref[0], NT)
    total += dot(delta_query_key_ref[:, : 2 * width], keys, NT)
    total += dot(small, rows_of(decay_beta_weight_ref))
    out_ref[...] = total.astype(BF16)


def run_input_gradient(
    delta_query_key, delta_value, delta_gate, query_key_weight, value_gate_weight, decay_beta_weight
):
    tokens, model = delta_value.shape[0], query_key_weight.shape[1]
    cut = 512

    def weight(array):
        return pl.BlockSpec((2, cut, array.shape[2]), lambda j: (0, j, 0))

    return pl.pallas_call(
        input_gradient_kernel,
        grid=(model // cut,),
        in_specs=[
            whole(delta_query_key.shape),
            whole(delta_value.shape),
            whole(delta_gate.shape),
            weight(query_key_weight),
            weight(value_gate_weight),
            pl.BlockSpec((2, decay_beta_weight.shape[1], cut), lambda j: (0, 0, j)),
        ],
        out_specs=pl.BlockSpec((tokens, cut), lambda j: (0, j)),
        out_shape=jax.ShapeDtypeStruct((tokens, model), BF16),
        compiler_params=PARAMS,
        interpret=INTERPRET,
        name="input_gradient",
    )(delta_query_key, delta_value, delta_gate, query_key_weight, value_gate_weight, decay_beta_weight)


def together(*arrays):
    return lax.optimization_barrier(arrays)


def exchange(array, distance):
    devices = range(lax.axis_size("ctx"))
    return lax.ppermute(array, "ctx", [(i, i ^ distance) for i in devices])


def block_of(step, place, flip):
    x, y = (place // 2) % 2, place // 4
    core = lax.rem(place + flip, 2)
    across_x, across_y = 1 - step // 2, 1 - lax.rem(step, 2)
    target_x, target_y = lax.rem(x + across_x, 2), lax.rem(y + across_y, 2)
    return target_y * 4 + target_x * 2 + core


def send_kernel(place_ref, left_a_ref, a_ref, left_b_ref, b_ref, a_out_ref, b_out_ref):
    a_out_ref[...] = dot(left_a_ref[...], a_ref[...], TN).astype(BF16)
    b_out_ref[...] = dot(left_b_ref[...], b_ref[...], TN).astype(BF16)


def keep_kernel(
    place_ref, left_a_ref, a_ref, left_b_ref, b_ref, a_arrived_ref, b_arrived_ref, *out_refs
):
    step = pl.program_id(0)
    a = dot(left_a_ref[...], a_ref[...], TN) + a_arrived_ref[...].astype(F32)
    b = dot(left_b_ref[...], b_ref[...], TN) + b_arrived_ref[...].astype(F32)
    for i in range(4):

        @pl.when(step == i)
        def _():
            out_refs[i][...] = a.astype(BF16)
            out_refs[4 + i][...] = b.astype(BF16)


def pair_specs(left_a, a, left_b, b, flip):
    def rows(left):
        return pl.BlockSpec(
            (left.shape[0], left.shape[1] // 8), lambda i, place: (0, block_of(i, place[0], flip))
        )

    def full(delta):
        return pl.BlockSpec(delta.shape, lambda i, place: (0, 0))

    return [rows(left_a), full(a), rows(left_b), full(b)]


def halving_start(place, left_a, a, left_b, b):
    rows = left_a.shape[1] // 8
    return pl.pallas_call(
        send_kernel,
        grid_spec=pltpu.PrefetchScalarGridSpec(
            num_scalar_prefetch=1,
            grid=(4,),
            in_specs=pair_specs(left_a, a, left_b, b, 1),
            out_specs=[
                pl.BlockSpec((rows, delta.shape[1]), lambda i, place: (i, 0)) for delta in (a, b)
            ],
        ),
        out_shape=[
            jax.ShapeDtypeStruct((4 * rows, delta.shape[1]), BF16) for delta in (a, b)
        ],
        compiler_params=PARAMS,
        interpret=INTERPRET,
        name="send_rows",
    )(place, left_a, a, left_b, b)


def halving_keep(place, left_a, a, left_b, b, a_arrived, b_arrived):
    rows = left_a.shape[1] // 8
    return pl.pallas_call(
        keep_kernel,
        grid_spec=pltpu.PrefetchScalarGridSpec(
            num_scalar_prefetch=1,
            grid=(4,),
            in_specs=pair_specs(left_a, a, left_b, b, 0)
            + [pl.BlockSpec((rows, delta.shape[1]), lambda i, place: (i, 0)) for delta in (a, b)],
            out_specs=[
                pl.BlockSpec((rows, delta.shape[1]), lambda i, place: (0, 0))
                for delta in (a, b)
                for _ in range(4)
            ],
        ),
        out_shape=[
            jax.ShapeDtypeStruct((rows, delta.shape[1]), BF16)
            for delta in (a, b)
            for _ in range(4)
        ],
        compiler_params=PARAMS,
        interpret=INTERPRET,
        name="keep_rows",
    )(place, left_a, a, left_b, b, a_arrived, b_arrived)


def summed(a, b):
    return (a.astype(F32) + b.astype(F32)).astype(BF16)


def halving_cross(pieces):
    return exchange(pieces[0], 2), exchange(pieces[4], 4)


def halving_stay(pieces):
    return exchange(pieces[1], 2), exchange(pieces[6], 4)


def halving_last(pieces, arrived):
    a, b = pieces[:4], pieces[4:]
    return exchange(summed(a[2], arrived[0]), 4), exchange(summed(b[1], arrived[1]), 2)


def halving_terms(pieces, stay, last):
    return (pieces[3], stay[0], last[0]), (pieces[7], stay[1], last[1])


def finish_kernel(key_width, heads, *refs):
    def total(*terms):
        return sum(term[...].astype(F32) for term in terms)

    query_key_ref, value_gate_ref, decay_beta_ref = refs[7:]
    value_gate_ref[0] = total(*refs[0:2])
    value_gate_ref[1] = total(*refs[2:5])
    packed = total(*refs[5:7])
    query_key_ref[0] = packed[:, :key_width]
    query_key_ref[1] = packed[:, key_width : 2 * key_width]
    small = packed[:, 2 * key_width :].T
    decay_beta_ref[0] = small[:heads]
    decay_beta_ref[1] = small[heads : 2 * heads]


def run_finish(key_width, heads, value, gate, packed):
    rows, width = value[0].shape
    step = 128

    def block(array):
        return pl.BlockSpec((step, array.shape[1]), lambda i: (i, 0))

    def pair(size):
        return pl.BlockSpec((2, step, size), lambda i: (0, i, 0))

    terms = [*value, *gate, *packed]
    return pl.pallas_call(
        functools.partial(finish_kernel, key_width, heads),
        grid=(rows // step,),
        in_specs=[block(term) for term in terms],
        out_specs=[
            pair(key_width),
            pair(width),
            pl.BlockSpec((2, heads, step), lambda i: (0, 0, i)),
        ],
        out_shape=[
            jax.ShapeDtypeStruct((2, rows, key_width), F32),
            jax.ShapeDtypeStruct((2, rows, width), F32),
            jax.ShapeDtypeStruct((2, heads, rows), F32),
        ],
        compiler_params=PARAMS,
        interpret=INTERPRET,
        name="finish",
    )(*terms)


def scatter(partial, axis, dimension):
    return lax.psum_scatter(partial.astype(BF16), axis, scatter_dimension=dimension, tiled=True)


def body(
    inputs,
    query_key_weight,
    value_gate_weight,
    decay_beta_weight,
    beta_bias,
    decay_scale,
    norm_gain,
    out_weight,
    boundaries,
    grad_mixed,
):
    tokens, heads = inputs.shape[0], beta_bias.shape[0]
    key_width = query_key_weight.shape[2]
    cubic = lax.axis_size("ctx") == 8
    small_weight = jnp.swapaxes(decay_beta_weight, 1, 2)
    query_key, value, decay_beta = run_projection(
        inputs, query_key_weight, value_gate_weight, small_weight
    )
    bias, scale = beta_bias.reshape(1, heads), decay_scale.reshape(1, heads)
    resets = boundaries.reshape(tokens // CHUNK, 1, CHUNK)
    solve, starts, reach, local, totals = run_forward(
        query_key, value, decay_beta, bias, scale, resets
    )

    held = swap(spread_totals(totals))
    gate = product("td,df->tf", inputs, value_gate_weight[1]).astype(BF16)
    held, gate = together(held, gate)
    states = swap(run_chain_forward(held))
    delta_hidden = product("td,fd->tf", grad_mixed, out_weight).astype(BF16)
    states, delta_hidden = together(states, delta_hidden)
    state_in = gather_parts(states, heads)
    hidden, delta_gate, delta_out, delta_state = run_output(
        local, reach, gate, delta_hidden, state_in, norm_gain.reshape(1, DV)
    )

    deltas = swap(spread(delta_state, lax.axis_size("ctx")))
    partial_out = product("tf,fd->td", hidden, out_weight).astype(BF16)
    deltas, partial_out = together(deltas, partial_out)
    mixed = scatter(partial_out, "head", 1)
    finals = swap(run_chain_backward(held, deltas))
    if cubic:
        place = lax.axis_index("ctx").astype(jnp.int32).reshape(1)
        early = (place, inputs, delta_gate, grad_mixed, hidden)
        sent = halving_start(*early)
        arrived = [exchange(part, 1) for part in sent]
        early_pieces = halving_keep(*early, *arrived)
        finals, early_pieces = together(finals, early_pieces)
        early_arrived = halving_cross(early_pieces)
        early_stay = halving_stay(early_pieces)
    delta_final = gather_parts(finals, heads)
    delta_query_key, delta_value = run_backward(
        query_key,
        value,
        decay_beta,
        bias,
        scale,
        resets,
        solve,
        starts,
        state_in,
        delta_out,
        delta_final,
    )
    if cubic:
        delta_value, early_arrived = together(delta_value, early_arrived)
        early_last = halving_last(early_pieces, early_arrived)
        late = (place, inputs, delta_value, inputs, delta_query_key)
        sent = halving_start(*late)
        sent, early_stay = together(sent, early_stay)
        arrived = [exchange(part, 1) for part in sent]
    grad_rows = run_input_gradient(
        delta_query_key,
        delta_value,
        delta_gate,
        query_key_weight,
        value_gate_weight,
        small_weight,
    )
    if cubic:
        grad_rows, arrived, early_last = together(grad_rows, arrived, early_last)
    grad_inputs = scatter(grad_rows, "head", 1)
    if cubic:
        late_pieces = halving_keep(*late, *arrived)
        late_arrived = halving_cross(late_pieces)
        late_stay = halving_stay(late_pieces)
        late_last = halving_last(late_pieces, late_arrived)
        gate_terms, out_terms = halving_terms(early_pieces, early_stay, early_last)
        value_terms, packed_terms = halving_terms(late_pieces, late_stay, late_last)
        value_terms = (value_terms[0].astype(F32) + value_terms[1].astype(F32), value_terms[2])
        packed_terms = (packed_terms[0].astype(F32) + packed_terms[1].astype(F32), packed_terms[2])
        grad_out = sum(term.astype(F32) for term in out_terms).T
        grad_query_key, grad_value_gate, grad_decay_beta = run_finish(
            key_width, heads, value_terms, gate_terms, packed_terms
        )
        grad_decay_beta = jnp.swapaxes(grad_decay_beta, 1, 2)
    else:
        grad_gate = scatter(product("td,tf->df", inputs, delta_gate), "ctx", 0).astype(F32)
        grad_out = scatter(product("tf,td->fd", hidden, grad_mixed), "ctx", 1).astype(F32)
        grad_value = scatter(product("td,tf->df", inputs, delta_value), "ctx", 0).astype(F32)
        packed = scatter(product("td,tf->df", inputs, delta_query_key), "ctx", 0).astype(F32)
        rest = packed[:, 2 * key_width :]
        grad_query_key = jnp.stack([packed[:, :key_width], packed[:, key_width : 2 * key_width]])
        grad_value_gate = jnp.stack([grad_value, grad_gate])
        grad_decay_beta = jnp.stack([rest[:, :heads], rest[:, heads : 2 * heads]])
    return (mixed, grad_inputs, grad_query_key, grad_value_gate, grad_decay_beta, grad_out)


def solution(mesh):
    in_specs = (
        P("ctx", None),
        P(None, None, "head"),
        P(None, None, "head"),
        P(None, None, "head"),
        P("head"),
        P("head"),
        P(),
        P("head", None),
        P("ctx"),
        P("ctx", None),
    )
    out_specs = (
        P("ctx", "head"),
        P("ctx", "head"),
        P(None, "ctx", "head"),
        P(None, "ctx", "head"),
        P(None, "ctx", "head"),
        P("head", "ctx"),
    )
    return jax.shard_map(body, mesh=mesh, in_specs=in_specs, out_specs=out_specs, check_vma=False)
```

```python
import functools

import jax
import jax.numpy as jnp
from jax import lax
from jax.experimental import pallas as pl
from jax.experimental.pallas import tpu as pltpu
from jax.sharding import PartitionSpec as P

DK = 128
DV = 128
CHUNK = 128
EPS = 1e-06
QUERY_SCALE = DK ** (-0.5)
LANES = 128
FORWARD_SPANS = 2
BACKWARD_SPANS = 2

F32 = jnp.float32
BF16 = jnp.bfloat16
NN = ((1,), (0,))
NT = ((1,), (1,))
TN = ((0,), (0,))


def dot(a, b, dims=NN):
    return lax.dot_general(
        a.astype(BF16), b.astype(BF16), (dims, ((), ())), preferred_element_type=F32
    )


def exact(a, b, dims=NN):
    return lax.dot_general(
        a, b, (dims, ((), ())), precision=lax.Precision.HIGHEST, preferred_element_type=F32
    )


def softplus(x):
    return jnp.maximum(x, 0.0) + jnp.log1p(jnp.exp(-jnp.abs(x)))


def sigmoid(x):
    return 1.0 / (1.0 + jnp.exp(-x))


def row_sum(x):
    return jnp.sum(x, axis=-1, keepdims=True)


def grid_of(size):
    row = lax.broadcasted_iota(jnp.int32, (size, size), 0)
    col = lax.broadcasted_iota(jnp.int32, (size, size), 1)
    return row, col


def decays(decay_beta, bias_ref, scale_ref, resets):
    row, col = grid_of(CHUNK)
    lower = (row >= col).astype(F32)
    heads = bias_ref.shape[1]
    decay_logit = decay_beta[:, :heads]
    beta = sigmoid(decay_beta[:, heads:] + bias_ref[...])
    log_decay = -scale_ref[...] * softplus(decay_logit)
    resets = jnp.broadcast_to(resets.astype(F32), (8, CHUNK))
    doc_row = dot(resets, lower, NT)[0:1]
    doc_col = dot(lower, resets, NT)[:, 0:1]
    cum_col = exact(lower, log_decay)
    cum_row = exact(log_decay, lower, ((0,), (1,)))
    same = (doc_col == doc_row) & (row >= col)
    start = jnp.where(doc_col == 0.0, jnp.exp(cum_col), 0.0)
    last = CHUNK - 1
    end = jnp.where(
        doc_col == doc_col[last:],
        jnp.exp(jnp.minimum(cum_col[last:] - cum_col, 0.0)),
        0.0,
    )
    return beta, cum_col, cum_row, same, start, end, start[last:], resets


def pair_decay(cum_col, cum_row, same, h):
    gap = jnp.minimum(spread_column(cum_col, h) - cum_row[h : h + 1, :], 0.0)
    return jnp.where(same, jnp.exp(gap), 0.0)


def spread_column(columns, h):
    return jnp.broadcast_to(columns[:, h : h + 1], (columns.shape[0], LANES))


def unit_rows(x):
    inverse = lax.rsqrt(row_sum(x * x) + EPS)
    return x * inverse, inverse


def forward_kernel(
    query_key_ref,
    value_ref,
    decay_beta_ref,
    bias_ref,
    scale_ref,
    resets_ref,
    solve_ref,
    start_ref,
    map_ref,
    local_ref,
    total_ref,
    state_ref,
):
    heads = state_ref.shape[0]
    key_heads = query_key_ref.shape[2] // DK
    repeat = heads // key_heads
    spans = solve_ref.shape[0]
    row, col = grid_of(CHUNK)

    @pl.when(pl.program_id(0) == 0)
    def _():
        first = jnp.concatenate([(row == col).astype(F32), jnp.zeros((DK, DV), F32)], axis=1)
        for h in range(heads):
            state_ref[h] = first

    strict = row > col
    differ = row ^ col
    rows = [slice(c * CHUNK, (c + 1) * CHUNK) for c in range(spans)]
    each = [(c, h) for c in range(spans) for h in range(heads)]
    terms = [
        decays(decay_beta_ref[rows[c]], bias_ref, scale_ref, resets_ref[c]) for c in range(spans)
    ]
    keys, queries = {}, {}
    for c in range(spans):
        for g in range(key_heads):
            cols = slice(g * DK, (g + 1) * DK)
            queries[c, g] = unit_rows(query_key_ref[0, rows[c], cols])[0] * QUERY_SCALE
            keys[c, g] = unit_rows(query_key_ref[1, rows[c], cols])[0]
    grams = {p: (dot(keys[p], keys[p], NT), dot(queries[p], keys[p], NT)) for p in keys}
    scores, systems, betas, starts = {}, {}, {}, {}
    for c, h in each:
        beta, cum_col, cum_row, same, start = terms[c][:5]
        betas[c, h] = spread_column(beta, h)
        starts[c, h] = spread_column(start, h)
        decay = pair_decay(cum_col, cum_row, same, h)
        key_gram, query_gram = grams[c, h // repeat]
        scores[c, h] = (decay * query_gram).astype(BF16)
        systems[c, h] = jnp.where(strict, betas[c, h] * decay * key_gram, 0.0)
    identity = (row == col).astype(F32)
    inverse = {
        p: (identity - jnp.where(differ == 1, systems[p], 0.0)).astype(BF16) for p in each
    }
    level = 1
    while (1 << level) < CHUNK:
        here = (differ >> level) == 1
        inner = {
            p: dot(jnp.where(here, systems[p], 0.0), inverse[p]).astype(BF16) for p in each
        }
        inverse = {p: inverse[p] - dot(inverse[p], inner[p]).astype(BF16) for p in each}
        level += 1
    weights = {}
    for c, h in each:
        k = keys[c, h // repeat]
        v = value_ref[rows[c], h * DV : (h + 1) * DV]
        b = betas[c, h]
        right = jnp.concatenate([(b * starts[c, h]) * k, b * v], axis=1)
        weights[c, h] = dot(inverse[c, h], right)
        solve_ref[c, h] = inverse[c, h]
    for c in range(spans):
        end, total = terms[c][5:7]
        values = []
        for h in range(heads):
            state = state_ref[h].astype(BF16)
            start_ref[c, h] = state
            solved = weights[c, h]
            base = jnp.concatenate([jnp.zeros((CHUNK, DK), F32), solved[:, DK:]], axis=1)
            values.append((base - dot(solved[:, :DK], state)).astype(BF16))
        for h in range(heads):
            k, q = keys[c, h // repeat], queries[c, h // repeat]
            state = state_ref[h]
            out = dot(starts[c, h] * q, state) + dot(scores[c, h], values[h])
            map_ref[rows[c], h * DK : (h + 1) * DK] = out[:, :DK].astype(BF16)
            local_ref[rows[c], h * DV : (h + 1) * DV] = out[:, DK:]
            state = total[:, h : h + 1] * state + dot(spread_column(end, h) * k, values[h], TN)
            state_ref[h] = state
            total_ref[h] = state.astype(BF16)


def output_kernel(
    local_ref,
    map_ref,
    gate_ref,
    delta_ref,
    state_ref,
    gain_ref,
    hidden_ref,
    delta_gate_ref,
    delta_out_ref,
    delta_state_ref,
    total_ref,
):
    heads = state_ref.shape[0]
    gain = gain_ref[...]

    @pl.when(pl.program_id(0) == 0)
    def _():
        total_ref[...] = jnp.zeros_like(total_ref)

    outs, deltas = [], []
    for h in range(heads):
        cols = slice(h * DV, (h + 1) * DV)
        outs.append(local_ref[:, cols] + dot(map_ref[:, cols], state_ref[h]))
    for h in range(heads):
        cols = slice(h * DV, (h + 1) * DV)
        out = outs[h]
        gate = gate_ref[:, cols].astype(F32)
        delta = delta_ref[:, cols].astype(F32)
        scale = lax.rsqrt(row_sum(out * out) * (1.0 / DV) + EPS)
        normed = out * scale
        share = sigmoid(gate)
        silu = gate * share
        scaled = normed * gain
        hidden_ref[:, cols] = (scaled * silu).astype(BF16)
        delta_gate_ref[:, cols] = (
            delta * scaled * (share * (1.0 + gate * (1.0 - share)))
        ).astype(BF16)
        delta_normed = delta * gain * silu
        delta_out = scale * (
            delta_normed - normed * (row_sum(normed * delta_normed) * (1.0 / DV))
        )
        delta_out = delta_out.astype(BF16)
        delta_out_ref[:, cols] = delta_out
        deltas.append(delta_out)
    for h in range(heads):
        cols = slice(h * DV, (h + 1) * DV)
        part = total_ref[h] + dot(map_ref[:, cols], deltas[h], TN)
        total_ref[h] = part
        delta_state_ref[h] = part.astype(BF16)


def backward_kernel(
    query_key_ref,
    value_ref,
    decay_beta_ref,
    bias_ref,
    scale_ref,
    resets_ref,
    solve_ref,
    start_ref,
    state_in_ref,
    delta_out_ref,
    delta_final_ref,
    delta_query_key_ref,
    delta_value_ref,
    carry_ref,
):
    heads = carry_ref.shape[0]
    key_heads = query_key_ref.shape[2] // DK
    repeat = heads // key_heads
    spans = solve_ref.shape[0]
    row, col = grid_of(CHUNK)

    @pl.when(pl.program_id(0) == 0)
    def _():
        carry_ref[...] = delta_final_ref[...].astype(F32)

    strict = row > col
    upper = (row <= col).astype(F32)
    identity = (row == col).astype(F32)
    rows = [slice(c * CHUNK, (c + 1) * CHUNK) for c in range(spans)]
    cols = [slice(h * DV, (h + 1) * DV) for h in range(heads)]
    each = [(c, h) for c in reversed(range(spans)) for h in range(heads)]
    terms = [
        decays(decay_beta_ref[rows[c]], bias_ref, scale_ref, resets_ref[c]) for c in range(spans)
    ]
    half = lax.broadcasted_iota(jnp.int32, (2 * DK, 2 * heads), 0) // DK
    lane = lax.broadcasted_iota(jnp.int32, (2 * DK, 2 * heads), 1)
    lane_one = lax.broadcasted_iota(jnp.int32, (1, heads), 1)
    qs, ks, q_inv, k_inv = {}, {}, {}, {}
    for c in range(spans):
        for g in range(key_heads):
            at = slice(g * DK, (g + 1) * DK)
            q, q_inv[c, g] = unit_rows(query_key_ref[0, rows[c], at])
            qs[c, g] = q * QUERY_SCALE
            ks[c, g], k_inv[c, g] = unit_rows(query_key_ref[1, rows[c], at])
    grams = {p: (dot(ks[p], ks[p], NT), dot(qs[p], ks[p], NT)) for p in ks}
    state_of, value_of, right_of = {}, {}, {}
    betas, starts, ends = {}, {}, {}
    for c, h in each:
        before = start_ref[c, h]
        state = dot(before[:, :DK], state_in_ref[h]) + before[:, DK:].astype(F32)
        state_of[c, h] = state.astype(BF16)
    for c, h in each:
        beta, start, end = terms[c][0], terms[c][4], terms[c][5]
        seen = dot(ks[c, h // repeat], state_of[c, h])
        betas[c, h] = spread_column(beta, h)
        starts[c, h] = spread_column(start, h)
        ends[c, h] = spread_column(end, h)
        right_of[c, h] = betas[c, h] * (value_ref[rows[c], cols[h]] - starts[c, h] * seen)
    for c, h in each:
        value_of[c, h] = dot(solve_ref[c, h], right_of[c, h]).astype(BF16)
    decay_of, delta_value_of, delta_right_of = {}, {}, {}
    for c, h in each:
        decay_of[c, h] = pair_decay(terms[c][1], terms[c][2], terms[c][3], h)
        delta_value_of[c, h] = dot(
            decay_of[c, h] * grams[c, h // repeat][1], delta_out_ref[rows[c], cols[h]], TN
        )
    both_of, held_of, carry_of = {}, {}, {}
    for c in reversed(range(spans)):
        total = terms[c][6]
        for h in range(heads):
            carry_of[c, h] = carry_ref[h].astype(BF16)
            delta_value_of[c, h] += dot(ends[c, h] * ks[c, h // repeat], carry_of[c, h])
        for h in range(heads):
            delta_right_of[c, h] = dot(solve_ref[c, h], delta_value_of[c, h], TN)
        for h in range(heads):
            q, k = qs[c, h // repeat], ks[c, h // repeat]
            b, s = betas[c, h], starts[c, h]
            delta_right = delta_right_of[c, h]
            delta_value_ref[rows[c], cols[h]] = (b * delta_right).astype(BF16)
            both_of[c, h] = jnp.concatenate(
                [delta_out_ref[rows[c], cols[h]], delta_right.astype(BF16)], axis=0
            )
            carry = carry_ref[h]
            held_of[c, h] = total[:, h : h + 1] * row_sum(
                jnp.sum(state_of[c, h].astype(F32) * carry, axis=0, keepdims=True)
            )
            carry_ref[h] = total[:, h : h + 1] * carry + dot(
                jnp.concatenate([s * q, (-b * s) * k], axis=0), both_of[c, h], TN
            )
    pairs_of = {p: dot(both_of[p], value_of[p], NT) for p in each}
    states_of = {p: dot(both_of[p], state_of[p], NT) for p in each}
    ends_of = {p: ends[p] * dot(value_of[p], carry_of[p], NT) for p in each}
    pair_of, sum_of, tail_of, lower_of = {}, {}, {}, {}
    for c, h in each:
        q, k = qs[c, h // repeat], ks[c, h // repeat]
        key_gram, query_gram = grams[c, h // repeat]
        decay, b, s = decay_of[c, h], betas[c, h], starts[c, h]
        pair_q = decay * pairs_of[c, h][:CHUNK]
        pair_k = jnp.where(strict, (-b) * decay * pairs_of[c, h][CHUNK:], 0.0)
        cross = jnp.where(strict, pair_q * query_gram + pair_k * key_gram, 0.0).astype(BF16)
        pair_of[c, h] = (pair_q.astype(BF16), pair_k.astype(BF16))
        state_q = s * states_of[c, h][:CHUNK]
        state_k = (b * s) * states_of[c, h][CHUNK:]
        states_of[c, h] = (state_q, ends_of[c, h] - state_k)
        sum_of[c, h] = jnp.concatenate(
            [cross, (state_q * q - state_k * k).astype(BF16)], axis=1
        )
        tail_of[c, h] = jnp.concatenate(
            [ends_of[c, h] * k, delta_right_of[c, h] * value_of[c, h].astype(F32)], axis=1
        ).astype(BF16)
        lower_of[c, h] = jnp.sum(cross.astype(F32), axis=0, keepdims=True)
    for c in range(spans):
        for g in range(key_heads):
            q, k = qs[c, g], ks[c, g]
            both = jnp.concatenate([q, k], axis=0)
            delta_q = jnp.zeros((CHUNK, DK), F32)
            delta_k = jnp.zeros((CHUNK, DK), F32)
            for h in range(g * repeat, (g + 1) * repeat):
                pair_q, pair_k = pair_of[c, h]
                delta_q += dot(pair_q, k) + states_of[c, h][0]
                delta_k += (
                    dot(pair_k, k)
                    + dot(jnp.concatenate([pair_q, pair_k], axis=0), both, TN)
                    + states_of[c, h][1]
                )
            delta_q = delta_q * QUERY_SCALE
            unit = q * (1.0 / QUERY_SCALE)
            delta_q = q_inv[c, g] * (delta_q - unit * row_sum(unit * delta_q))
            delta_k = k_inv[c, g] * (delta_k - k * row_sum(k * delta_k))
            at, after = g * DK, (key_heads + g) * DK
            delta_query_key_ref[rows[c], at : at + DK] = delta_q.astype(BF16)
            delta_query_key_ref[rows[c], after : after + DK] = delta_k.astype(BF16)
    for c in range(spans):
        beta, resets = terms[c][0], terms[c][7]
        sums = jnp.zeros((CHUNK, 2 * heads), F32)
        tails = jnp.zeros((CHUNK, 2 * heads), F32)
        tail = jnp.zeros((1, heads), F32)
        for h in range(heads):
            sums += dot(sum_of[c, h], lane == h)
            tails += dot(tail_of[c, h], lane == h + heads * half)
            tail = jnp.where(lane_one == h, held_of[c, h], tail)
        below = [lower_of[c, h] for h in range(heads)]
        if heads % 8:
            below.append(jnp.zeros((-heads % 8, CHUNK), F32))
        below = exact(upper, jnp.concatenate(below, axis=0), NT)[:, :heads]
        ends_sum = tails[:, :heads]
        tail = tail + jnp.sum(ends_sum, axis=0, keepdims=True)
        delta_log = exact(upper, sums[:, :heads] - ends_sum) - below + tail
        reset_col = dot(identity, resets, NT)[:, 0:1]
        delta_log = jnp.where(reset_col == 0.0, delta_log, 0.0)
        logits = decay_beta_ref[rows[c], :heads]
        delta_decay = delta_log * (-scale_ref[...]) * sigmoid(logits)
        delta_beta = tails[:, heads:] * (1.0 - beta)
        rest = jnp.zeros((CHUNK, LANES - 2 * heads), F32)
        delta_query_key_ref[rows[c], 2 * key_heads * DK :] = jnp.concatenate(
            [delta_decay, delta_beta, rest], axis=1
        ).astype(BF16)


def chain_forward_kernel(totals_ref, states_ref):
    devices, heads = totals_ref.shape[0], totals_ref.shape[1]
    for h in range(heads):
        state = jnp.zeros(states_ref.shape[2:], F32)
        for i in range(devices):
            states_ref[i, h] = state.astype(BF16)
            if i < devices - 1:
                step = totals_ref[i, h]
                high = state.astype(BF16)
                low = state - high.astype(F32)
                state = (
                    dot(step[:, :DK], high) + dot(step[:, :DK], low) + step[:, DK:].astype(F32)
                )


def chain_backward_kernel(totals_ref, deltas_ref, states_ref):
    devices, heads = totals_ref.shape[0], totals_ref.shape[1]
    for h in range(heads):
        state = jnp.zeros(states_ref.shape[2:], F32)
        for i in reversed(range(devices)):
            states_ref[i, h] = state.astype(BF16)
            if i > 0:
                step = totals_ref[i, h]
                high = state.astype(BF16)
                low = state - high.astype(F32)
                state = (
                    dot(step[:, :DK], high, TN)
                    + dot(step[:, :DK], low, TN)
                    + deltas_ref[i, h].astype(F32)
                )


PARAMS = pltpu.CompilerParams(
    dimension_semantics=("arbitrary",), vmem_limit_bytes=56 * 1024 * 1024
)
INTERPRET = False


def whole(shape):
    return pl.BlockSpec(shape, lambda c: (0,) * len(shape))


def run_forward(query_key, value, decay_beta, bias, scale, resets):
    tokens, heads = query_key.shape[1], bias.shape[1]
    chunks = tokens // CHUNK
    spans = min(FORWARD_SPANS, chunks)
    step = spans * CHUNK
    key_width, value_width = query_key.shape[2], heads * DV
    return pl.pallas_call(
        forward_kernel,
        grid=(chunks // spans,),
        in_specs=[
            pl.BlockSpec((2, step, key_width), lambda c: (0, c, 0)),
            pl.BlockSpec((step, value_width), lambda c: (c, 0)),
            pl.BlockSpec((step, 2 * heads), lambda c: (c, 0)),
            whole((1, heads)),
            whole((1, heads)),
            pl.BlockSpec((spans, 1, CHUNK), lambda c: (c, 0, 0)),
        ],
        out_specs=[
            pl.BlockSpec((spans, heads, CHUNK, CHUNK), lambda c: (c, 0, 0, 0)),
            pl.BlockSpec((spans, heads, DK, DK + DV), lambda c: (c, 0, 0, 0)),
            pl.BlockSpec((step, value_width), lambda c: (c, 0)),
            pl.BlockSpec((step, value_width), lambda c: (c, 0)),
            whole((heads, DK, DK + DV)),
        ],
        out_shape=[
            jax.ShapeDtypeStruct((chunks, heads, CHUNK, CHUNK), BF16),
            jax.ShapeDtypeStruct((chunks, heads, DK, DK + DV), BF16),
            jax.ShapeDtypeStruct((tokens, value_width), BF16),
            jax.ShapeDtypeStruct((tokens, value_width), F32),
            jax.ShapeDtypeStruct((heads, DK, DK + DV), BF16),
        ],
        scratch_shapes=[pltpu.VMEM((heads, DK, DK + DV), F32)],
        compiler_params=PARAMS,
        interpret=INTERPRET,
        name="forward_blocks",
    )(query_key, value, decay_beta, bias, scale, resets)


def run_output(local, reach, gate, delta_hidden, state_in, gain):
    tokens, value_width = local.shape
    heads = value_width // DV
    chunks = tokens // CHUNK
    block = pl.BlockSpec((CHUNK, value_width), lambda c: (c, 0))
    return pl.pallas_call(
        output_kernel,
        grid=(chunks,),
        in_specs=[
            block,
            block,
            block,
            block,
            whole((heads, DK, DV)),
            whole((1, DV)),
        ],
        out_specs=[block, block, block, whole((heads, DK, DV))],
        out_shape=[
            jax.ShapeDtypeStruct((tokens, value_width), BF16),
            jax.ShapeDtypeStruct((tokens, value_width), BF16),
            jax.ShapeDtypeStruct((tokens, value_width), BF16),
            jax.ShapeDtypeStruct((heads, DK, DV), BF16),
        ],
        scratch_shapes=[pltpu.VMEM((heads, DK, DV), F32)],
        compiler_params=PARAMS,
        interpret=INTERPRET,
        name="gated_norm",
    )(local, reach, gate, delta_hidden, state_in, gain)


def run_backward(
    query_key, value, decay_beta, bias, scale, resets, solve, starts, state_in, delta_out, final
):
    tokens, heads = query_key.shape[1], bias.shape[1]
    chunks = tokens // CHUNK
    spans = min(BACKWARD_SPANS, chunks)
    step = spans * CHUNK
    key_width, value_width = query_key.shape[2], heads * DV
    last = chunks // spans - 1
    return pl.pallas_call(
        backward_kernel,
        grid=(chunks // spans,),
        in_specs=[
            pl.BlockSpec((2, step, key_width), lambda c: (0, last - c, 0)),
            pl.BlockSpec((step, value_width), lambda c: (last - c, 0)),
            pl.BlockSpec((step, 2 * heads), lambda c: (last - c, 0)),
            whole((1, heads)),
            whole((1, heads)),
            pl.BlockSpec((spans, 1, CHUNK), lambda c: (last - c, 0, 0)),
            pl.BlockSpec((spans, heads, CHUNK, CHUNK), lambda c: (last - c, 0, 0, 0)),
            pl.BlockSpec((spans, heads, DK, DK + DV), lambda c: (last - c, 0, 0, 0)),
            whole((heads, DK, DV)),
            pl.BlockSpec((step, value_width), lambda c: (last - c, 0)),
            whole((heads, DK, DV)),
        ],
        out_specs=[
            pl.BlockSpec((step, 2 * key_width + LANES), lambda c: (last - c, 0)),
            pl.BlockSpec((step, value_width), lambda c: (last - c, 0)),
        ],
        out_shape=[
            jax.ShapeDtypeStruct((tokens, 2 * key_width + LANES), BF16),
            jax.ShapeDtypeStruct((tokens, value_width), BF16),
        ],
        scratch_shapes=[pltpu.VMEM((heads, DK, DV), F32)],
        compiler_params=PARAMS,
        interpret=INTERPRET,
        name="backward_blocks",
    )(query_key, value, decay_beta, bias, scale, resets, solve, starts, state_in, delta_out, final)


def spread(array, devices):
    heads, depth, width = array.shape
    if heads >= devices:
        return array.reshape(devices, heads // devices, depth, width)
    cuts = devices // heads
    parts = array.reshape(heads, depth, cuts, width // cuts)
    return jnp.transpose(parts, (0, 2, 1, 3)).reshape(devices, 1, depth, width // cuts)


def gather_parts(parts, heads):
    devices, each, depth, width = parts.shape
    if heads >= devices:
        return parts.reshape(heads, depth, width)
    cuts = devices // heads
    parts = parts.reshape(heads, cuts, depth, width)
    return jnp.transpose(parts, (0, 2, 1, 3)).reshape(heads, depth, cuts * width)


def swap(parts):
    return lax.all_to_all(parts, "ctx", split_axis=0, concat_axis=0, tiled=True)


def spread_totals(totals):
    devices, heads = lax.axis_size("ctx"), totals.shape[0]
    if heads >= devices:
        return spread(totals, devices)
    maps = jnp.repeat(totals[:, :, :DK], devices // heads, axis=0)[:, None]
    return jnp.concatenate([maps, spread(totals[:, :, DK:], devices)], axis=-1)


def run_chain_forward(held):
    return pl.pallas_call(
        chain_forward_kernel,
        out_shape=jax.ShapeDtypeStruct((*held.shape[:3], held.shape[3] - DK), BF16),
        interpret=INTERPRET,
        name="chain_forward",
    )(held)


def run_chain_backward(held, deltas):
    return pl.pallas_call(
        chain_backward_kernel,
        out_shape=jax.ShapeDtypeStruct(deltas.shape, BF16),
        interpret=INTERPRET,
        name="chain_backward",
    )(held, deltas)


def product(spec, a, b):
    return jnp.einsum(spec, a, b, preferred_element_type=F32)


def rows_of(small_weight_ref):
    return jnp.concatenate([small_weight_ref[0].astype(F32), small_weight_ref[1].astype(F32)], axis=0)


def projection_kernel(
    inputs_ref,
    query_key_weight_ref,
    value_weight_ref,
    decay_beta_weight_ref,
    query_key_ref,
    value_ref,
    decay_beta_ref,
):
    inputs = inputs_ref[...]
    query_key_ref[0] = dot(inputs, query_key_weight_ref[0])
    value_ref[...] = dot(inputs, value_weight_ref[0])

    @pl.when(pl.program_id(0) == 0)
    def _():
        decay_beta_ref[...] = dot(inputs, rows_of(decay_beta_weight_ref), NT)


def run_projection(inputs, query_key_weight, value_gate_weight, decay_beta_weight):
    tokens, model = inputs.shape
    key_width, value_width = query_key_weight.shape[2], value_gate_weight.shape[2]
    heads = decay_beta_weight.shape[1]
    steps = 4
    keys, values = 2 * key_width // steps, value_width // steps
    return pl.pallas_call(
        projection_kernel,
        grid=(steps,),
        in_specs=[
            whole((tokens, model)),
            pl.BlockSpec((1, model, keys), lambda j: (j // 2, 0, j % 2)),
            pl.BlockSpec((1, model, values), lambda j: (0, 0, j)),
            whole((2, heads, model)),
        ],
        out_specs=[
            pl.BlockSpec((1, tokens, keys), lambda j: (j // 2, 0, j % 2)),
            pl.BlockSpec((tokens, values), lambda j: (0, j)),
            whole((tokens, 2 * heads)),
        ],
        out_shape=[
            jax.ShapeDtypeStruct((2, tokens, key_width), F32),
            jax.ShapeDtypeStruct((tokens, value_width), F32),
            jax.ShapeDtypeStruct((tokens, 2 * heads), F32),
        ],
        compiler_params=PARAMS,
        interpret=INTERPRET,
        name="projection",
    )(inputs, query_key_weight, value_gate_weight, decay_beta_weight)


def input_gradient_kernel(
    delta_query_key_ref,
    delta_value_ref,
    delta_gate_ref,
    query_key_weight_ref,
    value_gate_weight_ref,
    decay_beta_weight_ref,
    out_ref,
):
    width = query_key_weight_ref.shape[2]
    heads = decay_beta_weight_ref.shape[1]
    keys = jnp.concatenate([query_key_weight_ref[0], query_key_weight_ref[1]], axis=1)
    small = delta_query_key_ref[:, 2 * width : 2 * width + 2 * heads]
    total = dot(delta_gate_ref[...], value_gate_weight_ref[1], NT)
    total += dot(delta_value_ref[...], value_gate_weight_ref[0], NT)
    total += dot(delta_query_key_ref[:, : 2 * width], keys, NT)
    total += dot(small, rows_of(decay_beta_weight_ref))
    out_ref[...] = total.astype(BF16)


def run_input_gradient(
    delta_query_key, delta_value, delta_gate, query_key_weight, value_gate_weight, decay_beta_weight
):
    tokens, model = delta_value.shape[0], query_key_weight.shape[1]
    cut = 512

    def weight(array):
        return pl.BlockSpec((2, cut, array.shape[2]), lambda j: (0, j, 0))

    return pl.pallas_call(
        input_gradient_kernel,
        grid=(model // cut,),
        in_specs=[
            whole(delta_query_key.shape),
            whole(delta_value.shape),
            whole(delta_gate.shape),
            weight(query_key_weight),
            weight(value_gate_weight),
            pl.BlockSpec((2, decay_beta_weight.shape[1], cut), lambda j: (0, 0, j)),
        ],
        out_specs=pl.BlockSpec((tokens, cut), lambda j: (0, j)),
        out_shape=jax.ShapeDtypeStruct((tokens, model), BF16),
        compiler_params=PARAMS,
        interpret=INTERPRET,
        name="input_gradient",
    )(delta_query_key, delta_value, delta_gate, query_key_weight, value_gate_weight, decay_beta_weight)


def together(*arrays):
    return lax.optimization_barrier(arrays)


def exchange(array, distance):
    devices = range(lax.axis_size("ctx"))
    return lax.ppermute(array, "ctx", [(i, i ^ distance) for i in devices])


def block_of(step, place, flip):
    x, y = (place // 2) % 2, place // 4
    core = lax.rem(place + flip, 2)
    across_x, across_y = 1 - step // 2, 1 - lax.rem(step, 2)
    target_x, target_y = lax.rem(x + across_x, 2), lax.rem(y + across_y, 2)
    return target_y * 4 + target_x * 2 + core


def send_kernel(place_ref, left_a_ref, a_ref, left_b_ref, b_ref, a_out_ref, b_out_ref):
    a_out_ref[...] = dot(left_a_ref[...], a_ref[...], TN).astype(BF16)
    b_out_ref[...] = dot(left_b_ref[...], b_ref[...], TN).astype(BF16)


def keep_step(
    step, left_a_ref, a_ref, left_b_ref, b_ref, a_arrived_ref, b_arrived_ref, *out_refs
):
    a = dot(left_a_ref[...], a_ref[...], TN) + a_arrived_ref[...].astype(F32)
    b = dot(left_b_ref[...], b_ref[...], TN) + b_arrived_ref[...].astype(F32)
    for i in range(4):

        @pl.when(step == i)
        def _():
            out_refs[i][...] = a.astype(BF16)
            out_refs[4 + i][...] = b.astype(BF16)


def keep_kernel(place_ref, *refs):
    keep_step(pl.program_id(0), *refs)


def pair_specs(left_a, a, left_b, b, flip):
    def rows(left):
        return pl.BlockSpec(
            (left.shape[0], left.shape[1] // 8), lambda i, place: (0, block_of(i, place[0], flip))
        )

    def full(delta):
        return pl.BlockSpec(delta.shape, lambda i, place: (0, 0))

    return [rows(left_a), full(a), rows(left_b), full(b)]


def send_and_sum_kernel(
    place_ref, left_a_ref, a_ref, left_b_ref, b_ref, *refs
):
    sums, outs = refs[:4], refs[4:]
    send_kernel(place_ref, left_a_ref, a_ref, left_b_ref, b_ref, outs[0], outs[1])
    for i in range(2):
        outs[2 + i][...] = summed(sums[2 * i][...], sums[2 * i + 1][...])


def halving_start_and_sum(place, left_a, a, left_b, b, pieces, arrived):
    rows = left_a.shape[1] // 8
    terms = [pieces[2], arrived[0], pieces[5], arrived[1]]

    def quarter(array):
        return pl.BlockSpec((rows // 4, array.shape[1]), lambda i, place: (i, 0))

    results = pl.pallas_call(
        send_and_sum_kernel,
        grid_spec=pltpu.PrefetchScalarGridSpec(
            num_scalar_prefetch=1,
            grid=(4,),
            in_specs=pair_specs(left_a, a, left_b, b, 1) + [quarter(term) for term in terms],
            out_specs=[
                pl.BlockSpec((rows, delta.shape[1]), lambda i, place: (i, 0)) for delta in (a, b)
            ]
            + [quarter(terms[0]), quarter(terms[2])],
        ),
        out_shape=[
            jax.ShapeDtypeStruct((4 * rows, delta.shape[1]), BF16) for delta in (a, b)
        ]
        + [jax.ShapeDtypeStruct(term.shape, BF16) for term in (terms[0], terms[2])],
        compiler_params=PARAMS,
        interpret=INTERPRET,
        name="send_rows_and_sum",
    )(place, left_a, a, left_b, b, *terms)
    return results[:2], results[2:]


def halving_start(place, left_a, a, left_b, b):
    rows = left_a.shape[1] // 8
    return pl.pallas_call(
        send_kernel,
        grid_spec=pltpu.PrefetchScalarGridSpec(
            num_scalar_prefetch=1,
            grid=(4,),
            in_specs=pair_specs(left_a, a, left_b, b, 1),
            out_specs=[
                pl.BlockSpec((rows, delta.shape[1]), lambda i, place: (i, 0)) for delta in (a, b)
            ],
        ),
        out_shape=[
            jax.ShapeDtypeStruct((4 * rows, delta.shape[1]), BF16) for delta in (a, b)
        ],
        compiler_params=PARAMS,
        interpret=INTERPRET,
        name="send_rows",
    )(place, left_a, a, left_b, b)


def halving_keep(place, left_a, a, left_b, b, a_arrived, b_arrived):
    rows = left_a.shape[1] // 8
    return pl.pallas_call(
        keep_kernel,
        grid_spec=pltpu.PrefetchScalarGridSpec(
            num_scalar_prefetch=1,
            grid=(4,),
            in_specs=pair_specs(left_a, a, left_b, b, 0)
            + [pl.BlockSpec((rows, delta.shape[1]), lambda i, place: (i, 0)) for delta in (a, b)],
            out_specs=[
                pl.BlockSpec((rows, delta.shape[1]), lambda i, place: (0, 0))
                for delta in (a, b)
                for _ in range(4)
            ],
        ),
        out_shape=[
            jax.ShapeDtypeStruct((rows, delta.shape[1]), BF16)
            for delta in (a, b)
            for _ in range(4)
        ],
        compiler_params=PARAMS,
        interpret=INTERPRET,
        name="keep_rows",
    )(place, left_a, a, left_b, b, a_arrived, b_arrived)


def summed(a, b):
    return (a.astype(F32) + b.astype(F32)).astype(BF16)


def halving_cross(pieces):
    return exchange(pieces[0], 2), exchange(pieces[4], 4)


def halving_stay(pieces):
    return exchange(pieces[1], 2), exchange(pieces[6], 4)


def halving_onward(pieces, arrived):
    return summed(pieces[2], arrived[0]), summed(pieces[5], arrived[1])


def halving_last(onward):
    return exchange(onward[0], 4), exchange(onward[1], 2)


def halving_terms(pieces, stay, last):
    return (pieces[3], stay[0], last[0]), (pieces[7], stay[1], last[1])


def finish_kernel(key_width, heads, *refs):
    def total(*terms):
        return sum(term[...].astype(F32) for term in terms)

    query_key_ref, value_gate_ref, decay_beta_ref = refs[7:]
    value_gate_ref[0] = total(*refs[0:2])
    value_gate_ref[1] = total(*refs[2:5])
    packed = total(*refs[5:7])
    query_key_ref[0] = packed[:, :key_width]
    query_key_ref[1] = packed[:, key_width : 2 * key_width]
    small = packed[:, 2 * key_width :].T
    decay_beta_ref[0] = small[:heads]
    decay_beta_ref[1] = small[heads : 2 * heads]


def run_finish(key_width, heads, value, gate, packed):
    rows, width = value[0].shape
    step = 128

    def block(array):
        return pl.BlockSpec((step, array.shape[1]), lambda i: (i, 0))

    def pair(size):
        return pl.BlockSpec((2, step, size), lambda i: (0, i, 0))

    terms = [*value, *gate, *packed]
    return pl.pallas_call(
        functools.partial(finish_kernel, key_width, heads),
        grid=(rows // step,),
        in_specs=[block(term) for term in terms],
        out_specs=[
            pair(key_width),
            pair(width),
            pl.BlockSpec((2, heads, step), lambda i: (0, 0, i)),
        ],
        out_shape=[
            jax.ShapeDtypeStruct((2, rows, key_width), F32),
            jax.ShapeDtypeStruct((2, rows, width), F32),
            jax.ShapeDtypeStruct((2, heads, rows), F32),
        ],
        compiler_params=PARAMS,
        interpret=INTERPRET,
        name="finish",
    )(*terms)


def gradient_and_keep_kernel(place_ref, *refs):
    step = pl.program_id(0)
    cuts = pl.num_programs(0) - 4
    gradient_refs, keep_refs = refs[:6], refs[6:12]
    out_ref, piece_refs = refs[12], refs[13:]

    @pl.when(step < cuts)
    def _():
        input_gradient_kernel(*gradient_refs, out_ref)

    @pl.when(step >= cuts)
    def _():
        keep_step(step - cuts, *keep_refs, *piece_refs)


def run_gradient_and_keep(place, gradient_args, keep_args):
    delta_query_key, delta_value, delta_gate, query_key_weight, value_gate_weight, small_weight = (
        gradient_args
    )
    left_a, a, left_b, b, a_arrived, b_arrived = keep_args
    tokens, model = delta_value.shape[0], query_key_weight.shape[1]
    cut = 512
    cuts = model // cut
    rows = left_a.shape[1] // 8

    def full(array):
        return pl.BlockSpec(array.shape, lambda i, place: (0, 0))

    def weight(array):
        return pl.BlockSpec(
            (2, cut, array.shape[2]), lambda i, place: (0, jnp.minimum(i, cuts - 1), 0)
        )

    def left(array):
        return pl.BlockSpec(
            (array.shape[0], rows),
            lambda i, place: (0, block_of(jnp.maximum(i - cuts, 0), place[0], 0)),
        )

    def arrived(array):
        return pl.BlockSpec((rows, array.shape[1]), lambda i, place: (jnp.maximum(i - cuts, 0), 0))

    widths = [delta.shape[1] for delta in (a, b) for _ in range(4)]
    results = pl.pallas_call(
        gradient_and_keep_kernel,
        grid_spec=pltpu.PrefetchScalarGridSpec(
            num_scalar_prefetch=1,
            grid=(cuts + 4,),
            in_specs=[
                full(delta_query_key),
                full(delta_value),
                full(delta_gate),
                weight(query_key_weight),
                weight(value_gate_weight),
                pl.BlockSpec(
                    (2, small_weight.shape[1], cut),
                    lambda i, place: (0, 0, jnp.minimum(i, cuts - 1)),
                ),
                left(left_a),
                full(a),
                left(left_b),
                full(b),
                arrived(a_arrived),
                arrived(b_arrived),
            ],
            out_specs=[
                pl.BlockSpec((tokens, cut), lambda i, place: (0, jnp.minimum(i, cuts - 1)))
            ]
            + [pl.BlockSpec((rows, width), lambda i, place: (0, 0)) for width in widths],
        ),
        out_shape=[jax.ShapeDtypeStruct((tokens, model), BF16)]
        + [jax.ShapeDtypeStruct((rows, width), BF16) for width in widths],
        compiler_params=PARAMS,
        interpret=INTERPRET,
        name="input_gradient_and_keep",
    )(place, *gradient_args, *keep_args)
    return results[0], results[1:]


def scatter(partial, axis, dimension):
    return lax.psum_scatter(partial.astype(BF16), axis, scatter_dimension=dimension, tiled=True)


def body(
    inputs,
    query_key_weight,
    value_gate_weight,
    decay_beta_weight,
    beta_bias,
    decay_scale,
    norm_gain,
    out_weight,
    boundaries,
    grad_mixed,
):
    tokens, heads = inputs.shape[0], beta_bias.shape[0]
    key_width = query_key_weight.shape[2]
    cubic = lax.axis_size("ctx") == 8
    small_weight = jnp.swapaxes(decay_beta_weight, 1, 2)
    query_key, value, decay_beta = run_projection(
        inputs, query_key_weight, value_gate_weight, small_weight
    )
    bias, scale = beta_bias.reshape(1, heads), decay_scale.reshape(1, heads)
    resets = boundaries.reshape(tokens // CHUNK, 1, CHUNK)
    solve, starts, reach, local, totals = run_forward(
        query_key, value, decay_beta, bias, scale, resets
    )

    held = swap(spread_totals(totals))
    gate = product("td,df->tf", inputs, value_gate_weight[1]).astype(BF16)
    held, gate = together(held, gate)
    states = swap(run_chain_forward(held))
    delta_hidden = product("td,fd->tf", grad_mixed, out_weight).astype(BF16)
    states, delta_hidden = together(states, delta_hidden)
    state_in = gather_parts(states, heads)
    hidden, delta_gate, delta_out, delta_state = run_output(
        local, reach, gate, delta_hidden, state_in, norm_gain.reshape(1, DV)
    )

    deltas = swap(spread(delta_state, lax.axis_size("ctx")))
    partial_out = product("tf,fd->td", hidden, out_weight).astype(BF16)
    deltas, partial_out = together(deltas, partial_out)
    mixed = scatter(partial_out, "head", 1)
    finals = swap(run_chain_backward(held, deltas))
    if cubic:
        place = lax.axis_index("ctx").astype(jnp.int32).reshape(1)
        early = (place, inputs, delta_gate, grad_mixed, hidden)
        sent = halving_start(*early)
        arrived = [exchange(part, 1) for part in sent]
        early_pieces = halving_keep(*early, *arrived)
        finals, early_pieces = together(finals, early_pieces)
        early_arrived = halving_cross(early_pieces)
        early_stay = halving_stay(early_pieces)
    delta_final = gather_parts(finals, heads)
    delta_query_key, delta_value = run_backward(
        query_key,
        value,
        decay_beta,
        bias,
        scale,
        resets,
        solve,
        starts,
        state_in,
        delta_out,
        delta_final,
    )
    gradient_args = (
        delta_query_key,
        delta_value,
        delta_gate,
        query_key_weight,
        value_gate_weight,
        small_weight,
    )
    if cubic:
        late = (inputs, delta_value, inputs, delta_query_key)
        sent, early_onward = halving_start_and_sum(place, *late, early_pieces, early_arrived)
        sent, early_stay = together(sent, early_stay)
        arrived = [exchange(part, 1) for part in sent]
        early_last = halving_last(early_onward)
        grad_rows, late_pieces = run_gradient_and_keep(place, gradient_args, (*late, *arrived))
        grad_rows, late_pieces, early_last = together(grad_rows, late_pieces, early_last)
    else:
        grad_rows = run_input_gradient(*gradient_args)
    grad_inputs = scatter(grad_rows, "head", 1)
    if cubic:
        late_arrived = halving_cross(late_pieces)
        late_stay = halving_stay(late_pieces)
        late_last = halving_last(halving_onward(late_pieces, late_arrived))
        gate_terms, out_terms = halving_terms(early_pieces, early_stay, early_last)
        value_terms, packed_terms = halving_terms(late_pieces, late_stay, late_last)
        value_terms = (value_terms[0].astype(F32) + value_terms[1].astype(F32), value_terms[2])
        packed_terms = (packed_terms[0].astype(F32) + packed_terms[1].astype(F32), packed_terms[2])
        grad_out = sum(term.astype(F32) for term in out_terms).T
        grad_query_key, grad_value_gate, grad_decay_beta = run_finish(
            key_width, heads, value_terms, gate_terms, packed_terms
        )
        grad_decay_beta = jnp.swapaxes(grad_decay_beta, 1, 2)
    else:
        grad_gate = scatter(product("td,tf->df", inputs, delta_gate), "ctx", 0).astype(F32)
        grad_out = scatter(product("tf,td->fd", hidden, grad_mixed), "ctx", 1).astype(F32)
        grad_value = scatter(product("td,tf->df", inputs, delta_value), "ctx", 0).astype(F32)
        packed = scatter(product("td,tf->df", inputs, delta_query_key), "ctx", 0).astype(F32)
        rest = packed[:, 2 * key_width :]
        grad_query_key = jnp.stack([packed[:, :key_width], packed[:, key_width : 2 * key_width]])
        grad_value_gate = jnp.stack([grad_value, grad_gate])
        grad_decay_beta = jnp.stack([rest[:, :heads], rest[:, heads : 2 * heads]])
    return (mixed, grad_inputs, grad_query_key, grad_value_gate, grad_decay_beta, grad_out)


def solution(mesh):
    in_specs = (
        P("ctx", None),
        P(None, None, "head"),
        P(None, None, "head"),
        P(None, None, "head"),
        P("head"),
        P("head"),
        P(),
        P("head", None),
        P("ctx"),
        P("ctx", None),
    )
    out_specs = (
        P("ctx", "head"),
        P("ctx", "head"),
        P(None, "ctx", "head"),
        P(None, "ctx", "head"),
        P(None, "ctx", "head"),
        P("head", "ctx"),
    )
    return jax.shard_map(body, mesh=mesh, in_specs=in_specs, out_specs=out_specs, check_vma=False)
```

```python
import functools

import jax
import jax.numpy as jnp
from jax import lax
from jax.experimental import pallas as pl
from jax.experimental.pallas import tpu as pltpu
from jax.sharding import PartitionSpec as P

DK = 128
DV = 128
CHUNK = 128
EPS = 1e-06
QUERY_SCALE = DK ** (-0.5)
LANES = 128
FORWARD_SPANS = 2
BACKWARD_SPANS = 2

F32 = jnp.float32
BF16 = jnp.bfloat16
NN = ((1,), (0,))
NT = ((1,), (1,))
TN = ((0,), (0,))


def dot(a, b, dims=NN):
    return lax.dot_general(
        a.astype(BF16), b.astype(BF16), (dims, ((), ())), preferred_element_type=F32
    )


def exact(a, b, dims=NN):
    return lax.dot_general(
        a, b, (dims, ((), ())), precision=lax.Precision.HIGHEST, preferred_element_type=F32
    )


def softplus(x):
    return jnp.maximum(x, 0.0) + jnp.log1p(jnp.exp(-jnp.abs(x)))


def sigmoid(x):
    return 1.0 / (1.0 + jnp.exp(-x))


def row_sum(x):
    return jnp.sum(x, axis=-1, keepdims=True)


def grid_of(size):
    row = lax.broadcasted_iota(jnp.int32, (size, size), 0)
    col = lax.broadcasted_iota(jnp.int32, (size, size), 1)
    return row, col


def decays(decay_beta, bias_ref, scale_ref, resets):
    row, col = grid_of(CHUNK)
    lower = (row >= col).astype(F32)
    heads = bias_ref.shape[1]
    decay_logit = decay_beta[:, :heads]
    beta = sigmoid(decay_beta[:, heads:] + bias_ref[...])
    log_decay = -scale_ref[...] * softplus(decay_logit)
    resets = jnp.broadcast_to(resets.astype(F32), (8, CHUNK))
    doc_row = dot(resets, lower, NT)[0:1]
    doc_col = dot(lower, resets, NT)[:, 0:1]
    cum_col = exact(lower, log_decay)
    cum_row = exact(log_decay, lower, ((0,), (1,)))
    same = (doc_col == doc_row) & (row >= col)
    start = jnp.where(doc_col == 0.0, jnp.exp(cum_col), 0.0)
    last = CHUNK - 1
    end = jnp.where(
        doc_col == doc_col[last:],
        jnp.exp(jnp.minimum(cum_col[last:] - cum_col, 0.0)),
        0.0,
    )
    return beta, cum_col, cum_row, same, start, end, start[last:], resets


def pair_decay(cum_col, cum_row, same, h):
    gap = jnp.minimum(spread_column(cum_col, h) - cum_row[h : h + 1, :], 0.0)
    return jnp.where(same, jnp.exp(gap), 0.0)


def spread_column(columns, h):
    return jnp.broadcast_to(columns[:, h : h + 1], (columns.shape[0], LANES))


def unit_rows(x):
    inverse = lax.rsqrt(row_sum(x * x) + EPS)
    return x * inverse, inverse


def forward_kernel(
    query_key_ref,
    value_ref,
    decay_beta_ref,
    bias_ref,
    scale_ref,
    resets_ref,
    solve_ref,
    start_ref,
    map_ref,
    local_ref,
    total_ref,
    state_ref,
):
    heads = state_ref.shape[0]
    key_heads = query_key_ref.shape[2] // DK
    repeat = heads // key_heads
    spans = solve_ref.shape[0]
    row, col = grid_of(CHUNK)

    @pl.when(pl.program_id(0) == 0)
    def _():
        first = jnp.concatenate([(row == col).astype(F32), jnp.zeros((DK, DV), F32)], axis=1)
        for h in range(heads):
            state_ref[h] = first

    strict = row > col
    differ = row ^ col
    rows = [slice(c * CHUNK, (c + 1) * CHUNK) for c in range(spans)]
    each = [(c, h) for c in range(spans) for h in range(heads)]
    terms = [
        decays(decay_beta_ref[rows[c]], bias_ref, scale_ref, resets_ref[c]) for c in range(spans)
    ]
    keys, queries = {}, {}
    for c in range(spans):
        for g in range(key_heads):
            cols = slice(g * DK, (g + 1) * DK)
            queries[c, g] = unit_rows(query_key_ref[0, rows[c], cols])[0] * QUERY_SCALE
            keys[c, g] = unit_rows(query_key_ref[1, rows[c], cols])[0]
    grams = {p: (dot(keys[p], keys[p], NT), dot(queries[p], keys[p], NT)) for p in keys}
    scores, systems, betas, starts = {}, {}, {}, {}
    for c, h in each:
        beta, cum_col, cum_row, same, start = terms[c][:5]
        betas[c, h] = spread_column(beta, h)
        starts[c, h] = spread_column(start, h)
        decay = pair_decay(cum_col, cum_row, same, h)
        key_gram, query_gram = grams[c, h // repeat]
        scores[c, h] = (decay * query_gram).astype(BF16)
        systems[c, h] = jnp.where(strict, betas[c, h] * decay * key_gram, 0.0)
    identity = (row == col).astype(F32)
    inverse = {
        p: (identity - jnp.where(differ == 1, systems[p], 0.0)).astype(BF16) for p in each
    }
    level = 1
    while (1 << level) < CHUNK:
        here = (differ >> level) == 1
        inner = {
            p: dot(jnp.where(here, systems[p], 0.0), inverse[p]).astype(BF16) for p in each
        }
        inverse = {p: inverse[p] - dot(inverse[p], inner[p]).astype(BF16) for p in each}
        level += 1
    weights = {}
    for c, h in each:
        k = keys[c, h // repeat]
        v = value_ref[rows[c], h * DV : (h + 1) * DV]
        b = betas[c, h]
        right = jnp.concatenate([(b * starts[c, h]) * k, b * v], axis=1)
        weights[c, h] = dot(inverse[c, h], right)
        solve_ref[c, h] = inverse[c, h]
    for c in range(spans):
        end, total = terms[c][5:7]
        values = []
        for h in range(heads):
            state = state_ref[h].astype(BF16)
            start_ref[c, h] = state
            solved = weights[c, h]
            base = jnp.concatenate([jnp.zeros((CHUNK, DK), F32), solved[:, DK:]], axis=1)
            values.append((base - dot(solved[:, :DK], state)).astype(BF16))
        for h in range(heads):
            k, q = keys[c, h // repeat], queries[c, h // repeat]
            state = state_ref[h]
            out = dot(starts[c, h] * q, state) + dot(scores[c, h], values[h])
            map_ref[rows[c], h * DK : (h + 1) * DK] = out[:, :DK].astype(BF16)
            local_ref[rows[c], h * DV : (h + 1) * DV] = out[:, DK:]
            state = total[:, h : h + 1] * state + dot(spread_column(end, h) * k, values[h], TN)
            state_ref[h] = state
            total_ref[h] = state.astype(BF16)


def output_kernel(
    local_ref,
    map_ref,
    gate_ref,
    delta_ref,
    state_ref,
    gain_ref,
    hidden_ref,
    delta_gate_ref,
    delta_out_ref,
    delta_state_ref,
    total_ref,
):
    heads = state_ref.shape[0]
    gain = gain_ref[...]

    @pl.when(pl.program_id(0) == 0)
    def _():
        total_ref[...] = jnp.zeros_like(total_ref)

    outs, deltas = [], []
    for h in range(heads):
        cols = slice(h * DV, (h + 1) * DV)
        outs.append(local_ref[:, cols] + dot(map_ref[:, cols], state_ref[h]))
    for h in range(heads):
        cols = slice(h * DV, (h + 1) * DV)
        out = outs[h]
        gate = gate_ref[:, cols].astype(F32)
        delta = delta_ref[:, cols].astype(F32)
        scale = lax.rsqrt(row_sum(out * out) * (1.0 / DV) + EPS)
        normed = out * scale
        share = sigmoid(gate)
        silu = gate * share
        scaled = normed * gain
        hidden_ref[:, cols] = (scaled * silu).astype(BF16)
        delta_gate_ref[:, cols] = (
            delta * scaled * (share * (1.0 + gate * (1.0 - share)))
        ).astype(BF16)
        delta_normed = delta * gain * silu
        delta_out = scale * (
            delta_normed - normed * (row_sum(normed * delta_normed) * (1.0 / DV))
        )
        delta_out = delta_out.astype(BF16)
        delta_out_ref[:, cols] = delta_out
        deltas.append(delta_out)
    for h in range(heads):
        cols = slice(h * DV, (h + 1) * DV)
        part = total_ref[h] + dot(map_ref[:, cols], deltas[h], TN)
        total_ref[h] = part
        delta_state_ref[h] = part.astype(BF16)


def backward_kernel(
    query_key_ref,
    value_ref,
    decay_beta_ref,
    bias_ref,
    scale_ref,
    resets_ref,
    solve_ref,
    start_ref,
    state_in_ref,
    delta_out_ref,
    delta_final_ref,
    delta_query_key_ref,
    delta_value_ref,
    carry_ref,
):
    heads = carry_ref.shape[0]
    key_heads = query_key_ref.shape[2] // DK
    repeat = heads // key_heads
    spans = solve_ref.shape[0]
    row, col = grid_of(CHUNK)

    @pl.when(pl.program_id(0) == 0)
    def _():
        carry_ref[...] = delta_final_ref[...].astype(F32)

    strict = row > col
    upper = (row <= col).astype(F32)
    identity = (row == col).astype(F32)
    rows = [slice(c * CHUNK, (c + 1) * CHUNK) for c in range(spans)]
    cols = [slice(h * DV, (h + 1) * DV) for h in range(heads)]
    each = [(c, h) for c in reversed(range(spans)) for h in range(heads)]
    terms = [
        decays(decay_beta_ref[rows[c]], bias_ref, scale_ref, resets_ref[c]) for c in range(spans)
    ]
    half = lax.broadcasted_iota(jnp.int32, (2 * DK, 2 * heads), 0) // DK
    lane = lax.broadcasted_iota(jnp.int32, (2 * DK, 2 * heads), 1)
    lane_one = lax.broadcasted_iota(jnp.int32, (1, heads), 1)
    qs, ks, q_inv, k_inv = {}, {}, {}, {}
    for c in range(spans):
        for g in range(key_heads):
            at = slice(g * DK, (g + 1) * DK)
            q, q_inv[c, g] = unit_rows(query_key_ref[0, rows[c], at])
            qs[c, g] = q * QUERY_SCALE
            ks[c, g], k_inv[c, g] = unit_rows(query_key_ref[1, rows[c], at])
    grams = {p: (dot(ks[p], ks[p], NT), dot(qs[p], ks[p], NT)) for p in ks}
    state_of, value_of, right_of = {}, {}, {}
    betas, starts, ends = {}, {}, {}
    for c, h in each:
        before = start_ref[c, h]
        state = dot(before[:, :DK], state_in_ref[h]) + before[:, DK:].astype(F32)
        state_of[c, h] = state.astype(BF16)
    for c, h in each:
        beta, start, end = terms[c][0], terms[c][4], terms[c][5]
        seen = dot(ks[c, h // repeat], state_of[c, h])
        betas[c, h] = spread_column(beta, h)
        starts[c, h] = spread_column(start, h)
        ends[c, h] = spread_column(end, h)
        right_of[c, h] = betas[c, h] * (value_ref[rows[c], cols[h]] - starts[c, h] * seen)
    for c, h in each:
        value_of[c, h] = dot(solve_ref[c, h], right_of[c, h]).astype(BF16)
    decay_of, delta_value_of, delta_right_of = {}, {}, {}
    for c, h in each:
        decay_of[c, h] = pair_decay(terms[c][1], terms[c][2], terms[c][3], h)
        delta_value_of[c, h] = dot(
            decay_of[c, h] * grams[c, h // repeat][1], delta_out_ref[rows[c], cols[h]], TN
        )
    both_of, held_of, carry_of = {}, {}, {}
    for c in reversed(range(spans)):
        total = terms[c][6]
        for h in range(heads):
            carry_of[c, h] = carry_ref[h].astype(BF16)
            delta_value_of[c, h] += dot(ends[c, h] * ks[c, h // repeat], carry_of[c, h])
        for h in range(heads):
            delta_right_of[c, h] = dot(solve_ref[c, h], delta_value_of[c, h], TN)
        for h in range(heads):
            q, k = qs[c, h // repeat], ks[c, h // repeat]
            b, s = betas[c, h], starts[c, h]
            delta_right = delta_right_of[c, h]
            delta_value_ref[rows[c], cols[h]] = (b * delta_right).astype(BF16)
            both_of[c, h] = jnp.concatenate(
                [delta_out_ref[rows[c], cols[h]], delta_right.astype(BF16)], axis=0
            )
            carry = carry_ref[h]
            held_of[c, h] = total[:, h : h + 1] * row_sum(
                jnp.sum(state_of[c, h].astype(F32) * carry, axis=0, keepdims=True)
            )
            carry_ref[h] = total[:, h : h + 1] * carry + dot(
                jnp.concatenate([s * q, (-b * s) * k], axis=0), both_of[c, h], TN
            )
    pairs_of = {p: dot(both_of[p], value_of[p], NT) for p in each}
    states_of = {p: dot(both_of[p], state_of[p], NT) for p in each}
    ends_of = {p: ends[p] * dot(value_of[p], carry_of[p], NT) for p in each}
    pair_of, sum_of, tail_of, lower_of = {}, {}, {}, {}
    for c, h in each:
        q, k = qs[c, h // repeat], ks[c, h // repeat]
        key_gram, query_gram = grams[c, h // repeat]
        decay, b, s = decay_of[c, h], betas[c, h], starts[c, h]
        pair_q = decay * pairs_of[c, h][:CHUNK]
        pair_k = jnp.where(strict, (-b) * decay * pairs_of[c, h][CHUNK:], 0.0)
        cross = jnp.where(strict, pair_q * query_gram + pair_k * key_gram, 0.0).astype(BF16)
        pair_of[c, h] = (pair_q.astype(BF16), pair_k.astype(BF16))
        state_q = s * states_of[c, h][:CHUNK]
        state_k = (b * s) * states_of[c, h][CHUNK:]
        states_of[c, h] = (state_q, ends_of[c, h] - state_k)
        sum_of[c, h] = jnp.concatenate(
            [cross, (state_q * q - state_k * k).astype(BF16)], axis=1
        )
        tail_of[c, h] = jnp.concatenate(
            [ends_of[c, h] * k, delta_right_of[c, h] * value_of[c, h].astype(F32)], axis=1
        ).astype(BF16)
        lower_of[c, h] = jnp.sum(cross.astype(F32), axis=0, keepdims=True)
    for c in range(spans):
        for g in range(key_heads):
            q, k = qs[c, g], ks[c, g]
            both = jnp.concatenate([q, k], axis=0)
            delta_q = jnp.zeros((CHUNK, DK), F32)
            delta_k = jnp.zeros((CHUNK, DK), F32)
            for h in range(g * repeat, (g + 1) * repeat):
                pair_q, pair_k = pair_of[c, h]
                delta_q += dot(pair_q, k) + states_of[c, h][0]
                delta_k += (
                    dot(pair_k, k)
                    + dot(jnp.concatenate([pair_q, pair_k], axis=0), both, TN)
                    + states_of[c, h][1]
                )
            delta_q = delta_q * QUERY_SCALE
            unit = q * (1.0 / QUERY_SCALE)
            delta_q = q_inv[c, g] * (delta_q - unit * row_sum(unit * delta_q))
            delta_k = k_inv[c, g] * (delta_k - k * row_sum(k * delta_k))
            at, after = g * DK, (key_heads + g) * DK
            delta_query_key_ref[rows[c], at : at + DK] = delta_q.astype(BF16)
            delta_query_key_ref[rows[c], after : after + DK] = delta_k.astype(BF16)
    for c in range(spans):
        beta, resets = terms[c][0], terms[c][7]
        sums = jnp.zeros((CHUNK, 2 * heads), F32)
        tails = jnp.zeros((CHUNK, 2 * heads), F32)
        tail = jnp.zeros((1, heads), F32)
        for h in range(heads):
            sums += dot(sum_of[c, h], lane == h)
            tails += dot(tail_of[c, h], lane == h + heads * half)
            tail = jnp.where(lane_one == h, held_of[c, h], tail)
        below = [lower_of[c, h] for h in range(heads)]
        if heads % 8:
            below.append(jnp.zeros((-heads % 8, CHUNK), F32))
        below = exact(upper, jnp.concatenate(below, axis=0), NT)[:, :heads]
        ends_sum = tails[:, :heads]
        tail = tail + jnp.sum(ends_sum, axis=0, keepdims=True)
        delta_log = exact(upper, sums[:, :heads] - ends_sum) - below + tail
        reset_col = dot(identity, resets, NT)[:, 0:1]
        delta_log = jnp.where(reset_col == 0.0, delta_log, 0.0)
        logits = decay_beta_ref[rows[c], :heads]
        delta_decay = delta_log * (-scale_ref[...]) * sigmoid(logits)
        delta_beta = tails[:, heads:] * (1.0 - beta)
        rest = jnp.zeros((CHUNK, LANES - 2 * heads), F32)
        delta_query_key_ref[rows[c], 2 * key_heads * DK :] = jnp.concatenate(
            [delta_decay, delta_beta, rest], axis=1
        ).astype(BF16)


def chain_forward_kernel(totals_ref, states_ref):
    devices, heads = totals_ref.shape[0], totals_ref.shape[1]
    for h in range(heads):
        state = jnp.zeros(states_ref.shape[2:], F32)
        for i in range(devices):
            states_ref[i, h] = state.astype(BF16)
            if i < devices - 1:
                step = totals_ref[i, h]
                high = state.astype(BF16)
                low = state - high.astype(F32)
                state = (
                    dot(step[:, :DK], high) + dot(step[:, :DK], low) + step[:, DK:].astype(F32)
                )


def chain_backward_kernel(totals_ref, deltas_ref, states_ref):
    devices, heads = totals_ref.shape[0], totals_ref.shape[1]
    for h in range(heads):
        state = jnp.zeros(states_ref.shape[2:], F32)
        for i in reversed(range(devices)):
            states_ref[i, h] = state.astype(BF16)
            if i > 0:
                step = totals_ref[i, h]
                high = state.astype(BF16)
                low = state - high.astype(F32)
                state = (
                    dot(step[:, :DK], high, TN)
                    + dot(step[:, :DK], low, TN)
                    + deltas_ref[i, h].astype(F32)
                )


PARAMS = pltpu.CompilerParams(
    dimension_semantics=("arbitrary",), vmem_limit_bytes=56 * 1024 * 1024
)
INTERPRET = False


def whole(shape):
    return pl.BlockSpec(shape, lambda c: (0,) * len(shape))


def run_forward(query_key, value, decay_beta, bias, scale, resets):
    tokens, heads = query_key.shape[1], bias.shape[1]
    chunks = tokens // CHUNK
    spans = min(FORWARD_SPANS, chunks)
    step = spans * CHUNK
    key_width, value_width = query_key.shape[2], heads * DV
    return pl.pallas_call(
        forward_kernel,
        grid=(chunks // spans,),
        in_specs=[
            pl.BlockSpec((2, step, key_width), lambda c: (0, c, 0)),
            pl.BlockSpec((step, value_width), lambda c: (c, 0)),
            pl.BlockSpec((step, 2 * heads), lambda c: (c, 0)),
            whole((1, heads)),
            whole((1, heads)),
            pl.BlockSpec((spans, 1, CHUNK), lambda c: (c, 0, 0)),
        ],
        out_specs=[
            pl.BlockSpec((spans, heads, CHUNK, CHUNK), lambda c: (c, 0, 0, 0)),
            pl.BlockSpec((spans, heads, DK, DK + DV), lambda c: (c, 0, 0, 0)),
            pl.BlockSpec((step, value_width), lambda c: (c, 0)),
            pl.BlockSpec((step, value_width), lambda c: (c, 0)),
            whole((heads, DK, DK + DV)),
        ],
        out_shape=[
            jax.ShapeDtypeStruct((chunks, heads, CHUNK, CHUNK), BF16),
            jax.ShapeDtypeStruct((chunks, heads, DK, DK + DV), BF16),
            jax.ShapeDtypeStruct((tokens, value_width), BF16),
            jax.ShapeDtypeStruct((tokens, value_width), F32),
            jax.ShapeDtypeStruct((heads, DK, DK + DV), BF16),
        ],
        scratch_shapes=[pltpu.VMEM((heads, DK, DK + DV), F32)],
        compiler_params=PARAMS,
        interpret=INTERPRET,
        name="forward_blocks",
    )(query_key, value, decay_beta, bias, scale, resets)


def run_output(local, reach, gate, delta_hidden, state_in, gain):
    tokens, value_width = local.shape
    heads = value_width // DV
    chunks = tokens // CHUNK
    block = pl.BlockSpec((CHUNK, value_width), lambda c: (c, 0))
    return pl.pallas_call(
        output_kernel,
        grid=(chunks,),
        in_specs=[
            block,
            block,
            block,
            block,
            whole((heads, DK, DV)),
            whole((1, DV)),
        ],
        out_specs=[block, block, block, whole((heads, DK, DV))],
        out_shape=[
            jax.ShapeDtypeStruct((tokens, value_width), BF16),
            jax.ShapeDtypeStruct((tokens, value_width), BF16),
            jax.ShapeDtypeStruct((tokens, value_width), BF16),
            jax.ShapeDtypeStruct((heads, DK, DV), BF16),
        ],
        scratch_shapes=[pltpu.VMEM((heads, DK, DV), F32)],
        compiler_params=PARAMS,
        interpret=INTERPRET,
        name="gated_norm",
    )(local, reach, gate, delta_hidden, state_in, gain)


def run_backward(
    query_key, value, decay_beta, bias, scale, resets, solve, starts, state_in, delta_out, final
):
    tokens, heads = query_key.shape[1], bias.shape[1]
    chunks = tokens // CHUNK
    spans = min(BACKWARD_SPANS, chunks)
    step = spans * CHUNK
    key_width, value_width = query_key.shape[2], heads * DV
    last = chunks // spans - 1
    return pl.pallas_call(
        backward_kernel,
        grid=(chunks // spans,),
        in_specs=[
            pl.BlockSpec((2, step, key_width), lambda c: (0, last - c, 0)),
            pl.BlockSpec((step, value_width), lambda c: (last - c, 0)),
            pl.BlockSpec((step, 2 * heads), lambda c: (last - c, 0)),
            whole((1, heads)),
            whole((1, heads)),
            pl.BlockSpec((spans, 1, CHUNK), lambda c: (last - c, 0, 0)),
            pl.BlockSpec((spans, heads, CHUNK, CHUNK), lambda c: (last - c, 0, 0, 0)),
            pl.BlockSpec((spans, heads, DK, DK + DV), lambda c: (last - c, 0, 0, 0)),
            whole((heads, DK, DV)),
            pl.BlockSpec((step, value_width), lambda c: (last - c, 0)),
            whole((heads, DK, DV)),
        ],
        out_specs=[
            pl.BlockSpec((step, 2 * key_width + LANES), lambda c: (last - c, 0)),
            pl.BlockSpec((step, value_width), lambda c: (last - c, 0)),
        ],
        out_shape=[
            jax.ShapeDtypeStruct((tokens, 2 * key_width + LANES), BF16),
            jax.ShapeDtypeStruct((tokens, value_width), BF16),
        ],
        scratch_shapes=[pltpu.VMEM((heads, DK, DV), F32)],
        compiler_params=PARAMS,
        interpret=INTERPRET,
        name="backward_blocks",
    )(query_key, value, decay_beta, bias, scale, resets, solve, starts, state_in, delta_out, final)


def spread(array, devices):
    heads, depth, width = array.shape
    if heads >= devices:
        return array.reshape(devices, heads // devices, depth, width)
    cuts = devices // heads
    parts = array.reshape(heads, depth, cuts, width // cuts)
    return jnp.transpose(parts, (0, 2, 1, 3)).reshape(devices, 1, depth, width // cuts)


def gather_parts(parts, heads):
    devices, each, depth, width = parts.shape
    if heads >= devices:
        return parts.reshape(heads, depth, width)
    cuts = devices // heads
    parts = parts.reshape(heads, cuts, depth, width)
    return jnp.transpose(parts, (0, 2, 1, 3)).reshape(heads, depth, cuts * width)


def swap(parts):
    return lax.all_to_all(parts, "ctx", split_axis=0, concat_axis=0, tiled=True)


def spread_totals(totals):
    devices, heads = lax.axis_size("ctx"), totals.shape[0]
    if heads >= devices:
        return spread(totals, devices)
    maps = jnp.repeat(totals[:, :, :DK], devices // heads, axis=0)[:, None]
    return jnp.concatenate([maps, spread(totals[:, :, DK:], devices)], axis=-1)


def run_chain_forward(held):
    return pl.pallas_call(
        chain_forward_kernel,
        out_shape=jax.ShapeDtypeStruct((*held.shape[:3], held.shape[3] - DK), BF16),
        interpret=INTERPRET,
        name="chain_forward",
    )(held)


def run_chain_backward(held, deltas):
    return pl.pallas_call(
        chain_backward_kernel,
        out_shape=jax.ShapeDtypeStruct(deltas.shape, BF16),
        interpret=INTERPRET,
        name="chain_backward",
    )(held, deltas)


def product(spec, a, b):
    return jnp.einsum(spec, a, b, preferred_element_type=F32)


def rows_of(small_weight_ref):
    return jnp.concatenate([small_weight_ref[0].astype(F32), small_weight_ref[1].astype(F32)], axis=0)


def projection_kernel(
    inputs_ref,
    query_key_weight_ref,
    value_weight_ref,
    decay_beta_weight_ref,
    query_key_ref,
    value_ref,
    decay_beta_ref,
):
    inputs = inputs_ref[...]
    query_key_ref[0] = dot(inputs, query_key_weight_ref[0])
    value_ref[...] = dot(inputs, value_weight_ref[0])

    @pl.when(pl.program_id(0) == 0)
    def _():
        decay_beta_ref[...] = dot(inputs, rows_of(decay_beta_weight_ref), NT)


def run_projection(inputs, query_key_weight, value_gate_weight, decay_beta_weight):
    tokens, model = inputs.shape
    key_width, value_width = query_key_weight.shape[2], value_gate_weight.shape[2]
    heads = decay_beta_weight.shape[1]
    steps = 4
    keys, values = 2 * key_width // steps, value_width // steps
    return pl.pallas_call(
        projection_kernel,
        grid=(steps,),
        in_specs=[
            whole((tokens, model)),
            pl.BlockSpec((1, model, keys), lambda j: (j // 2, 0, j % 2)),
            pl.BlockSpec((1, model, values), lambda j: (0, 0, j)),
            whole((2, heads, model)),
        ],
        out_specs=[
            pl.BlockSpec((1, tokens, keys), lambda j: (j // 2, 0, j % 2)),
            pl.BlockSpec((tokens, values), lambda j: (0, j)),
            whole((tokens, 2 * heads)),
        ],
        out_shape=[
            jax.ShapeDtypeStruct((2, tokens, key_width), F32),
            jax.ShapeDtypeStruct((tokens, value_width), F32),
            jax.ShapeDtypeStruct((tokens, 2 * heads), F32),
        ],
        compiler_params=PARAMS,
        interpret=INTERPRET,
        name="projection",
    )(inputs, query_key_weight, value_gate_weight, decay_beta_weight)


def input_gradient_kernel(
    delta_query_key_ref,
    delta_value_ref,
    delta_gate_ref,
    query_key_weight_ref,
    value_gate_weight_ref,
    decay_beta_weight_ref,
    out_ref,
):
    width = query_key_weight_ref.shape[2]
    heads = decay_beta_weight_ref.shape[1]
    keys = jnp.concatenate([query_key_weight_ref[0], query_key_weight_ref[1]], axis=1)
    small = delta_query_key_ref[:, 2 * width : 2 * width + 2 * heads]
    total = dot(delta_gate_ref[...], value_gate_weight_ref[1], NT)
    total += dot(delta_value_ref[...], value_gate_weight_ref[0], NT)
    total += dot(delta_query_key_ref[:, : 2 * width], keys, NT)
    total += dot(small, rows_of(decay_beta_weight_ref))
    out_ref[...] = total.astype(BF16)


def run_input_gradient(
    delta_query_key, delta_value, delta_gate, query_key_weight, value_gate_weight, decay_beta_weight
):
    tokens, model = delta_value.shape[0], query_key_weight.shape[1]
    cut = 512

    def weight(array):
        return pl.BlockSpec((2, cut, array.shape[2]), lambda j: (0, j, 0))

    return pl.pallas_call(
        input_gradient_kernel,
        grid=(model // cut,),
        in_specs=[
            whole(delta_query_key.shape),
            whole(delta_value.shape),
            whole(delta_gate.shape),
            weight(query_key_weight),
            weight(value_gate_weight),
            pl.BlockSpec((2, decay_beta_weight.shape[1], cut), lambda j: (0, 0, j)),
        ],
        out_specs=pl.BlockSpec((tokens, cut), lambda j: (0, j)),
        out_shape=jax.ShapeDtypeStruct((tokens, model), BF16),
        compiler_params=PARAMS,
        interpret=INTERPRET,
        name="input_gradient",
    )(delta_query_key, delta_value, delta_gate, query_key_weight, value_gate_weight, decay_beta_weight)


def together(*arrays):
    return lax.optimization_barrier(arrays)


def exchange(array, distance):
    devices = range(lax.axis_size("ctx"))
    return lax.ppermute(array, "ctx", [(i, i ^ distance) for i in devices])


def block_of(step, place, flip):
    x, y = (place // 2) % 2, place // 4
    core = lax.rem(place + flip, 2)
    across_x, across_y = 1 - step // 2, 1 - step % 2
    target_x, target_y = lax.rem(x + across_x, 2), lax.rem(y + across_y, 2)
    return target_y * 4 + target_x * 2 + core


def send_kernel(place_ref, left_a_ref, a_ref, left_b_ref, b_ref, a_out_ref, b_out_ref):
    a_out_ref[...] = dot(left_a_ref[...], a_ref[...], TN).astype(BF16)
    b_out_ref[...] = dot(left_b_ref[...], b_ref[...], TN).astype(BF16)


def keep_kernel(place_ref, *refs):
    lefts_a, a_ref, lefts_b, b_ref = refs[:4], refs[4], refs[5:9], refs[9]
    a_arrived_ref, b_arrived_ref = refs[10:12]
    out_refs = refs[12:]
    rows = lefts_a[0].shape[1]
    for i in range(4):
        at = slice(i * rows, (i + 1) * rows)
        a = dot(lefts_a[i][...], a_ref[...], TN) + a_arrived_ref[at].astype(F32)
        b = dot(lefts_b[i][...], b_ref[...], TN) + b_arrived_ref[at].astype(F32)
        out_refs[i][...] = a.astype(BF16)
        out_refs[4 + i][...] = b.astype(BF16)


def at_start(array):
    return pl.BlockSpec(array.shape, lambda i, place: (0, 0))


def pair_specs(left_a, a, left_b, b, flip):
    def rows(left, k):
        return pl.BlockSpec(
            (left.shape[0], left.shape[1] // 8), lambda i, place: (0, block_of(k, place[0], flip))
        )

    return [
        *[rows(left_a, k) for k in range(4)],
        at_start(a),
        *[rows(left_b, k) for k in range(4)],
        at_start(b),
    ]


def step_specs(left_a, a, left_b, b, flip):
    def rows(left):
        return pl.BlockSpec(
            (left.shape[0], left.shape[1] // 8), lambda i, place: (0, block_of(i, place[0], flip))
        )

    def full(delta):
        return pl.BlockSpec(delta.shape, lambda i, place: (0, 0))

    return [rows(left_a), full(a), rows(left_b), full(b)]


def halving_start(place, left_a, a, left_b, b):
    rows = left_a.shape[1] // 8
    return pl.pallas_call(
        send_kernel,
        grid_spec=pltpu.PrefetchScalarGridSpec(
            num_scalar_prefetch=1,
            grid=(4,),
            in_specs=step_specs(left_a, a, left_b, b, 1),
            out_specs=[
                pl.BlockSpec((rows, delta.shape[1]), lambda i, place: (i, 0)) for delta in (a, b)
            ],
        ),
        out_shape=[
            jax.ShapeDtypeStruct((4 * rows, delta.shape[1]), BF16) for delta in (a, b)
        ],
        compiler_params=PARAMS,
        interpret=INTERPRET,
        name="send_rows",
    )(place, left_a, a, left_b, b)


def halving_keep(place, left_a, a, left_b, b, a_arrived, b_arrived):
    rows = left_a.shape[1] // 8
    outs = [
        jax.ShapeDtypeStruct((rows, delta.shape[1]), BF16) for delta in (a, b) for _ in range(4)
    ]
    return pl.pallas_call(
        keep_kernel,
        grid_spec=pltpu.PrefetchScalarGridSpec(
            num_scalar_prefetch=1,
            grid=(1,),
            in_specs=pair_specs(left_a, a, left_b, b, 0)
            + [at_start(a_arrived), at_start(b_arrived)],
            out_specs=[at_start(out) for out in outs],
        ),
        out_shape=outs,
        compiler_params=PARAMS,
        interpret=INTERPRET,
        name="keep_rows",
    )(place, *[left_a] * 4, a, *[left_b] * 4, b, a_arrived, b_arrived)


def summed(a, b):
    return (a.astype(F32) + b.astype(F32)).astype(BF16)


def halving_cross(pieces):
    return exchange(pieces[0], 2), exchange(pieces[4], 4)


def halving_stay(pieces):
    return exchange(pieces[1], 2), exchange(pieces[6], 4)


def halving_last(pieces, arrived):
    a, b = pieces[:4], pieces[4:]
    return exchange(summed(a[2], arrived[0]), 4), exchange(summed(b[1], arrived[1]), 2)


def halving_terms(pieces, stay, last):
    return (pieces[3], stay[0], last[0]), (pieces[7], stay[1], last[1])


def finish_kernel(key_width, heads, *refs):
    def total(*terms):
        return sum(term[...].astype(F32) for term in terms)

    query_key_ref, value_gate_ref, decay_beta_ref = refs[7:]
    value_gate_ref[0] = total(*refs[0:2])
    value_gate_ref[1] = total(*refs[2:5])
    packed = total(*refs[5:7])
    query_key_ref[0] = packed[:, :key_width]
    query_key_ref[1] = packed[:, key_width : 2 * key_width]
    small = packed[:, 2 * key_width :].T
    decay_beta_ref[0] = small[:heads]
    decay_beta_ref[1] = small[heads : 2 * heads]


def run_finish(key_width, heads, value, gate, packed):
    rows, width = value[0].shape
    step = 128

    def block(array):
        return pl.BlockSpec((step, array.shape[1]), lambda i: (i, 0))

    def pair(size):
        return pl.BlockSpec((2, step, size), lambda i: (0, i, 0))

    terms = [*value, *gate, *packed]
    return pl.pallas_call(
        functools.partial(finish_kernel, key_width, heads),
        grid=(rows // step,),
        in_specs=[block(term) for term in terms],
        out_specs=[
            pair(key_width),
            pair(width),
            pl.BlockSpec((2, heads, step), lambda i: (0, 0, i)),
        ],
        out_shape=[
            jax.ShapeDtypeStruct((2, rows, key_width), F32),
            jax.ShapeDtypeStruct((2, rows, width), F32),
            jax.ShapeDtypeStruct((2, heads, rows), F32),
        ],
        compiler_params=PARAMS,
        interpret=INTERPRET,
        name="finish",
    )(*terms)


def scatter(partial, axis, dimension):
    return lax.psum_scatter(partial.astype(BF16), axis, scatter_dimension=dimension, tiled=True)


def body(
    inputs,
    query_key_weight,
    value_gate_weight,
    decay_beta_weight,
    beta_bias,
    decay_scale,
    norm_gain,
    out_weight,
    boundaries,
    grad_mixed,
):
    tokens, heads = inputs.shape[0], beta_bias.shape[0]
    key_width = query_key_weight.shape[2]
    cubic = lax.axis_size("ctx") == 8
    small_weight = jnp.swapaxes(decay_beta_weight, 1, 2)
    query_key, value, decay_beta = run_projection(
        inputs, query_key_weight, value_gate_weight, small_weight
    )
    bias, scale = beta_bias.reshape(1, heads), decay_scale.reshape(1, heads)
    resets = boundaries.reshape(tokens // CHUNK, 1, CHUNK)
    solve, starts, reach, local, totals = run_forward(
        query_key, value, decay_beta, bias, scale, resets
    )

    held = swap(spread_totals(totals))
    gate = product("td,df->tf", inputs, value_gate_weight[1]).astype(BF16)
    held, gate = together(held, gate)
    states = swap(run_chain_forward(held))
    delta_hidden = product("td,fd->tf", grad_mixed, out_weight).astype(BF16)
    states, delta_hidden = together(states, delta_hidden)
    state_in = gather_parts(states, heads)
    hidden, delta_gate, delta_out, delta_state = run_output(
        local, reach, gate, delta_hidden, state_in, norm_gain.reshape(1, DV)
    )

    deltas = swap(spread(delta_state, lax.axis_size("ctx")))
    partial_out = product("tf,fd->td", hidden, out_weight).astype(BF16)
    deltas, partial_out = together(deltas, partial_out)
    mixed = scatter(partial_out, "head", 1)
    finals = swap(run_chain_backward(held, deltas))
    if cubic:
        place = lax.axis_index("ctx").astype(jnp.int32).reshape(1)
        early = (place, inputs, delta_gate, grad_mixed, hidden)
        sent = halving_start(*early)
        arrived = [exchange(part, 1) for part in sent]
        early_pieces = halving_keep(*early, *arrived)
        finals, early_pieces = together(finals, early_pieces)
        early_arrived = halving_cross(early_pieces)
        early_stay = halving_stay(early_pieces)
    delta_final = gather_parts(finals, heads)
    delta_query_key, delta_value = run_backward(
        query_key,
        value,
        decay_beta,
        bias,
        scale,
        resets,
        solve,
        starts,
        state_in,
        delta_out,
        delta_final,
    )
    if cubic:
        delta_value, early_arrived = together(delta_value, early_arrived)
        early_last = halving_last(early_pieces, early_arrived)
        late = (place, inputs, delta_value, inputs, delta_query_key)
        sent = halving_start(*late)
        sent, early_stay = together(sent, early_stay)
        arrived = [exchange(part, 1) for part in sent]
    grad_rows = run_input_gradient(
        delta_query_key,
        delta_value,
        delta_gate,
        query_key_weight,
        value_gate_weight,
        small_weight,
    )
    if cubic:
        grad_rows, arrived, early_last = together(grad_rows, arrived, early_last)
    grad_inputs = scatter(grad_rows, "head", 1)
    if cubic:
        late_pieces = halving_keep(*late, *arrived)
        late_arrived = halving_cross(late_pieces)
        late_stay = halving_stay(late_pieces)
        late_last = halving_last(late_pieces, late_arrived)
        gate_terms, out_terms = halving_terms(early_pieces, early_stay, early_last)
        value_terms, packed_terms = halving_terms(late_pieces, late_stay, late_last)
        value_terms = (value_terms[0].astype(F32) + value_terms[1].astype(F32), value_terms[2])
        packed_terms = (packed_terms[0].astype(F32) + packed_terms[1].astype(F32), packed_terms[2])
        grad_out = sum(term.astype(F32) for term in out_terms).T
        grad_query_key, grad_value_gate, grad_decay_beta = run_finish(
            key_width, heads, value_terms, gate_terms, packed_terms
        )
        grad_decay_beta = jnp.swapaxes(grad_decay_beta, 1, 2)
    else:
        grad_gate = scatter(product("td,tf->df", inputs, delta_gate), "ctx", 0).astype(F32)
        grad_out = scatter(product("tf,td->fd", hidden, grad_mixed), "ctx", 1).astype(F32)
        grad_value = scatter(product("td,tf->df", inputs, delta_value), "ctx", 0).astype(F32)
        packed = scatter(product("td,tf->df", inputs, delta_query_key), "ctx", 0).astype(F32)
        rest = packed[:, 2 * key_width :]
        grad_query_key = jnp.stack([packed[:, :key_width], packed[:, key_width : 2 * key_width]])
        grad_value_gate = jnp.stack([grad_value, grad_gate])
        grad_decay_beta = jnp.stack([rest[:, :heads], rest[:, heads : 2 * heads]])
    return (mixed, grad_inputs, grad_query_key, grad_value_gate, grad_decay_beta, grad_out)


def solution(mesh):
    in_specs = (
        P("ctx", None),
        P(None, None, "head"),
        P(None, None, "head"),
        P(None, None, "head"),
        P("head"),
        P("head"),
        P(),
        P("head", None),
        P("ctx"),
        P("ctx", None),
    )
    out_specs = (
        P("ctx", "head"),
        P("ctx", "head"),
        P(None, "ctx", "head"),
        P(None, "ctx", "head"),
        P(None, "ctx", "head"),
        P("head", "ctx"),
    )
    return jax.shard_map(body, mesh=mesh, in_specs=in_specs, out_specs=out_specs, check_vma=False)
```

```python
import functools

import jax
import jax.numpy as jnp
from jax import lax
from jax.experimental import pallas as pl
from jax.experimental.pallas import tpu as pltpu
from jax.sharding import PartitionSpec as P

DK = 128
DV = 128
CHUNK = 128
EPS = 1e-06
QUERY_SCALE = DK ** (-0.5)
LANES = 128
FORWARD_SPANS = 2
BACKWARD_SPANS = 2

F32 = jnp.float32
BF16 = jnp.bfloat16
NN = ((1,), (0,))
NT = ((1,), (1,))
TN = ((0,), (0,))


def dot(a, b, dims=NN):
    return lax.dot_general(
        a.astype(BF16), b.astype(BF16), (dims, ((), ())), preferred_element_type=F32
    )


def exact(a, b, dims=NN):
    return lax.dot_general(
        a, b, (dims, ((), ())), precision=lax.Precision.HIGHEST, preferred_element_type=F32
    )


def softplus(x):
    return jnp.maximum(x, 0.0) + jnp.log1p(jnp.exp(-jnp.abs(x)))


def sigmoid(x):
    return 1.0 / (1.0 + jnp.exp(-x))


def row_sum(x):
    return jnp.sum(x, axis=-1, keepdims=True)


def grid_of(size):
    row = lax.broadcasted_iota(jnp.int32, (size, size), 0)
    col = lax.broadcasted_iota(jnp.int32, (size, size), 1)
    return row, col


def decays(decay_beta, bias_ref, scale_ref, resets):
    row, col = grid_of(CHUNK)
    lower = (row >= col).astype(F32)
    heads = bias_ref.shape[1]
    decay_logit = decay_beta[:, :heads]
    beta = sigmoid(decay_beta[:, heads:] + bias_ref[...])
    log_decay = -scale_ref[...] * softplus(decay_logit)
    resets = jnp.broadcast_to(resets.astype(F32), (8, CHUNK))
    doc_row = dot(resets, lower, NT)[0:1]
    doc_col = dot(lower, resets, NT)[:, 0:1]
    cum_col = exact(lower, log_decay)
    cum_row = exact(log_decay, lower, ((0,), (1,)))
    same = (doc_col == doc_row) & (row >= col)
    start = jnp.where(doc_col == 0.0, jnp.exp(cum_col), 0.0)
    last = CHUNK - 1
    end = jnp.where(
        doc_col == doc_col[last:],
        jnp.exp(jnp.minimum(cum_col[last:] - cum_col, 0.0)),
        0.0,
    )
    return beta, cum_col, cum_row, same, start, end, start[last:], resets


def pair_decay(cum_col, cum_row, same, h):
    gap = jnp.minimum(spread_column(cum_col, h) - cum_row[h : h + 1, :], 0.0)
    return jnp.where(same, jnp.exp(gap), 0.0)


def spread_column(columns, h):
    return jnp.broadcast_to(columns[:, h : h + 1], (columns.shape[0], LANES))


def unit_rows(x):
    inverse = lax.rsqrt(row_sum(x * x) + EPS)
    return x * inverse, inverse


def forward_kernel(
    query_key_ref,
    value_ref,
    decay_beta_ref,
    bias_ref,
    scale_ref,
    resets_ref,
    solve_ref,
    start_ref,
    map_ref,
    local_ref,
    total_ref,
    state_ref,
):
    heads = state_ref.shape[0]
    key_heads = query_key_ref.shape[2] // DK
    repeat = heads // key_heads
    spans = solve_ref.shape[0]
    row, col = grid_of(CHUNK)

    @pl.when(pl.program_id(0) == 0)
    def _():
        first = jnp.concatenate([(row == col).astype(F32), jnp.zeros((DK, DV), F32)], axis=1)
        for h in range(heads):
            state_ref[h] = first

    strict = row > col
    differ = row ^ col
    rows = [slice(c * CHUNK, (c + 1) * CHUNK) for c in range(spans)]
    each = [(c, h) for c in range(spans) for h in range(heads)]
    terms = [
        decays(decay_beta_ref[rows[c]], bias_ref, scale_ref, resets_ref[c]) for c in range(spans)
    ]
    keys, queries = {}, {}
    for c in range(spans):
        for g in range(key_heads):
            cols = slice(g * DK, (g + 1) * DK)
            queries[c, g] = unit_rows(query_key_ref[0, rows[c], cols])[0] * QUERY_SCALE
            keys[c, g] = unit_rows(query_key_ref[1, rows[c], cols])[0]
    grams = {p: (dot(keys[p], keys[p], NT), dot(queries[p], keys[p], NT)) for p in keys}
    scores, systems, betas, starts = {}, {}, {}, {}
    for c, h in each:
        beta, cum_col, cum_row, same, start = terms[c][:5]
        betas[c, h] = spread_column(beta, h)
        starts[c, h] = spread_column(start, h)
        decay = pair_decay(cum_col, cum_row, same, h)
        key_gram, query_gram = grams[c, h // repeat]
        scores[c, h] = (decay * query_gram).astype(BF16)
        systems[c, h] = jnp.where(strict, betas[c, h] * decay * key_gram, 0.0)
    identity = (row == col).astype(F32)
    inverse = {
        p: (identity - jnp.where(differ == 1, systems[p], 0.0)).astype(BF16) for p in each
    }
    level = 1
    while (1 << level) < CHUNK:
        here = (differ >> level) == 1
        inner = {
            p: dot(jnp.where(here, systems[p], 0.0), inverse[p]).astype(BF16) for p in each
        }
        inverse = {p: inverse[p] - dot(inverse[p], inner[p]).astype(BF16) for p in each}
        level += 1
    weights = {}
    for c, h in each:
        k = keys[c, h // repeat]
        v = value_ref[rows[c], h * DV : (h + 1) * DV].astype(F32)
        b = betas[c, h]
        right = jnp.concatenate([(b * starts[c, h]) * k, b * v], axis=1)
        weights[c, h] = dot(inverse[c, h], right)
        solve_ref[c, h] = inverse[c, h]
    for c in range(spans):
        end, total = terms[c][5:7]
        values = []
        for h in range(heads):
            state = state_ref[h].astype(BF16)
            start_ref[c, h] = state
            solved = weights[c, h]
            base = jnp.concatenate([jnp.zeros((CHUNK, DK), F32), solved[:, DK:]], axis=1)
            values.append((base - dot(solved[:, :DK], state)).astype(BF16))
        for h in range(heads):
            k, q = keys[c, h // repeat], queries[c, h // repeat]
            state = state_ref[h]
            out = dot(starts[c, h] * q, state) + dot(scores[c, h], values[h])
            map_ref[rows[c], h * DK : (h + 1) * DK] = out[:, :DK].astype(BF16)
            local_ref[rows[c], h * DV : (h + 1) * DV] = out[:, DK:].astype(BF16)
            state = total[:, h : h + 1] * state + dot(spread_column(end, h) * k, values[h], TN)
            state_ref[h] = state
            total_ref[h] = state.astype(BF16)


def output_kernel(
    local_ref,
    map_ref,
    gate_ref,
    delta_ref,
    state_ref,
    gain_ref,
    hidden_ref,
    delta_gate_ref,
    delta_out_ref,
    delta_state_ref,
    total_ref,
):
    heads = state_ref.shape[0]
    gain = gain_ref[...]

    @pl.when(pl.program_id(0) == 0)
    def _():
        total_ref[...] = jnp.zeros_like(total_ref)

    outs, deltas = [], []
    for h in range(heads):
        cols = slice(h * DV, (h + 1) * DV)
        outs.append(local_ref[:, cols].astype(F32) + dot(map_ref[:, cols], state_ref[h]))
    for h in range(heads):
        cols = slice(h * DV, (h + 1) * DV)
        out = outs[h]
        gate = gate_ref[:, cols].astype(F32)
        delta = delta_ref[:, cols].astype(F32)
        scale = lax.rsqrt(row_sum(out * out) * (1.0 / DV) + EPS)
        normed = out * scale
        share = sigmoid(gate)
        silu = gate * share
        scaled = normed * gain
        hidden_ref[:, cols] = (scaled * silu).astype(BF16)
        delta_gate_ref[:, cols] = (
            delta * scaled * (share * (1.0 + gate * (1.0 - share)))
        ).astype(BF16)
        delta_normed = delta * gain * silu
        delta_out = scale * (
            delta_normed - normed * (row_sum(normed * delta_normed) * (1.0 / DV))
        )
        delta_out = delta_out.astype(BF16)
        delta_out_ref[:, cols] = delta_out
        deltas.append(delta_out)
    for h in range(heads):
        cols = slice(h * DV, (h + 1) * DV)
        part = total_ref[h] + dot(map_ref[:, cols], deltas[h], TN)
        total_ref[h] = part
        delta_state_ref[h] = part.astype(BF16)


def backward_kernel(
    query_key_ref,
    value_ref,
    decay_beta_ref,
    bias_ref,
    scale_ref,
    resets_ref,
    solve_ref,
    start_ref,
    state_in_ref,
    delta_out_ref,
    delta_final_ref,
    delta_query_key_ref,
    delta_value_ref,
    carry_ref,
):
    heads = carry_ref.shape[0]
    key_heads = query_key_ref.shape[2] // DK
    repeat = heads // key_heads
    spans = solve_ref.shape[0]
    row, col = grid_of(CHUNK)

    @pl.when(pl.program_id(0) == 0)
    def _():
        carry_ref[...] = delta_final_ref[...].astype(F32)

    strict = row > col
    upper = (row <= col).astype(F32)
    identity = (row == col).astype(F32)
    rows = [slice(c * CHUNK, (c + 1) * CHUNK) for c in range(spans)]
    cols = [slice(h * DV, (h + 1) * DV) for h in range(heads)]
    each = [(c, h) for c in reversed(range(spans)) for h in range(heads)]
    terms = [
        decays(decay_beta_ref[rows[c]], bias_ref, scale_ref, resets_ref[c]) for c in range(spans)
    ]
    half = lax.broadcasted_iota(jnp.int32, (2 * DK, 2 * heads), 0) // DK
    lane = lax.broadcasted_iota(jnp.int32, (2 * DK, 2 * heads), 1)
    lane_one = lax.broadcasted_iota(jnp.int32, (1, heads), 1)
    qs, ks, q_inv, k_inv = {}, {}, {}, {}
    for c in range(spans):
        for g in range(key_heads):
            at = slice(g * DK, (g + 1) * DK)
            q, q_inv[c, g] = unit_rows(query_key_ref[0, rows[c], at])
            qs[c, g] = q * QUERY_SCALE
            ks[c, g], k_inv[c, g] = unit_rows(query_key_ref[1, rows[c], at])
    grams = {p: (dot(ks[p], ks[p], NT), dot(qs[p], ks[p], NT)) for p in ks}
    state_of, value_of, right_of = {}, {}, {}
    betas, starts, ends = {}, {}, {}
    for c, h in each:
        before = start_ref[c, h]
        state = dot(before[:, :DK], state_in_ref[h]) + before[:, DK:].astype(F32)
        state_of[c, h] = state.astype(BF16)
    for c, h in each:
        beta, start, end = terms[c][0], terms[c][4], terms[c][5]
        seen = dot(ks[c, h // repeat], state_of[c, h])
        betas[c, h] = spread_column(beta, h)
        starts[c, h] = spread_column(start, h)
        ends[c, h] = spread_column(end, h)
        right_of[c, h] = betas[c, h] * (
            value_ref[rows[c], cols[h]].astype(F32) - starts[c, h] * seen
        )
    for c, h in each:
        value_of[c, h] = dot(solve_ref[c, h], right_of[c, h]).astype(BF16)
    decay_of, delta_value_of, delta_right_of = {}, {}, {}
    for c, h in each:
        decay_of[c, h] = pair_decay(terms[c][1], terms[c][2], terms[c][3], h)
        delta_value_of[c, h] = dot(
            decay_of[c, h] * grams[c, h // repeat][1], delta_out_ref[rows[c], cols[h]], TN
        )
    both_of, held_of, carry_of = {}, {}, {}
    for c in reversed(range(spans)):
        total = terms[c][6]
        for h in range(heads):
            carry_of[c, h] = carry_ref[h].astype(BF16)
            delta_value_of[c, h] += dot(ends[c, h] * ks[c, h // repeat], carry_of[c, h])
        for h in range(heads):
            delta_right_of[c, h] = dot(solve_ref[c, h], delta_value_of[c, h], TN)
        for h in range(heads):
            q, k = qs[c, h // repeat], ks[c, h // repeat]
            b, s = betas[c, h], starts[c, h]
            delta_right = delta_right_of[c, h]
            delta_value_ref[rows[c], cols[h]] = (b * delta_right).astype(BF16)
            both_of[c, h] = jnp.concatenate(
                [delta_out_ref[rows[c], cols[h]], delta_right.astype(BF16)], axis=0
            )
            carry = carry_ref[h]
            held_of[c, h] = total[:, h : h + 1] * row_sum(
                jnp.sum(state_of[c, h].astype(F32) * carry, axis=0, keepdims=True)
            )
            carry_ref[h] = total[:, h : h + 1] * carry + dot(
                jnp.concatenate([s * q, (-b * s) * k], axis=0), both_of[c, h], TN
            )
    pairs_of = {p: dot(both_of[p], value_of[p], NT) for p in each}
    states_of = {p: dot(both_of[p], state_of[p], NT) for p in each}
    ends_of = {p: ends[p] * dot(value_of[p], carry_of[p], NT) for p in each}
    pair_of, sum_of, tail_of, lower_of = {}, {}, {}, {}
    for c, h in each:
        q, k = qs[c, h // repeat], ks[c, h // repeat]
        key_gram, query_gram = grams[c, h // repeat]
        decay, b, s = decay_of[c, h], betas[c, h], starts[c, h]
        pair_q = decay * pairs_of[c, h][:CHUNK]
        pair_k = jnp.where(strict, (-b) * decay * pairs_of[c, h][CHUNK:], 0.0)
        cross = jnp.where(strict, pair_q * query_gram + pair_k * key_gram, 0.0).astype(BF16)
        pair_of[c, h] = (pair_q.astype(BF16), pair_k.astype(BF16))
        state_q = s * states_of[c, h][:CHUNK]
        state_k = (b * s) * states_of[c, h][CHUNK:]
        states_of[c, h] = (state_q, ends_of[c, h] - state_k)
        sum_of[c, h] = jnp.concatenate(
            [cross, (state_q * q - state_k * k).astype(BF16)], axis=1
        )
        tail_of[c, h] = jnp.concatenate(
            [ends_of[c, h] * k, delta_right_of[c, h] * value_of[c, h].astype(F32)], axis=1
        ).astype(BF16)
        lower_of[c, h] = jnp.sum(cross.astype(F32), axis=0, keepdims=True)
    for c in range(spans):
        for g in range(key_heads):
            q, k = qs[c, g], ks[c, g]
            both = jnp.concatenate([q, k], axis=0)
            delta_q = jnp.zeros((CHUNK, DK), F32)
            delta_k = jnp.zeros((CHUNK, DK), F32)
            for h in range(g * repeat, (g + 1) * repeat):
                pair_q, pair_k = pair_of[c, h]
                delta_q += dot(pair_q, k) + states_of[c, h][0]
                delta_k += (
                    dot(pair_k, k)
                    + dot(jnp.concatenate([pair_q, pair_k], axis=0), both, TN)
                    + states_of[c, h][1]
                )
            delta_q = delta_q * QUERY_SCALE
            unit = q * (1.0 / QUERY_SCALE)
            delta_q = q_inv[c, g] * (delta_q - unit * row_sum(unit * delta_q))
            delta_k = k_inv[c, g] * (delta_k - k * row_sum(k * delta_k))
            at, after = g * DK, (key_heads + g) * DK
            delta_query_key_ref[rows[c], at : at + DK] = delta_q.astype(BF16)
            delta_query_key_ref[rows[c], after : after + DK] = delta_k.astype(BF16)
    for c in range(spans):
        beta, resets = terms[c][0], terms[c][7]
        sums = jnp.zeros((CHUNK, 2 * heads), F32)
        tails = jnp.zeros((CHUNK, 2 * heads), F32)
        tail = jnp.zeros((1, heads), F32)
        for h in range(heads):
            sums += dot(sum_of[c, h], lane == h)
            tails += dot(tail_of[c, h], lane == h + heads * half)
            tail = jnp.where(lane_one == h, held_of[c, h], tail)
        below = [lower_of[c, h] for h in range(heads)]
        if heads % 8:
            below.append(jnp.zeros((-heads % 8, CHUNK), F32))
        below = exact(upper, jnp.concatenate(below, axis=0), NT)[:, :heads]
        ends_sum = tails[:, :heads]
        tail = tail + jnp.sum(ends_sum, axis=0, keepdims=True)
        delta_log = exact(upper, sums[:, :heads] - ends_sum) - below + tail
        reset_col = dot(identity, resets, NT)[:, 0:1]
        delta_log = jnp.where(reset_col == 0.0, delta_log, 0.0)
        logits = decay_beta_ref[rows[c], :heads]
        delta_decay = delta_log * (-scale_ref[...]) * sigmoid(logits)
        delta_beta = tails[:, heads:] * (1.0 - beta)
        rest = jnp.zeros((CHUNK, LANES - 2 * heads), F32)
        delta_query_key_ref[rows[c], 2 * key_heads * DK :] = jnp.concatenate(
            [delta_decay, delta_beta, rest], axis=1
        ).astype(BF16)


def chain_forward_kernel(totals_ref, states_ref):
    devices, heads = totals_ref.shape[0], totals_ref.shape[1]
    for h in range(heads):
        state = jnp.zeros(states_ref.shape[2:], F32)
        for i in range(devices):
            states_ref[i, h] = state.astype(BF16)
            if i < devices - 1:
                step = totals_ref[i, h]
                high = state.astype(BF16)
                low = state - high.astype(F32)
                state = (
                    dot(step[:, :DK], high) + dot(step[:, :DK], low) + step[:, DK:].astype(F32)
                )


def chain_backward_kernel(totals_ref, deltas_ref, states_ref):
    devices, heads = totals_ref.shape[0], totals_ref.shape[1]
    for h in range(heads):
        state = jnp.zeros(states_ref.shape[2:], F32)
        for i in reversed(range(devices)):
            states_ref[i, h] = state.astype(BF16)
            if i > 0:
                step = totals_ref[i, h]
                high = state.astype(BF16)
                low = state - high.astype(F32)
                state = (
                    dot(step[:, :DK], high, TN)
                    + dot(step[:, :DK], low, TN)
                    + deltas_ref[i, h].astype(F32)
                )


PARAMS = pltpu.CompilerParams(
    dimension_semantics=("arbitrary",), vmem_limit_bytes=56 * 1024 * 1024
)
INTERPRET = False


def whole(shape):
    return pl.BlockSpec(shape, lambda c: (0,) * len(shape))


def run_forward(query_key, value, decay_beta, bias, scale, resets):
    tokens, heads = query_key.shape[1], bias.shape[1]
    chunks = tokens // CHUNK
    spans = min(FORWARD_SPANS, chunks)
    step = spans * CHUNK
    key_width, value_width = query_key.shape[2], heads * DV
    return pl.pallas_call(
        forward_kernel,
        grid=(chunks // spans,),
        in_specs=[
            pl.BlockSpec((2, step, key_width), lambda c: (0, c, 0)),
            pl.BlockSpec((step, value_width), lambda c: (c, 0)),
            pl.BlockSpec((step, 2 * heads), lambda c: (c, 0)),
            whole((1, heads)),
            whole((1, heads)),
            pl.BlockSpec((spans, 1, CHUNK), lambda c: (c, 0, 0)),
        ],
        out_specs=[
            pl.BlockSpec((spans, heads, CHUNK, CHUNK), lambda c: (c, 0, 0, 0)),
            pl.BlockSpec((spans, heads, DK, DK + DV), lambda c: (c, 0, 0, 0)),
            pl.BlockSpec((step, value_width), lambda c: (c, 0)),
            pl.BlockSpec((step, value_width), lambda c: (c, 0)),
            whole((heads, DK, DK + DV)),
        ],
        out_shape=[
            jax.ShapeDtypeStruct((chunks, heads, CHUNK, CHUNK), BF16),
            jax.ShapeDtypeStruct((chunks, heads, DK, DK + DV), BF16),
            jax.ShapeDtypeStruct((tokens, value_width), BF16),
            jax.ShapeDtypeStruct((tokens, value_width), BF16),
            jax.ShapeDtypeStruct((heads, DK, DK + DV), BF16),
        ],
        scratch_shapes=[pltpu.VMEM((heads, DK, DK + DV), F32)],
        compiler_params=PARAMS,
        interpret=INTERPRET,
        name="forward_blocks",
    )(query_key, value, decay_beta, bias, scale, resets)


def run_output(local, reach, gate, delta_hidden, state_in, gain):
    tokens, value_width = local.shape
    heads = value_width // DV
    chunks = tokens // CHUNK
    block = pl.BlockSpec((CHUNK, value_width), lambda c: (c, 0))
    return pl.pallas_call(
        output_kernel,
        grid=(chunks,),
        in_specs=[
            block,
            block,
            block,
            block,
            whole((heads, DK, DV)),
            whole((1, DV)),
        ],
        out_specs=[block, block, block, whole((heads, DK, DV))],
        out_shape=[
            jax.ShapeDtypeStruct((tokens, value_width), BF16),
            jax.ShapeDtypeStruct((tokens, value_width), BF16),
            jax.ShapeDtypeStruct((tokens, value_width), BF16),
            jax.ShapeDtypeStruct((heads, DK, DV), BF16),
        ],
        scratch_shapes=[pltpu.VMEM((heads, DK, DV), F32)],
        compiler_params=PARAMS,
        interpret=INTERPRET,
        name="gated_norm",
    )(local, reach, gate, delta_hidden, state_in, gain)


def run_backward(
    query_key, value, decay_beta, bias, scale, resets, solve, starts, state_in, delta_out, final
):
    tokens, heads = query_key.shape[1], bias.shape[1]
    chunks = tokens // CHUNK
    spans = min(BACKWARD_SPANS, chunks)
    step = spans * CHUNK
    key_width, value_width = query_key.shape[2], heads * DV
    last = chunks // spans - 1
    return pl.pallas_call(
        backward_kernel,
        grid=(chunks // spans,),
        in_specs=[
            pl.BlockSpec((2, step, key_width), lambda c: (0, last - c, 0)),
            pl.BlockSpec((step, value_width), lambda c: (last - c, 0)),
            pl.BlockSpec((step, 2 * heads), lambda c: (last - c, 0)),
            whole((1, heads)),
            whole((1, heads)),
            pl.BlockSpec((spans, 1, CHUNK), lambda c: (last - c, 0, 0)),
            pl.BlockSpec((spans, heads, CHUNK, CHUNK), lambda c: (last - c, 0, 0, 0)),
            pl.BlockSpec((spans, heads, DK, DK + DV), lambda c: (last - c, 0, 0, 0)),
            whole((heads, DK, DV)),
            pl.BlockSpec((step, value_width), lambda c: (last - c, 0)),
            whole((heads, DK, DV)),
        ],
        out_specs=[
            pl.BlockSpec((step, 2 * key_width + LANES), lambda c: (last - c, 0)),
            pl.BlockSpec((step, value_width), lambda c: (last - c, 0)),
        ],
        out_shape=[
            jax.ShapeDtypeStruct((tokens, 2 * key_width + LANES), BF16),
            jax.ShapeDtypeStruct((tokens, value_width), BF16),
        ],
        scratch_shapes=[pltpu.VMEM((heads, DK, DV), F32)],
        compiler_params=PARAMS,
        interpret=INTERPRET,
        name="backward_blocks",
    )(query_key, value, decay_beta, bias, scale, resets, solve, starts, state_in, delta_out, final)


def spread(array, devices):
    heads, depth, width = array.shape
    if heads >= devices:
        return array.reshape(devices, heads // devices, depth, width)
    cuts = devices // heads
    parts = array.reshape(heads, depth, cuts, width // cuts)
    return jnp.transpose(parts, (0, 2, 1, 3)).reshape(devices, 1, depth, width // cuts)


def gather_parts(parts, heads):
    devices, each, depth, width = parts.shape
    if heads >= devices:
        return parts.reshape(heads, depth, width)
    cuts = devices // heads
    parts = parts.reshape(heads, cuts, depth, width)
    return jnp.transpose(parts, (0, 2, 1, 3)).reshape(heads, depth, cuts * width)


def swap(parts):
    return lax.all_to_all(parts, "ctx", split_axis=0, concat_axis=0, tiled=True)


def spread_totals(totals):
    devices, heads = lax.axis_size("ctx"), totals.shape[0]
    if heads >= devices:
        return spread(totals, devices)
    maps = jnp.repeat(totals[:, :, :DK], devices // heads, axis=0)[:, None]
    return jnp.concatenate([maps, spread(totals[:, :, DK:], devices)], axis=-1)


def run_chain_forward(held):
    return pl.pallas_call(
        chain_forward_kernel,
        out_shape=jax.ShapeDtypeStruct((*held.shape[:3], held.shape[3] - DK), BF16),
        interpret=INTERPRET,
        name="chain_forward",
    )(held)


def run_chain_backward(held, deltas):
    return pl.pallas_call(
        chain_backward_kernel,
        out_shape=jax.ShapeDtypeStruct(deltas.shape, BF16),
        interpret=INTERPRET,
        name="chain_backward",
    )(held, deltas)


def product(spec, a, b):
    return jnp.einsum(spec, a, b, preferred_element_type=F32)


def rows_of(small_weight_ref):
    return jnp.concatenate([small_weight_ref[0].astype(F32), small_weight_ref[1].astype(F32)], axis=0)


def projection_kernel(
    inputs_ref,
    query_key_weight_ref,
    value_weight_ref,
    decay_beta_weight_ref,
    query_key_ref,
    value_ref,
    decay_beta_ref,
):
    inputs = inputs_ref[...]
    query_key_ref[0] = dot(inputs, query_key_weight_ref[0])
    value_ref[...] = dot(inputs, value_weight_ref[0]).astype(BF16)

    @pl.when(pl.program_id(0) == 0)
    def _():
        decay_beta_ref[...] = dot(inputs, rows_of(decay_beta_weight_ref), NT)


def run_projection(inputs, query_key_weight, value_gate_weight, decay_beta_weight):
    tokens, model = inputs.shape
    key_width, value_width = query_key_weight.shape[2], value_gate_weight.shape[2]
    heads = decay_beta_weight.shape[1]
    steps = 4
    keys, values = 2 * key_width // steps, value_width // steps
    return pl.pallas_call(
        projection_kernel,
        grid=(steps,),
        in_specs=[
            whole((tokens, model)),
            pl.BlockSpec((1, model, keys), lambda j: (j // 2, 0, j % 2)),
            pl.BlockSpec((1, model, values), lambda j: (0, 0, j)),
            whole((2, heads, model)),
        ],
        out_specs=[
            pl.BlockSpec((1, tokens, keys), lambda j: (j // 2, 0, j % 2)),
            pl.BlockSpec((tokens, values), lambda j: (0, j)),
            whole((tokens, 2 * heads)),
        ],
        out_shape=[
            jax.ShapeDtypeStruct((2, tokens, key_width), F32),
            jax.ShapeDtypeStruct((tokens, value_width), BF16),
            jax.ShapeDtypeStruct((tokens, 2 * heads), F32),
        ],
        compiler_params=PARAMS,
        interpret=INTERPRET,
        name="projection",
    )(inputs, query_key_weight, value_gate_weight, decay_beta_weight)


def input_gradient_kernel(
    delta_query_key_ref,
    delta_value_ref,
    delta_gate_ref,
    query_key_weight_ref,
    value_gate_weight_ref,
    decay_beta_weight_ref,
    out_ref,
):
    width = query_key_weight_ref.shape[2]
    heads = decay_beta_weight_ref.shape[1]
    keys = jnp.concatenate([query_key_weight_ref[0], query_key_weight_ref[1]], axis=1)
    small = delta_query_key_ref[:, 2 * width : 2 * width + 2 * heads]
    total = dot(delta_gate_ref[...], value_gate_weight_ref[1], NT)
    total += dot(delta_value_ref[...], value_gate_weight_ref[0], NT)
    total += dot(delta_query_key_ref[:, : 2 * width], keys, NT)
    total += dot(small, rows_of(decay_beta_weight_ref))
    out_ref[...] = total.astype(BF16)


def run_input_gradient(
    delta_query_key, delta_value, delta_gate, query_key_weight, value_gate_weight, decay_beta_weight
):
    tokens, model = delta_value.shape[0], query_key_weight.shape[1]
    cut = 512

    def weight(array):
        return pl.BlockSpec((2, cut, array.shape[2]), lambda j: (0, j, 0))

    return pl.pallas_call(
        input_gradient_kernel,
        grid=(model // cut,),
        in_specs=[
            whole(delta_query_key.shape),
            whole(delta_value.shape),
            whole(delta_gate.shape),
            weight(query_key_weight),
            weight(value_gate_weight),
            pl.BlockSpec((2, decay_beta_weight.shape[1], cut), lambda j: (0, 0, j)),
        ],
        out_specs=pl.BlockSpec((tokens, cut), lambda j: (0, j)),
        out_shape=jax.ShapeDtypeStruct((tokens, model), BF16),
        compiler_params=PARAMS,
        interpret=INTERPRET,
        name="input_gradient",
    )(delta_query_key, delta_value, delta_gate, query_key_weight, value_gate_weight, decay_beta_weight)


def together(*arrays):
    return lax.optimization_barrier(arrays)


def exchange(array, distance):
    devices = range(lax.axis_size("ctx"))
    return lax.ppermute(array, "ctx", [(i, i ^ distance) for i in devices])


def block_of(step, place, flip):
    x, y = (place // 2) % 2, place // 4
    core = lax.rem(place + flip, 2)
    across_x, across_y = 1 - step // 2, 1 - step % 2
    target_x, target_y = lax.rem(x + across_x, 2), lax.rem(y + across_y, 2)
    return target_y * 4 + target_x * 2 + core


def send_kernel(place_ref, left_a_ref, a_ref, left_b_ref, b_ref, a_out_ref, b_out_ref):
    a_out_ref[...] = dot(left_a_ref[...], a_ref[...], TN).astype(BF16)
    b_out_ref[...] = dot(left_b_ref[...], b_ref[...], TN).astype(BF16)


def keep_kernel(place_ref, *refs):
    lefts_a, a_ref, lefts_b, b_ref = refs[:4], refs[4], refs[5:9], refs[9]
    a_arrived_ref, b_arrived_ref = refs[10:12]
    out_refs = refs[12:]
    rows = lefts_a[0].shape[1]
    for i in range(4):
        at = slice(i * rows, (i + 1) * rows)
        a = dot(lefts_a[i][...], a_ref[...], TN) + a_arrived_ref[at].astype(F32)
        b = dot(lefts_b[i][...], b_ref[...], TN) + b_arrived_ref[at].astype(F32)
        out_refs[i][...] = a.astype(BF16)
        out_refs[4 + i][...] = b.astype(BF16)


def at_start(array):
    return pl.BlockSpec(array.shape, lambda i, place: (0, 0))


def pair_specs(left_a, a, left_b, b, flip):
    def rows(left, k):
        return pl.BlockSpec(
            (left.shape[0], left.shape[1] // 8), lambda i, place: (0, block_of(k, place[0], flip))
        )

    return [
        *[rows(left_a, k) for k in range(4)],
        at_start(a),
        *[rows(left_b, k) for k in range(4)],
        at_start(b),
    ]


def step_specs(left_a, a, left_b, b, flip):
    def rows(left):
        return pl.BlockSpec(
            (left.shape[0], left.shape[1] // 8), lambda i, place: (0, block_of(i, place[0], flip))
        )

    def full(delta):
        return pl.BlockSpec(delta.shape, lambda i, place: (0, 0))

    return [rows(left_a), full(a), rows(left_b), full(b)]


def halving_start(place, left_a, a, left_b, b):
    rows = left_a.shape[1] // 8
    return pl.pallas_call(
        send_kernel,
        grid_spec=pltpu.PrefetchScalarGridSpec(
            num_scalar_prefetch=1,
            grid=(4,),
            in_specs=step_specs(left_a, a, left_b, b, 1),
            out_specs=[
                pl.BlockSpec((rows, delta.shape[1]), lambda i, place: (i, 0)) for delta in (a, b)
            ],
        ),
        out_shape=[
            jax.ShapeDtypeStruct((4 * rows, delta.shape[1]), BF16) for delta in (a, b)
        ],
        compiler_params=PARAMS,
        interpret=INTERPRET,
        name="send_rows",
    )(place, left_a, a, left_b, b)


def halving_keep(place, left_a, a, left_b, b, a_arrived, b_arrived):
    rows = left_a.shape[1] // 8
    outs = [
        jax.ShapeDtypeStruct((rows, delta.shape[1]), BF16) for delta in (a, b) for _ in range(4)
    ]
    return pl.pallas_call(
        keep_kernel,
        grid_spec=pltpu.PrefetchScalarGridSpec(
            num_scalar_prefetch=1,
            grid=(1,),
            in_specs=pair_specs(left_a, a, left_b, b, 0)
            + [at_start(a_arrived), at_start(b_arrived)],
            out_specs=[at_start(out) for out in outs],
        ),
        out_shape=outs,
        compiler_params=PARAMS,
        interpret=INTERPRET,
        name="keep_rows",
    )(place, *[left_a] * 4, a, *[left_b] * 4, b, a_arrived, b_arrived)


def summed(a, b):
    return (a.astype(F32) + b.astype(F32)).astype(BF16)


def halving_cross(pieces):
    return exchange(pieces[0], 2), exchange(pieces[4], 4)


def halving_stay(pieces):
    return exchange(pieces[1], 2), exchange(pieces[6], 4)


def halving_last(pieces, arrived):
    a, b = pieces[:4], pieces[4:]
    return exchange(summed(a[2], arrived[0]), 4), exchange(summed(b[1], arrived[1]), 2)


def halving_terms(pieces, stay, last):
    return (pieces[3], stay[0], last[0]), (pieces[7], stay[1], last[1])


def finish_kernel(key_width, heads, *refs):
    def total(*terms):
        return sum(term[...].astype(F32) for term in terms)

    query_key_ref, value_gate_ref, decay_beta_ref = refs[7:]
    value_gate_ref[0] = total(*refs[0:2])
    value_gate_ref[1] = total(*refs[2:5])
    packed = total(*refs[5:7])
    query_key_ref[0] = packed[:, :key_width]
    query_key_ref[1] = packed[:, key_width : 2 * key_width]
    small = packed[:, 2 * key_width :].T
    decay_beta_ref[0] = small[:heads]
    decay_beta_ref[1] = small[heads : 2 * heads]


def run_finish(key_width, heads, value, gate, packed):
    rows, width = value[0].shape
    step = 128

    def block(array):
        return pl.BlockSpec((step, array.shape[1]), lambda i: (i, 0))

    def pair(size):
        return pl.BlockSpec((2, step, size), lambda i: (0, i, 0))

    terms = [*value, *gate, *packed]
    return pl.pallas_call(
        functools.partial(finish_kernel, key_width, heads),
        grid=(rows // step,),
        in_specs=[block(term) for term in terms],
        out_specs=[
            pair(key_width),
            pair(width),
            pl.BlockSpec((2, heads, step), lambda i: (0, 0, i)),
        ],
        out_shape=[
            jax.ShapeDtypeStruct((2, rows, key_width), F32),
            jax.ShapeDtypeStruct((2, rows, width), F32),
            jax.ShapeDtypeStruct((2, heads, rows), F32),
        ],
        compiler_params=PARAMS,
        interpret=INTERPRET,
        name="finish",
    )(*terms)


def scatter(partial, axis, dimension):
    return lax.psum_scatter(partial.astype(BF16), axis, scatter_dimension=dimension, tiled=True)


def body(
    inputs,
    query_key_weight,
    value_gate_weight,
    decay_beta_weight,
    beta_bias,
    decay_scale,
    norm_gain,
    out_weight,
    boundaries,
    grad_mixed,
):
    tokens, heads = inputs.shape[0], beta_bias.shape[0]
    key_width = query_key_weight.shape[2]
    cubic = lax.axis_size("ctx") == 8
    small_weight = jnp.swapaxes(decay_beta_weight, 1, 2)
    query_key, value, decay_beta = run_projection(
        inputs, query_key_weight, value_gate_weight, small_weight
    )
    bias, scale = beta_bias.reshape(1, heads), decay_scale.reshape(1, heads)
    resets = boundaries.reshape(tokens // CHUNK, 1, CHUNK)
    solve, starts, reach, local, totals = run_forward(
        query_key, value, decay_beta, bias, scale, resets
    )

    held = swap(spread_totals(totals))
    gate = product("td,df->tf", inputs, value_gate_weight[1]).astype(BF16)
    held, gate = together(held, gate)
    states = swap(run_chain_forward(held))
    delta_hidden = product("td,fd->tf", grad_mixed, out_weight).astype(BF16)
    states, delta_hidden = together(states, delta_hidden)
    state_in = gather_parts(states, heads)
    hidden, delta_gate, delta_out, delta_state = run_output(
        local, reach, gate, delta_hidden, state_in, norm_gain.reshape(1, DV)
    )

    deltas = swap(spread(delta_state, lax.axis_size("ctx")))
    partial_out = product("tf,fd->td", hidden, out_weight).astype(BF16)
    deltas, partial_out = together(deltas, partial_out)
    mixed = scatter(partial_out, "head", 1)
    finals = swap(run_chain_backward(held, deltas))
    if cubic:
        place = lax.axis_index("ctx").astype(jnp.int32).reshape(1)
        early = (place, inputs, delta_gate, grad_mixed, hidden)
        sent = halving_start(*early)
        arrived = [exchange(part, 1) for part in sent]
        early_pieces = halving_keep(*early, *arrived)
        finals, early_pieces = together(finals, early_pieces)
        early_arrived = halving_cross(early_pieces)
        early_stay = halving_stay(early_pieces)
    delta_final = gather_parts(finals, heads)
    delta_query_key, delta_value = run_backward(
        query_key,
        value,
        decay_beta,
        bias,
        scale,
        resets,
        solve,
        starts,
        state_in,
        delta_out,
        delta_final,
    )
    if cubic:
        delta_value, early_arrived = together(delta_value, early_arrived)
        early_last = halving_last(early_pieces, early_arrived)
        late = (place, inputs, delta_value, inputs, delta_query_key)
        sent = halving_start(*late)
        sent, early_stay = together(sent, early_stay)
        arrived = [exchange(part, 1) for part in sent]
    grad_rows = run_input_gradient(
        delta_query_key,
        delta_value,
        delta_gate,
        query_key_weight,
        value_gate_weight,
        small_weight,
    )
    if cubic:
        grad_rows, arrived, early_last = together(grad_rows, arrived, early_last)
    grad_inputs = scatter(grad_rows, "head", 1)
    if cubic:
        late_pieces = halving_keep(*late, *arrived)
        late_arrived = halving_cross(late_pieces)
        late_stay = halving_stay(late_pieces)
        late_last = halving_last(late_pieces, late_arrived)
        gate_terms, out_terms = halving_terms(early_pieces, early_stay, early_last)
        value_terms, packed_terms = halving_terms(late_pieces, late_stay, late_last)
        value_terms = (value_terms[0].astype(F32) + value_terms[1].astype(F32), value_terms[2])
        packed_terms = (packed_terms[0].astype(F32) + packed_terms[1].astype(F32), packed_terms[2])
        grad_out = sum(term.astype(F32) for term in out_terms).T
        grad_query_key, grad_value_gate, grad_decay_beta = run_finish(
            key_width, heads, value_terms, gate_terms, packed_terms
        )
        grad_decay_beta = jnp.swapaxes(grad_decay_beta, 1, 2)
    else:
        grad_gate = scatter(product("td,tf->df", inputs, delta_gate), "ctx", 0).astype(F32)
        grad_out = scatter(product("tf,td->fd", hidden, grad_mixed), "ctx", 1).astype(F32)
        grad_value = scatter(product("td,tf->df", inputs, delta_value), "ctx", 0).astype(F32)
        packed = scatter(product("td,tf->df", inputs, delta_query_key), "ctx", 0).astype(F32)
        rest = packed[:, 2 * key_width :]
        grad_query_key = jnp.stack([packed[:, :key_width], packed[:, key_width : 2 * key_width]])
        grad_value_gate = jnp.stack([grad_value, grad_gate])
        grad_decay_beta = jnp.stack([rest[:, :heads], rest[:, heads : 2 * heads]])
    return (mixed, grad_inputs, grad_query_key, grad_value_gate, grad_decay_beta, grad_out)


def solution(mesh):
    in_specs = (
        P("ctx", None),
        P(None, None, "head"),
        P(None, None, "head"),
        P(None, None, "head"),
        P("head"),
        P("head"),
        P(),
        P("head", None),
        P("ctx"),
        P("ctx", None),
    )
    out_specs = (
        P("ctx", "head"),
        P("ctx", "head"),
        P(None, "ctx", "head"),
        P(None, "ctx", "head"),
        P(None, "ctx", "head"),
        P("head", "ctx"),
    )
    return jax.shard_map(body, mesh=mesh, in_specs=in_specs, out_specs=out_specs, check_vma=False)
```
